32 devices in a mesh: dp: 8 (over y, x, core), expert: 4 (over z).
Axes of the slice: x: 2, y: 2, z: 4, core: 2. Of those that a mesh axis runs over, the one named last changes fastest.
Arguments:
- tokens: bfloat16 [2, 8192, 1024], P(None, ('dp', 'expert')), may hold values from -6 to 6
- cotangent: bfloat16 [2, 8192, 1024], P(None, ('dp', 'expert')), may hold values from -6 to 6
- segment_ids: int32 [2, 8192], P(None, ('dp', 'expert')), may hold values from 0 to 3, as said below
- parent_ids: int32 [2, 8192], P(None, ('dp', 'expert')), may hold values from 0 to 3, as said below
- routes: int32 [2, 8192, 2], P(None, ('dp', 'expert')), may hold values from 0 to 3, all different within a row; in each aligned block of 256 rows (0 to 255, 256 to 511, ..., all dimensions but the last counted through in order) at most 160 rows name the same one
- gain_attn: float32 [1024], replicated, may hold values from 0.5 to 1.5
- w_qkv: bfloat16 [1024, 3072], P(('dp', 'expert')), may hold values from -0.25 to 0.25
- w_proj: bfloat16 [1024, 1024], P(('dp', 'expert')), may hold values from -0.5 to 0.5
- rel_bias: float32 [32, 16], replicated, may hold values from -4 to 4
- gain_moe: float32 [1024], replicated, may hold values from 0.5 to 1.5
- w_router: bfloat16 [1024, 4], replicated, may hold values from -0.125 to 0.125
- w_in: bfloat16 [4, 1024, 5632], P('expert', 'dp'), may hold values from -0.1875 to 0.1875
- w_out: bfloat16 [4, 2816, 1024], P('expert', 'dp'), may hold values from -0.4375 to 0.4375
Outputs:
- output: bfloat16 [2, 8192, 1024], P(None, ('dp', 'expert'))
- input_grad: bfloat16 [2, 8192, 1024], P(None, ('dp', 'expert'))
- gain_attn_grad: float32 [1024], replicated
- w_qkv_grad: float32 [1024, 3072], P(('dp', 'expert'))
- w_proj_grad: float32 [1024, 1024], P(('dp', 'expert'))
- rel_bias_grad: float32 [32, 16], replicated
- gain_moe_grad: float32 [1024], replicated
- w_router_grad: float32 [1024, 4], replicated
- w_in_grad: float32 [4, 1024, 5632], P('expert', 'dp')
- w_out_grad: float32 [4, 2816, 1024], P('expert', 'dp')
The draws below stay inside these ranges and needn't reach their ends.
Inputs may be any that keep to these rules, and one draw needn't show every extreme that they name: `routes`: each token names two different experts; in each micro-batch the 256 tokens of one device (rows of one device) name any expert at most 160 times, a bound that some block reaches. `segment_ids`: within each sequence of 256 tokens segment ids start at 0, never fall and take exactly 4 values. `parent_ids`: tokens of one segment share one parent: the segment itself or one of the two segments before it in the same sequence.
All inputs are finite; a program needn't handle non-finite values.
Results may differ from the reference program's by a relative error of at most 0.017.
The reference program's roundings to bfloat16 on the way count: a program that leaves them out, or rounds other values in their place, can miss the bound.
Values may be sent and summed in bfloat16 or wider, within the bound.
No kernel may reach another device: no remote copies, remote signals or barrier semaphores. Data moves between devices by JAX's collectives and lax.ppermute only.
A program may use at most 256 MiB of HBM per device.

```python
import math
from functools import partial
import jax
import jax.numpy as jnp
import numpy as np
from jax import lax

D = 1024
HEADS = 16
HEAD_DIM = 64
FF = 2816
BUCKETS = 32
MB = 2
SEQ = 256
NSEG = 4
EXPERTS = 4
CAP = 160
TOKENS = 8192


def tree_tables(key):
    base_key = jax.random.fold_in(key, 11)
    sequences = MB * TOKENS // SEQ
    seq_keys = jax.random.split(base_key, sequences)

    def one_sequence(seq_key):
        first_key, second_key = jax.random.split(seq_key)
        order = jax.random.permutation(first_key, SEQ - 1) + 1
        flags = jnp.zeros((SEQ,), jnp.int32).at[order[:NSEG - 1]].set(1)
        segment = jnp.cumsum(flags).astype(jnp.int32)
        steps_back = jax.random.randint(second_key, (SEQ,), 0, 3)
        self_ids = jnp.arange(SEQ, dtype=jnp.int32)
        parent_table = jnp.where(steps_back == 0, self_ids, jnp.maximum(self_ids - steps_back, 0))
        return (segment, parent_table[segment].astype(jnp.int32))
    segment, parent = jax.vmap(one_sequence)(seq_keys)
    return (segment.reshape(MB, TOKENS), parent.reshape(MB, TOKENS))


def draw_segment_ids(key, part):
    return tree_tables(key)[0]


def draw_parent_ids(key, part):
    return tree_tables(key)[1]


def shard_levels(own_key, dims, cuts, low, largest):
    loudness, own = 1.0, jax.random.fold_in(own_key, 6)
    for position, parts in cuts:
        steps = jnp.exp(jax.random.uniform(jax.random.fold_in(own, position), (parts,), jnp.float32, low / len(cuts), largest / len(cuts)))
        loudness = loudness * jnp.repeat(steps, dims[position] // parts).reshape([-1 if axis == position else 1 for axis in range(len(dims))])
    return loudness


def assign_block(rng, own, number, rows, amount, top, bound, skew):
    ranking = jax.random.permutation(rng, amount)
    packed, usual = load_shares(amount, rows * top, bound, skew, True), load_shares(amount, rows * top, bound, skew, False)
    places = jnp.arange(amount)

    def named(tallies, offset_by):
        used = int((tallies > 0).sum())
        fixed = max(1, used // 4)
        shifted = fixed + (places - fixed + offset_by * (used - fixed)) % max(1, amount - fixed)
        return jnp.zeros((amount,), jnp.int32).at[ranking[jnp.where(places < fixed, places, shifted)]].set(jnp.asarray(tallies, jnp.int32))

    tallies = jnp.where(number % 4 == 0, named(packed, number // 4), named(usual, number - number // 4 - 1))
    mixed = jax.random.permutation(jax.random.fold_in(own, 3), amount)
    giver, taker = mixed[0:amount // 2 * 2:2], mixed[1:amount // 2 * 2:2]
    slack = jnp.minimum(tallies[giver] - 1, bound - tallies[taker]) // 2
    slack = jnp.where((giver == ranking[0]) | (taker == ranking[0]) | (tallies[taker] == 0), 0, jnp.maximum(slack, 0))
    shifted = jax.random.randint(jax.random.fold_in(own, 4), (amount // 2,), 0, 1 << 20) % (slack + 1)
    tallies = tallies.at[giver].add(-shifted).at[taker].add(shifted)
    labels = jnp.searchsorted(jnp.cumsum(tallies), jnp.arange(rows * top), side="right").astype(jnp.int32)
    grid = labels.reshape(top, rows).T
    grid = grid[jax.random.permutation(jax.random.fold_in(own, 1), rows)]
    offset_by = jax.random.randint(jax.random.fold_in(own, 2), (rows, 1), 0, top)
    return jnp.take_along_axis(grid, (jnp.arange(top)[None, :] + offset_by) % top, axis=1)


def load_shares(amount, total, most, slope, full):
    weights = [(1 << 20) // math.isqrt(rank ** slope) + 1 for rank in range(1, amount + 1)]
    largest = most if full else min(most, max(-(-total // amount), total * weights[0] // sum(weights)))
    least = 1 if total - largest >= amount - 1 else 0
    holding, spare = [largest] + [least] * (amount - 1), total - largest - least * (amount - 1)
    while spare > 0:
        movable = [i for i in range(1, amount) if holding[i] < largest] or [i for i in range(1, amount) if holding[i] < most]
        whole, left = sum([weights[i] for i in movable]), spare
        for i in movable:
            extra = min(most - holding[i], max(1, left * weights[i] // whole), spare)
            holding[i] = holding[i] + extra
            spare = spare - extra
    return np.array(holding)


def centred(key, dims, spread, reach, cuts=(), kind=jnp.bfloat16):
    values = spread * jax.random.normal(key, dims, jnp.float32)
    if cuts:
        values = values * shard_levels(key, dims, cuts, -0.22, 0.18)
    return jnp.clip(values, -reach, reach).astype(kind)


def setup_inputs(seed: int = 0) -> dict:
    seeds = jax.random.split(jax.random.key(seed), 14)
    tokens = centred(seeds[0], (MB, TOKENS, D), 1.0, 6.0, ((1, 32),))
    cotangent = centred(seeds[1], (MB, TOKENS, D), 1.0, 6.0, ((1, 32),))
    segment_ids = draw_segment_ids(jax.random.fold_in(seeds[13], 71), 0)
    parent_ids = draw_parent_ids(jax.random.fold_in(seeds[13], 71), 0)
    routes_keys = jax.random.split(jax.random.fold_in(seeds[4], 1), MB * TOKENS // SEQ)
    routes_turns = jax.random.permutation(jax.random.fold_in(seeds[4], 3), MB * TOKENS // SEQ)
    routes = jax.vmap(lambda own, number: assign_block(jax.random.fold_in(seeds[4], 2), own, number, SEQ, EXPERTS, 2, CAP, 2))(routes_keys, routes_turns).reshape((MB, TOKENS, 2))
    gain_attn = jnp.clip(1.0 + 0.1 * jax.random.normal(seeds[5], (D,), jnp.float32), 0.5, 1.5)
    w_qkv = centred(seeds[6], (D, 3 * D), (D // 2) ** -0.5, 0.25, ((0, 32),))
    w_proj = centred(seeds[7], (D, D), (D // 8) ** -0.5, 0.5, ((0, 32),))
    rel_bias = centred(seeds[8], (BUCKETS, HEADS), 1.0, 4.0, (), jnp.float32)
    gain_moe = jnp.clip(1.0 + 0.1 * jax.random.normal(seeds[9], (D,), jnp.float32), 0.5, 1.5)
    w_router = centred(seeds[10], (D, EXPERTS), (2 * D) ** -0.5, 0.125)
    w_in = centred(seeds[11], (EXPERTS, D, 2 * FF), D ** -0.5, 0.1875, ((0, 4), (1, 8)))
    w_out = centred(seeds[12], (EXPERTS, FF, D), (FF // 16) ** -0.5, 0.4375, ((0, 4), (1, 8)))
    return {"tokens": tokens, "cotangent": cotangent, "segment_ids": segment_ids, "parent_ids": parent_ids, "routes": routes, "gain_attn": gain_attn, "w_qkv": w_qkv, "w_proj": w_proj, "rel_bias": rel_bias, "gain_moe": gain_moe, "w_router": w_router, "w_in": w_in, "w_out": w_out}


@jax.custom_vjp
def low(v):
    return lax.optimization_barrier(v.astype(jnp.bfloat16)).astype(jnp.float32)

@jax.custom_vjp
def low_back(v):
    return v

def low_keep(v):
    return (low(v), None)

def low_pass(kept, grad):
    return (grad,)

def back_keep(v):
    return (v, None)

def back_low(kept, grad):
    return (low(grad),)
low.defvjp(low_keep, low_pass)
low_back.defvjp(back_keep, back_low)
EPSILON = 1e-06
NEG_BIG = -1e+30
LIMITS = (12, 16, 23, 32, 46, 64, 91)

def bucket_of(offset):
    distance = jnp.abs(offset)
    far_part = 8 + sum(((distance >= limit).astype(jnp.int32) for limit in LIMITS))
    near_far = jnp.where(distance < 8, distance, far_part)
    return (jnp.where(offset > 0, 16, 0) + near_far).astype(jnp.int32)

def slot_positions(routes, experts):
    order = jnp.concatenate([routes[:, 0], routes[:, 1]])
    chosen = (order[:, None] == jnp.arange(experts, dtype=jnp.int32)[None, :]).astype(jnp.int32)
    before = jnp.cumsum(chosen, axis=0) - chosen
    place = lax.optimization_barrier(jnp.sum(before * chosen, axis=1))
    return place.reshape(2, -1).T.astype(jnp.int32)

def tree_mask(segment, parent):
    same = segment[:, None, :] == segment[:, :, None]
    upward = segment[:, None, :] == parent[:, :, None]
    downward = parent[:, None, :] == segment[:, :, None]
    return same | upward | downward

def rms_scale(values):
    return lax.rsqrt(lax.optimization_barrier(jnp.mean(values * values, axis=-1, keepdims=True)) + EPSILON)

def gelu_product(gate_part, up_part):
    return jax.nn.gelu(gate_part, approximate=True) * up_part

def block_forward(weights_all, inputs_group, segment, parent, chosen, places, buckets):
    gain_attn, w_qkv, w_proj, rel_bias, gain_moe, w_router, w_in, w_out = weights_all
    group = inputs_group.shape[0]
    best = lax.Precision.HIGHEST
    first_norm = low(inputs_group * rms_scale(inputs_group) * gain_attn)
    projected = low_back(low(jnp.einsum('gsd,df->gsf', first_norm, w_qkv, precision=best)))
    split_parts = projected.reshape(group, SEQ, 3, HEADS, HEAD_DIM)
    queries, keys, values = (split_parts[:, :, 0], split_parts[:, :, 1], split_parts[:, :, 2])
    bias_heads = jnp.transpose(rel_bias[buckets], (2, 0, 1))
    raw = jnp.einsum('gqhd,gkhd->ghqk', queries, keys, precision=best) * HEAD_DIM ** (-0.5) + bias_heads[None]
    scores = jnp.where(tree_mask(segment, parent)[:, None], low_back(raw), NEG_BIG)
    attn_weights = jnp.exp(scores - jax.nn.logsumexp(scores, axis=-1, keepdims=True))
    mixed = jnp.einsum('ghqk,gkhd->gqhd', low(attn_weights), values, precision=best).reshape(group, SEQ, D)
    attended = low_back(jnp.einsum('gsd,de->gse', low_back(low(mixed)), w_proj, precision=best))
    hidden_mid = inputs_group + attended
    second_norm = low(hidden_mid * rms_scale(hidden_mid) * gain_moe)
    logits = low_back(jnp.einsum('gsd,de->gse', second_norm, w_router, precision=best))
    router_log = jax.nn.logsumexp(logits, axis=-1, keepdims=True)
    router_weights = jnp.exp(logits - router_log)
    route_hot = (chosen[..., None] == jnp.arange(EXPERTS, dtype=jnp.int32)).astype(jnp.float32)
    gates = lax.optimization_barrier(jnp.sum(router_weights[:, :, None, :] * route_hot, axis=-1))
    group_ids = jnp.broadcast_to(jnp.arange(group, dtype=jnp.int32)[:, None, None], chosen.shape)
    spread_rows = jnp.broadcast_to(second_norm[:, :, None, :], chosen.shape + (D,))
    filled = jnp.zeros((group, EXPERTS, CAP, D), jnp.float32).at[group_ids, chosen, places].set(spread_rows)
    slot_inputs = low_back(filled)
    gate_part = jnp.einsum('gecd,edf->gecf', slot_inputs, w_in[:, :, :FF], precision=best)
    up_part = jnp.einsum('gecd,edf->gecf', slot_inputs, w_in[:, :, FF:], precision=best)
    joined = low_back(jnp.concatenate([gate_part, up_part], axis=-1))
    product = low(gelu_product(joined[..., :FF], joined[..., FF:]))
    slot_outputs = low_back(low(jnp.einsum('gecf,efd->gecd', product, w_out, precision=best)))
    returned = slot_outputs[group_ids, chosen, places]
    mixture = gates[:, :, 0, None] * returned[:, :, 0] + gates[:, :, 1, None] * returned[:, :, 1]
    return hidden_mid + mixture

def reference(tokens, cotangent, segment_ids, parent_ids, routes, gain_attn, w_qkv, w_proj, rel_bias, gain_moe, w_router, w_in, w_out):
    sequences = MB * TOKENS // SEQ
    group = math.gcd(sequences, max(1, 4096 // SEQ))
    rounds = sequences // group

    def regroup(array):
        return array.reshape((rounds, group, SEQ) + array.shape[2:])
    segment_all = regroup(segment_ids)
    parent_all = regroup(parent_ids)
    route_all = regroup(routes)
    place_all = jax.vmap(jax.vmap(partial(slot_positions, experts=EXPERTS)))(route_all)
    positions = jnp.arange(SEQ, dtype=jnp.int32)
    buckets = bucket_of(positions[None, :] - positions[:, None])
    checked = jax.checkpoint(block_forward)

    def whole(inputs_all, *weights_all):

        def one_round(pieces):
            inputs_group, segment, parent, chosen, places = pieces
            return checked(weights_all, inputs_group, segment, parent, chosen, places, buckets)
        return lax.map(one_round, (inputs_all, segment_all, parent_all, route_all, place_all))
    primals = (regroup(tokens.astype(jnp.float32)), gain_attn.astype(jnp.float32), w_qkv.astype(jnp.float32), w_proj.astype(jnp.float32), rel_bias.astype(jnp.float32), gain_moe.astype(jnp.float32), w_router.astype(jnp.float32), w_in.astype(jnp.float32), w_out.astype(jnp.float32))
    results, pullback = jax.vjp(whole, *primals)
    grads = pullback(regroup(cotangent.astype(jnp.float32)))
    output = results.reshape(tokens.shape).astype(jnp.bfloat16)
    input_grad = grads[0].reshape(tokens.shape).astype(jnp.bfloat16)
    return (output, input_grad, grads[1], grads[2], grads[3], grads[4], grads[5], grads[6], grads[7], grads[8])
```

```python
from functools import partial

import jax
import jax.numpy as jnp
from jax import lax
from jax.sharding import PartitionSpec as P

EPSILON = 1e-06
NEG_BIG = -1e30
LIMITS = (12, 16, 23, 32, 46, 64, 91)
F32 = jnp.float32
BF16 = jnp.bfloat16


def bucket_of(offset):
    distance = jnp.abs(offset)
    far_part = 8 + sum(((distance >= limit).astype(jnp.int32) for limit in LIMITS))
    near_far = jnp.where(distance < 8, distance, far_part)
    return jnp.where(offset > 0, 16, 0) + near_far


def slot_positions(routes, experts):
    order = jnp.concatenate([routes[:, 0], routes[:, 1]])
    chosen = (order[:, None] == jnp.arange(experts, dtype=jnp.int32)[None, :]).astype(jnp.int32)
    before = jnp.cumsum(chosen, axis=0) - chosen
    place = jnp.sum(before * chosen, axis=1)
    return place.reshape(2, -1).T


def tree_mask(segment, parent):
    same = segment[None, :] == segment[:, None]
    upward = segment[None, :] == parent[:, None]
    downward = parent[None, :] == segment[:, None]
    return same | upward | downward


def rms_scale(values):
    return lax.rsqrt(jnp.mean(values * values, axis=-1, keepdims=True) + EPSILON)


def gelu_product(gate_part, up_part):
    return jax.nn.gelu(gate_part, approximate=True) * up_part


def flip(value, axis, size, bit):
    return lax.ppermute(value, axis, [(i, i ^ bit) for i in range(size)])


def shift(value, axis, size, step):
    return lax.ppermute(value, axis, [(i, (i + step) % size) for i in range(size)])


def halving_orders(size):
    bits = [1 << k for k in range(1, size.bit_length() - 1)]
    return (bits, bits[::-1])


def gather_pieces(block, size):
    half = block.shape[0] // 2
    found = []
    for part, order in enumerate(halving_orders(size)):
        have = [(0, block[part * half : (part + 1) * half])]
        for bit in order:
            have = have + [(rel ^ bit, flip(piece, "dp", size, bit)) for rel, piece in have]
        have = have + [(rel ^ 1, flip(piece, "dp", size, 1)) for rel, piece in have]
        found += [(rel, part * half, piece) for rel, piece in have]
    return found


def gather_dp(block, size):
    me = lax.axis_index("dp")
    full = jnp.zeros((size,) + block.shape, block.dtype)
    for rel, offset, piece in gather_pieces(block, size):
        full = lax.dynamic_update_slice(full, piece[None], (me ^ rel, offset, 0))
    return full.reshape(size * block.shape[0], block.shape[1])


def gather_expert(block, size):
    me = lax.axis_index("expert")
    full = jnp.zeros((size,) + block.shape, block.dtype)
    for step in range(size):
        piece = shift(block, "expert", size, step) if step else block
        full = lax.dynamic_update_slice(full, piece[None], ((me - step) % size, 0, 0))
    return full.reshape(size * block.shape[0], block.shape[1])


def split_bit(value, me, bit):
    mine = (me // bit) % 2
    kept = lax.dynamic_index_in_dim(value, mine, 0, keepdims=False)
    sent = lax.dynamic_index_in_dim(value, 1 - mine, 0, keepdims=False)
    return kept, sent


def scatter_dp(total, size):
    me = lax.axis_index("dp")
    rows, width = total.shape[0] // size, total.shape[1]
    half = rows // 2
    kept, sent = split_bit(jnp.moveaxis(total.reshape(size // 2, 2, rows, width), 1, 0), me, 1)
    summed = kept.astype(F32) + flip(sent, "dp", size, 1).astype(F32)
    outs = []
    for part, order in enumerate(halving_orders(size)):
        value = summed[:, part * half : (part + 1) * half]
        left = [1 << k for k in range(1, size.bit_length() - 1)]
        for bit in order:
            place = left.index(bit)
            high, low = 1 << (len(left) - 1 - place), 1 << place
            shaped = value.astype(BF16).reshape(high, 2, low, half, width)
            kept, sent = split_bit(jnp.moveaxis(shaped, 1, 0), me, bit)
            value = kept.astype(F32) + flip(sent, "dp", size, bit).astype(F32)
            left.remove(bit)
        outs.append(value.reshape(half, width))
    return jnp.concatenate(outs, axis=0)


def scatter_expert(total, size):
    me = lax.axis_index("expert")
    rows = total.shape[0] // size
    low = total.astype(BF16)
    result = lax.dynamic_slice_in_dim(total, me * rows, rows, 0)
    for step in range(1, size):
        block = lax.dynamic_slice_in_dim(low, ((me + step) % size) * rows, rows, 0)
        result = result + shift(block, "expert", size, step).astype(F32)
    return result


def sum_all(value, sizes):
    for axis in ("dp", "expert"):
        bit = 1
        while bit < sizes[axis]:
            value = value + flip(value, axis, sizes[axis], bit)
            bit *= 2
    return value


def dot(left, right):
    return jnp.dot(left, right, preferred_element_type=F32)


def dot_t(left, right):
    return lax.dot_general(left, right, (((1,), (1,)), ((), ())), preferred_element_type=F32)


def t_dot(left, right):
    return lax.dot_general(left, right, (((0,), (0,)), ((), ())), preferred_element_type=F32)


def on_device(
    sizes,
    tokens,
    cotangent,
    segment_ids,
    parent_ids,
    routes,
    gain_attn,
    w_qkv,
    w_proj,
    rel_bias,
    gain_moe,
    w_router,
    w_in,
    w_out,
):
    dp, experts = sizes["dp"], sizes["expert"]
    batches, length, width = tokens.shape
    heads = rel_bias.shape[1]
    head_size = width // heads
    inner = w_in.shape[2] // 2
    capacity = (10 * length + 4 * experts - 1) // (4 * experts)
    slot_count = experts * capacity
    scale = head_size ** (-0.5)
    me_e = lax.axis_index("expert")

    attn_w = gather_dp(gather_expert(jnp.concatenate([w_qkv, w_proj], axis=1), experts), dp)
    full_qkv, full_proj = attn_w[:, : 3 * width], attn_w[:, 3 * width :]

    relative = (routes - me_e) % experts
    places = jax.vmap(partial(slot_positions, experts=experts))(routes)
    targets = relative * capacity + places
    hot = targets[..., None] == jnp.arange(slot_count, dtype=jnp.int32)
    select = hot.astype(BF16)
    both = select[:, :, 0] + select[:, :, 1]

    def exchange(blocks, sign):
        parts = [blocks[:capacity]]
        for step in range(1, experts):
            parts.append(
                shift(blocks[step * capacity : (step + 1) * capacity], "expert", experts, sign * step)
            )
        return jnp.concatenate(parts, axis=0)

    out_grads = [cotangent[n] for n in range(batches)]
    go_slots = [
        exchange(t_dot(both[n], out_grads[n]).astype(BF16), 1) for n in range(batches)
    ]

    win_full = gather_dp(w_in[0], dp)
    wout_full = gather_dp(w_out[0], dp)

    positions = jnp.arange(length, dtype=jnp.int32)
    buckets = bucket_of(positions[None, :] - positions[:, None])
    bucket_hot = (buckets[:, :, None] == jnp.arange(rel_bias.shape[0], dtype=jnp.int32)).astype(F32)
    bias_heads = jnp.einsum("qkc,ch->hqk", bucket_hot, rel_bias, precision=lax.Precision.HIGHEST)

    saved = []
    for n in range(batches):
        h0 = tokens[n].astype(F32)
        r1 = rms_scale(h0)
        n1_hat = h0 * r1
        n1 = (n1_hat * gain_attn).astype(BF16)
        qkv = dot(n1, full_qkv).astype(BF16).reshape(length, 3, heads, head_size)
        q, k, v = qkv[:, 0], qkv[:, 1], qkv[:, 2]
        allowed = tree_mask(segment_ids[n], parent_ids[n])
        raw = jnp.einsum("qhd,khd->hqk", q, k, preferred_element_type=F32) * scale + bias_heads
        scores = jnp.where(allowed[None], raw, NEG_BIG)
        lse = jax.nn.logsumexp(scores, axis=-1, keepdims=True)
        p = jnp.exp(scores - lse)
        p_low = p.astype(BF16)
        o = jnp.einsum("hqk,khd->qhd", p_low, v, preferred_element_type=F32)
        o = o.reshape(length, width).astype(BF16)
        h1 = h0 + dot(o, full_proj)
        r2 = rms_scale(h1)
        n2_hat = h1 * r2
        n2 = (n2_hat * gain_moe).astype(BF16)
        probs = jax.nn.softmax(dot(n2, w_router), axis=-1)
        x_slots = exchange(t_dot(both[n], n2).astype(BF16), 1)
        saved.append((h0, r1, n1_hat, n1, q, k, v, p, p_low, o, h1, r2, n2_hat, n2, probs, x_slots))

    mine_hot = jnp.arange(experts, dtype=jnp.int32) == me_e
    held = []
    for n in range(batches):
        x = saved[n][-1]
        go = go_slots[n].astype(F32)
        gate = jnp.sum(
            jnp.where(mine_hot, jax.nn.softmax(dot(x, w_router), axis=-1), 0.0), -1, keepdims=True
        )
        dy = (gate * go).astype(BF16)
        a = dot(x, win_full[:, :inner])
        b = dot(x, win_full[:, inner:])
        g, back = jax.vjp(gelu_product, a, b)
        g = g.astype(BF16)
        y = dot(g, wout_full).astype(BF16)
        dgate = jnp.sum(go * y.astype(F32), axis=-1)
        da, db = back(dot_t(dy, wout_full))
        du = jnp.concatenate([da, db], axis=1).astype(BF16)
        dx = dot_t(du, win_full).astype(BF16)
        dgate_back = exchange(dgate, -1)
        dx_back = exchange(dx, -1)
        y_back = exchange(y, -1)
        held.append((x, du, g, dy, dgate_back, dx_back, y_back))

    in_part = sum(t_dot(h[0], h[1]) for h in held).astype(BF16)
    out_part = sum(t_dot(h[2], h[3]) for h in held).astype(BF16)
    in_total = scatter_dp(in_part, dp)
    out_total = scatter_dp(out_part, dp)

    outputs, input_grads = [], []
    qkv_part = proj_part = None
    table_grad = gain_attn_grad = gain_moe_grad = router_grad = 0.0
    for n in range(batches):
        h0, r1, n1_hat, n1, q, k, v, p, p_low, o, h1, r2, n2_hat, n2, probs, _ = saved[n]
        _, _, _, _, dgate_back, dx_back, y_back = held[n]
        go = out_grads[n].astype(F32)
        route_hot = (routes[n][:, :, None] == jnp.arange(experts, dtype=jnp.int32)).astype(F32)
        gates = jnp.sum(probs[:, None, :] * route_hot, axis=-1)
        picked0, picked1 = dot(select[n][:, 0], y_back), dot(select[n][:, 1], y_back)
        moe = gates[:, :1] * picked0 + gates[:, 1:] * picked1
        outputs.append((h1 + moe).astype(BF16))
        dgate = jnp.sum(jnp.where(hot[n], dgate_back, 0.0), axis=-1)
        dprobs = jnp.sum(route_hot * dgate[:, :, None], axis=1)
        dlogits = probs * (dprobs - jnp.sum(probs * dprobs, axis=-1, keepdims=True))
        dlogits = dlogits.astype(BF16)
        dn2 = dot(both[n], dx_back) + dot_t(dlogits, w_router)
        router_grad = router_grad + t_dot(n2, dlogits)
        gain_moe_grad = gain_moe_grad + jnp.sum(dn2 * n2_hat, axis=0)
        scaled = dn2 * gain_moe
        dh1 = go + r2 * (scaled - n2_hat * jnp.mean(scaled * n2_hat, axis=-1, keepdims=True))
        dbranch = dh1.astype(BF16)
        term = t_dot(o, dbranch)
        proj_part = term if proj_part is None else proj_part + term
        do = dot_t(dbranch, full_proj).astype(BF16).reshape(length, heads, head_size)
        dv = jnp.einsum("hqk,qhd->khd", p_low, do, preferred_element_type=F32)
        dp_ = jnp.einsum("qhd,khd->hqk", do, v, preferred_element_type=F32)
        ds = (p * (dp_ - jnp.sum(p * dp_, axis=-1, keepdims=True))).astype(BF16)
        dq = jnp.einsum("hqk,khd->qhd", ds, k, preferred_element_type=F32) * scale
        dk = jnp.einsum("hqk,qhd->khd", ds, q, preferred_element_type=F32) * scale
        table_grad = table_grad + jnp.einsum(
            "hqk,qkc->ch", ds, bucket_hot.astype(BF16), preferred_element_type=F32
        )
        dqkv = jnp.stack([dq, dk, dv], axis=1).reshape(length, 3 * width).astype(BF16)
        term = t_dot(n1, dqkv)
        qkv_part = term if qkv_part is None else qkv_part + term
        dn1 = dot_t(dqkv, full_qkv)
        gain_attn_grad = gain_attn_grad + jnp.sum(dn1 * n1_hat, axis=0)
        scaled = dn1 * gain_attn
        input_grad = dh1 + r1 * (
            scaled - n1_hat * jnp.mean(scaled * n1_hat, axis=-1, keepdims=True)
        )
        input_grads.append(input_grad.astype(BF16))

    proj_total = scatter_expert(scatter_dp(proj_part.astype(BF16), dp), experts)
    qkv_total = scatter_expert(scatter_dp(qkv_part.astype(BF16), dp), experts)
    small = jnp.concatenate(
        [gain_attn_grad, table_grad.reshape(-1), gain_moe_grad, router_grad.reshape(-1)]
    )
    small = sum_all(small.reshape(-1, 128), sizes).reshape(-1)
    cuts = (width, width + table_grad.size, 2 * width + table_grad.size)
    return (
        jnp.stack(outputs),
        jnp.stack(input_grads),
        small[: cuts[0]],
        qkv_total,
        proj_total,
        small[cuts[0] : cuts[1]].reshape(table_grad.shape),
        small[cuts[1] : cuts[2]],
        small[cuts[2] :].reshape(router_grad.shape),
        in_total[None],
        out_total[None],
    )


def solution(mesh):
    rows = P(None, ("dp", "expert"), None)
    in_specs = (
        rows,
        rows,
        P(None, ("dp", "expert")),
        P(None, ("dp", "expert")),
        rows,
        P(),
        P(("dp", "expert"), None),
        P(("dp", "expert"), None),
        P(),
        P(),
        P(),
        P("expert", "dp", None),
        P("expert", "dp", None),
    )
    out_specs = (
        rows,
        rows,
        P(),
        P(("dp", "expert"), None),
        P(("dp", "expert"), None),
        P(),
        P(),
        P(),
        P("expert", "dp", None),
        P("expert", "dp", None),
    )
    return jax.shard_map(
        partial(on_device, dict(mesh.shape)),
        mesh=mesh,
        in_specs=in_specs,
        out_specs=out_specs,
        check_vma=False,
    )
```

```python
from functools import partial

import jax
import jax.numpy as jnp
from jax import lax
from jax.sharding import PartitionSpec as P

EPSILON = 1e-06
NEG_BIG = -1e30
LIMITS = (12, 16, 23, 32, 46, 64, 91)
F32 = jnp.float32
BF16 = jnp.bfloat16


def bucket_of(offset):
    distance = jnp.abs(offset)
    far_part = 8 + sum(((distance >= limit).astype(jnp.int32) for limit in LIMITS))
    near_far = jnp.where(distance < 8, distance, far_part)
    return jnp.where(offset > 0, 16, 0) + near_far


def slot_positions(routes, experts):
    order = jnp.concatenate([routes[:, 0], routes[:, 1]])
    chosen = (order[:, None] == jnp.arange(experts, dtype=jnp.int32)[None, :]).astype(jnp.int32)
    before = jnp.cumsum(chosen, axis=0) - chosen
    place = jnp.sum(before * chosen, axis=1)
    return place.reshape(2, -1).T


def tree_mask(segment, parent):
    same = segment[None, :] == segment[:, None]
    upward = segment[None, :] == parent[:, None]
    downward = parent[None, :] == segment[:, None]
    return same | upward | downward


def rms_scale(values):
    return lax.rsqrt(jnp.mean(values * values, axis=-1, keepdims=True) + EPSILON)


def gelu_product(gate_part, up_part):
    return jax.nn.gelu(gate_part, approximate=True) * up_part


def flip(value, axis, size, bit):
    return lax.ppermute(value, axis, [(i, i ^ bit) for i in range(size)])


def shift(value, axis, size, step):
    return lax.ppermute(value, axis, [(i, (i + step) % size) for i in range(size)])


def halving_orders(size):
    bits = [1 << k for k in range(1, size.bit_length() - 1)]
    return (bits, bits[::-1])


def gather_dp(block, size):
    me = lax.axis_index("dp")
    rows, width = block.shape
    half = rows // 2
    columns = []
    for part, order in enumerate(halving_orders(size)):
        have = block[None, part * half : (part + 1) * half]
        rels = [0]
        for bit in order:
            have = jnp.concatenate([have, flip(have, "dp", size, bit)], axis=0)
            rels = rels + [rel ^ bit for rel in rels]
        columns.append((have, rels))
    near = [columns[0][0], columns[1][0]]
    far = [flip(have, "dp", size, 1) for have in near]
    full = jnp.zeros((size, rows, width), block.dtype)
    for part in range(2):
        for other, have in ((0, near[part]), (1, far[part])):
            for place, rel in enumerate(columns[part][1]):
                full = lax.dynamic_update_slice(
                    full, have[place : place + 1], (me ^ rel ^ other, part * half, 0)
                )
    return full.reshape(size * rows, width)


def gather_expert(block, size):
    me = lax.axis_index("expert")
    full = jnp.zeros((size,) + block.shape, block.dtype)
    for step in range(size):
        piece = shift(block, "expert", size, step) if step else block
        full = lax.dynamic_update_slice(full, piece[None], ((me - step) % size, 0, 0))
    return full.reshape(size * block.shape[0], block.shape[1])


def all_to_all(value):
    return lax.all_to_all(value, "expert", split_axis=0, concat_axis=0, tiled=True)


def split_bit(value, me, bit):
    mine = (me // bit) % 2
    kept = lax.dynamic_index_in_dim(value, mine, 0, keepdims=False)
    sent = lax.dynamic_index_in_dim(value, 1 - mine, 0, keepdims=False)
    return kept, sent


def scatter_dp(total, size):
    me = lax.axis_index("dp")
    rows, width = total.shape[0] // size, total.shape[1]
    half = rows // 2
    kept, sent = split_bit(jnp.moveaxis(total.reshape(size // 2, 2, rows, width), 1, 0), me, 1)
    summed = kept.astype(F32) + flip(sent, "dp", size, 1).astype(F32)
    outs = []
    for part, order in enumerate(halving_orders(size)):
        value = summed[:, part * half : (part + 1) * half]
        left = [1 << k for k in range(1, size.bit_length() - 1)]
        for bit in order:
            place = left.index(bit)
            high, low = 1 << (len(left) - 1 - place), 1 << place
            shaped = value.astype(BF16).reshape(high, 2, low, half, width)
            kept, sent = split_bit(jnp.moveaxis(shaped, 1, 0), me, bit)
            value = kept.astype(F32) + flip(sent, "dp", size, bit).astype(F32)
            left.remove(bit)
        outs.append(value.reshape(half, width))
    return jnp.concatenate(outs, axis=0)


def scatter_expert(total, size):
    rows = total.shape[0] // size
    low = total.astype(BF16).reshape(size, rows, total.shape[1])
    return jnp.sum(all_to_all(low).astype(F32), axis=0)


def exchange(value, size):
    me = lax.axis_index("expert")
    full = value
    for step in range(1, size):
        sent = lax.dynamic_slice_in_dim(value, (me + step) % size, 1, 0)
        got = shift(sent, "expert", size, step)
        full = lax.dynamic_update_slice_in_dim(full, got, (me - step) % size, 0)
    return full


def sum_all(value, sizes):
    for axis in ("dp", "expert"):
        bit = 1
        while bit < sizes[axis]:
            value = value + flip(value, axis, sizes[axis], bit)
            bit *= 2
    return value


def dot(left, right):
    return jnp.dot(left, right, preferred_element_type=F32)


def dot_t(left, right):
    return lax.dot_general(left, right, (((1,), (1,)), ((), ())), preferred_element_type=F32)


def t_dot(left, right):
    return lax.dot_general(left, right, (((0,), (0,)), ((), ())), preferred_element_type=F32)


def on_device(
    sizes,
    tokens,
    cotangent,
    segment_ids,
    parent_ids,
    routes,
    gain_attn,
    w_qkv,
    w_proj,
    rel_bias,
    gain_moe,
    w_router,
    w_in,
    w_out,
):
    dp, experts = sizes["dp"], sizes["expert"]
    batches, length, width = tokens.shape
    heads = rel_bias.shape[1]
    head_size = width // heads
    inner = w_in.shape[2] // 2
    capacity = (10 * length + 4 * experts - 1) // (4 * experts)
    slot_count = experts * capacity
    scale = head_size ** (-0.5)
    me_e = lax.axis_index("expert")

    attn_block = gather_expert(jnp.concatenate([w_qkv, w_proj], axis=1), experts)
    attn_w = gather_dp(attn_block, dp)
    full_qkv, full_proj = attn_w[:, : 3 * width], attn_w[:, 3 * width :]

    places = jax.vmap(partial(slot_positions, experts=experts))(routes)
    targets = routes * capacity + places
    hot = targets[..., None] == jnp.arange(slot_count, dtype=jnp.int32)
    select = hot.astype(BF16)
    both = select[:, :, 0] + select[:, :, 1]
    out_grads = [cotangent[n] for n in range(batches)]
    outgoing = [
        t_dot(both[n], out_grads[n]).astype(BF16).reshape(experts, capacity, width)
        for n in range(batches)
    ]
    outgoing, _ = lax.optimization_barrier((jnp.stack(outgoing, axis=1), attn_block))
    go_slots = all_to_all(outgoing)

    win_full = lax.all_gather(w_in[0], "dp", axis=0, tiled=True)
    wout_full = lax.all_gather(w_out[0], "dp", axis=0, tiled=True)

    positions = jnp.arange(length, dtype=jnp.int32)
    buckets = bucket_of(positions[None, :] - positions[:, None])
    bucket_hot = (buckets[:, :, None] == jnp.arange(rel_bias.shape[0], dtype=jnp.int32)).astype(F32)
    bias_heads = jnp.einsum("qkc,ch->hqk", bucket_hot, rel_bias, precision=lax.Precision.HIGHEST)

    saved = []
    for n in range(batches):
        h0 = tokens[n].astype(F32)
        r1 = rms_scale(h0)
        n1_hat = h0 * r1
        n1 = (n1_hat * gain_attn).astype(BF16)
        qkv = dot(n1, full_qkv).astype(BF16).reshape(length, 3, heads, head_size)
        q, k, v = qkv[:, 0], qkv[:, 1], qkv[:, 2]
        allowed = tree_mask(segment_ids[n], parent_ids[n])
        raw = jnp.einsum("qhd,khd->hqk", q, k, preferred_element_type=F32) * scale + bias_heads
        scores = jnp.where(allowed[None], raw, NEG_BIG)
        lse = jax.nn.logsumexp(scores, axis=-1, keepdims=True)
        p = jnp.exp(scores - lse)
        p_low = p.astype(BF16)
        o = jnp.einsum("hqk,khd->qhd", p_low, v, preferred_element_type=F32)
        o = o.reshape(length, width).astype(BF16)
        h1 = h0 + dot(o, full_proj)
        r2 = rms_scale(h1)
        n2_hat = h1 * r2
        n2 = (n2_hat * gain_moe).astype(BF16)
        probs = jax.nn.softmax(dot(n2, w_router), axis=-1)
        x_slots = all_to_all(t_dot(both[n], n2).astype(BF16).reshape(experts, capacity, width))
        saved.append((h0, r1, n1_hat, n1, q, k, v, p, p_low, o, h1, r2, n2_hat, n2, probs, x_slots))

    mine_hot = jnp.arange(experts, dtype=jnp.int32) == me_e
    held = []
    for n in range(batches):
        x = saved[n][-1].reshape(slot_count, width)
        go = go_slots[:, n].reshape(slot_count, width).astype(F32)
        gate = jnp.sum(
            jnp.where(mine_hot, jax.nn.softmax(dot(x, w_router), axis=-1), 0.0), -1, keepdims=True
        )
        dy = (gate * go).astype(BF16)
        a = dot(x, win_full[:, :inner])
        b = dot(x, win_full[:, inner:])
        g, back = jax.vjp(gelu_product, a, b)
        g = g.astype(BF16)
        y = dot(g, wout_full).astype(BF16)
        dgate = jnp.sum(go * y.astype(F32), axis=-1)
        da, db = back(dot_t(dy, wout_full))
        du = jnp.concatenate([da, db], axis=1).astype(BF16)
        dx = dot_t(du, win_full).astype(BF16)
        dx_back = all_to_all(dx.reshape(experts, capacity, width)).reshape(slot_count, width)
        held.append((x, du, g, dy, dgate, dx_back, y))
    dgate_all = jnp.stack([h[4].reshape(experts, capacity) for h in held], axis=1)
    dgate_back = exchange(dgate_all, experts)
    y_back = all_to_all(
        jnp.stack([h[6].reshape(experts, capacity, width) for h in held], axis=1)
    )

    in_part = sum(t_dot(h[0], h[1]) for h in held).astype(BF16)
    out_part = sum(t_dot(h[2], h[3]) for h in held).astype(BF16)
    in_total = lax.psum_scatter(in_part, "dp", scatter_dimension=0, tiled=True).astype(F32)
    out_total = scatter_dp(out_part, dp)

    outputs, input_grads = [], []
    qkv_part = proj_part = None
    table_grad = gain_attn_grad = gain_moe_grad = router_grad = 0.0
    for n in range(batches):
        h0, r1, n1_hat, n1, q, k, v, p, p_low, o, h1, r2, n2_hat, n2, probs, _ = saved[n]
        dx_back = held[n][5]
        y_n = y_back[:, n].reshape(slot_count, width)
        go = out_grads[n].astype(F32)
        route_hot = (routes[n][:, :, None] == jnp.arange(experts, dtype=jnp.int32)).astype(F32)
        gates = jnp.sum(probs[:, None, :] * route_hot, axis=-1)
        picked0, picked1 = dot(select[n][:, 0], y_n), dot(select[n][:, 1], y_n)
        moe = gates[:, :1] * picked0 + gates[:, 1:] * picked1
        outputs.append((h1 + moe).astype(BF16))
        dgate = jnp.sum(jnp.where(hot[n], dgate_back[:, n].reshape(-1), 0.0), axis=-1)
        dprobs = jnp.sum(route_hot * dgate[:, :, None], axis=1)
        dlogits = probs * (dprobs - jnp.sum(probs * dprobs, axis=-1, keepdims=True))
        dlogits = dlogits.astype(BF16)
        dn2 = dot(both[n], dx_back) + dot_t(dlogits, w_router)
        router_grad = router_grad + t_dot(n2, dlogits)
        gain_moe_grad = gain_moe_grad + jnp.sum(dn2 * n2_hat, axis=0)
        scaled = dn2 * gain_moe
        dh1 = go + r2 * (scaled - n2_hat * jnp.mean(scaled * n2_hat, axis=-1, keepdims=True))
        dbranch = dh1.astype(BF16)
        term = t_dot(o, dbranch)
        proj_part = term if proj_part is None else proj_part + term
        do = dot_t(dbranch, full_proj).astype(BF16).reshape(length, heads, head_size)
        dv = jnp.einsum("hqk,qhd->khd", p_low, do, preferred_element_type=F32)
        dp_ = jnp.einsum("qhd,khd->hqk", do, v, preferred_element_type=F32)
        ds = (p * (dp_ - jnp.sum(p * dp_, axis=-1, keepdims=True))).astype(BF16)
        dq = jnp.einsum("hqk,khd->qhd", ds, k, preferred_element_type=F32) * scale
        dk = jnp.einsum("hqk,qhd->khd", ds, q, preferred_element_type=F32) * scale
        table_grad = table_grad + jnp.einsum(
            "hqk,qkc->ch", ds, bucket_hot.astype(BF16), preferred_element_type=F32
        )
        dqkv = jnp.stack([dq, dk, dv], axis=1).reshape(length, 3 * width).astype(BF16)
        term = t_dot(n1, dqkv)
        qkv_part = term if qkv_part is None else qkv_part + term
        dn1 = dot_t(dqkv, full_qkv)
        gain_attn_grad = gain_attn_grad + jnp.sum(dn1 * n1_hat, axis=0)
        scaled = dn1 * gain_attn
        input_grad = dh1 + r1 * (
            scaled - n1_hat * jnp.mean(scaled * n1_hat, axis=-1, keepdims=True)
        )
        input_grads.append(input_grad.astype(BF16))

    proj_total = scatter_expert(scatter_dp(proj_part.astype(BF16), dp), experts)
    qkv_total = scatter_expert(scatter_dp(qkv_part.astype(BF16), dp), experts)
    small = jnp.concatenate(
        [gain_attn_grad, table_grad.reshape(-1), gain_moe_grad, router_grad.reshape(-1)]
    )
    small = sum_all(small.reshape(-1, 128), sizes).reshape(-1)
    cuts = (width, width + table_grad.size, 2 * width + table_grad.size)
    return (
        jnp.stack(outputs),
        jnp.stack(input_grads),
        small[: cuts[0]],
        qkv_total,
        proj_total,
        small[cuts[0] : cuts[1]].reshape(table_grad.shape),
        small[cuts[1] : cuts[2]],
        small[cuts[2] :].reshape(router_grad.shape),
        in_total[None],
        out_total[None],
    )


def solution(mesh):
    rows = P(None, ("dp", "expert"), None)
    in_specs = (
        rows,
        rows,
        P(None, ("dp", "expert")),
        P(None, ("dp", "expert")),
        rows,
        P(),
        P(("dp", "expert"), None),
        P(("dp", "expert"), None),
        P(),
        P(),
        P(),
        P("expert", "dp", None),
        P("expert", "dp", None),
    )
    out_specs = (
        rows,
        rows,
        P(),
        P(("dp", "expert"), None),
        P(("dp", "expert"), None),
        P(),
        P(),
        P(),
        P("expert", "dp", None),
        P("expert", "dp", None),
    )
    return jax.shard_map(
        partial(on_device, dict(mesh.shape)),
        mesh=mesh,
        in_specs=in_specs,
        out_specs=out_specs,
        check_vma=False,
    )
```

```python
from functools import partial

import jax
import jax.numpy as jnp
from jax import lax
from jax.experimental import pallas as pl
from jax.experimental.pallas import tpu as pltpu
from jax.sharding import PartitionSpec as P

EPSILON = 1e-06
NEG_BIG = -1e30
LIMITS = (12, 16, 23, 32, 46, 64, 91)
F32 = jnp.float32
BF16 = jnp.bfloat16


def bucket_of(offset):
    distance = jnp.abs(offset)
    far_part = 8 + sum(((distance >= limit).astype(jnp.int32) for limit in LIMITS))
    near_far = jnp.where(distance < 8, distance, far_part)
    return jnp.where(offset > 0, 16, 0) + near_far


def slot_positions(routes, experts):
    order = jnp.concatenate([routes[:, 0], routes[:, 1]])
    chosen = (order[:, None] == jnp.arange(experts, dtype=jnp.int32)[None, :]).astype(jnp.int32)
    before = jnp.cumsum(chosen, axis=0) - chosen
    place = jnp.sum(before * chosen, axis=1)
    return place.reshape(2, -1).T


def tree_mask(segment, parent):
    same = segment[None, :] == segment[:, None]
    upward = segment[None, :] == parent[:, None]
    downward = parent[None, :] == segment[:, None]
    return same | upward | downward


def rms_scale(values):
    return lax.rsqrt(jnp.mean(values * values, axis=-1, keepdims=True) + EPSILON)


def gelu_product(gate_part, up_part):
    return jax.nn.gelu(gate_part, approximate=True) * up_part


def after(value, *others):
    return lax.optimization_barrier((value, others))[0]


def flip(value, axis, size, bit):
    return lax.ppermute(value, axis, [(i, i ^ bit) for i in range(size)])


def shift(value, axis, size, step):
    return lax.ppermute(value, axis, [(i, (i + step) % size) for i in range(size)])


def halving_orders(size):
    bits = [1 << k for k in range(1, size.bit_length() - 1)]
    return (bits, bits[::-1])


def gather_dp(block, size, hold):
    rows = block.shape[0]
    half = rows // 2
    columns = []
    for part, order in enumerate(halving_orders(size)):
        have = block[None, part * half : (part + 1) * half]
        rels = [0]
        for bit in order:
            if len(rels) == 2:
                have = after(have, hold)
            have = jnp.concatenate([have, flip(have, "dp", size, bit)], axis=0)
            rels = rels + [rel ^ bit for rel in rels]
        columns.append((have, rels))
    near = [columns[0][0], columns[1][0]]
    far = [flip(have, "dp", size, 1) for have in near]
    return near + far, [columns[0][1], columns[1][1]]


def gather_expert(block, size):
    me = lax.axis_index("expert")
    full = jnp.zeros((size,) + block.shape, block.dtype)
    for step in range(size):
        piece = shift(block, "expert", size, step) if step else block
        full = lax.dynamic_update_slice(full, piece[None], ((me - step) % size, 0, 0))
    return full.reshape(size * block.shape[0], block.shape[1])


def all_to_all(value):
    return lax.all_to_all(value, "expert", split_axis=0, concat_axis=0, tiled=True)


def split_bit(value, me, bit):
    mine = (me // bit) % 2
    kept = lax.dynamic_index_in_dim(value, mine, 0, keepdims=False)
    sent = lax.dynamic_index_in_dim(value, 1 - mine, 0, keepdims=False)
    return kept, sent


def scatter_core(total, size):
    me = lax.axis_index("dp")
    rows, width = total.shape[0] // size, total.shape[1]
    kept, sent = split_bit(jnp.moveaxis(total.reshape(size // 2, 2, rows, width), 1, 0), me, 1)
    return kept.astype(F32) + flip(sent, "dp", size, 1).astype(F32)


def scatter_dp(summed, size):
    me = lax.axis_index("dp")
    _, rows, width = summed.shape
    half = rows // 2
    outs = []
    for part, order in enumerate(halving_orders(size)):
        value = summed[:, part * half : (part + 1) * half]
        left = [1 << k for k in range(1, size.bit_length() - 1)]
        for bit in order:
            place = left.index(bit)
            high, low = 1 << (len(left) - 1 - place), 1 << place
            shaped = value.astype(BF16).reshape(high, 2, low, half, width)
            kept, sent = split_bit(jnp.moveaxis(shaped, 1, 0), me, bit)
            value = kept.astype(F32) + flip(sent, "dp", size, bit).astype(F32)
            left.remove(bit)
        outs.append(value.reshape(half, width))
    return jnp.concatenate(outs, axis=0)


def scatter_expert(total, size):
    rows = total.shape[0] // size
    low = total.astype(BF16).reshape(size, rows, total.shape[1])
    return jnp.sum(all_to_all(low).astype(F32), axis=0)


def sum_all(value, sizes):
    for axis in ("dp", "expert"):
        bit = 1
        while bit < sizes[axis]:
            value = value + flip(value, axis, sizes[axis], bit)
            bit *= 2
    return value


def dot(left, right):
    return jnp.dot(left, right, preferred_element_type=F32)


def dot_t(left, right):
    return lax.dot_general(left, right, (((1,), (1,)), ((), ())), preferred_element_type=F32)


def t_dot(left, right):
    return lax.dot_general(left, right, (((0,), (0,)), ((), ())), preferred_element_type=F32)

LIGHT = pl.CostEstimate(flops=1, bytes_accessed=1, transcendentals=0)


GELU_C = 0.7978845608028654
GELU_A = 0.044715


def expert_body(
    mine, x_ref, go_ref, wr_ref, wg_ref, wu_ref, wo_ref, *refs
):
    y_ref, dx_ref, gt_ref, du_ref, dy_ref, y_acc, dx_acc = refs[-7:]
    step, last = pl.program_id(0), pl.num_programs(0) - 1

    @pl.when(step == 0)
    def _():
        logits = dot(x_ref[...], wr_ref[...])
        lane = lax.broadcasted_iota(jnp.int32, logits.shape, 1)
        logits = jnp.where(lane < mine[1], logits, NEG_BIG)
        top = jnp.max(logits, axis=-1, keepdims=True)
        weights = jnp.exp(logits - top)
        total = jnp.sum(weights, axis=-1, keepdims=True)
        gate = jnp.sum(jnp.where(lane == mine[0], weights, 0.0), axis=-1, keepdims=True) / total
        dy_ref[...] = (gate * go_ref[...].astype(F32)).astype(BF16)
        y_acc[...] = jnp.zeros_like(y_acc)
        dx_acc[...] = jnp.zeros_like(dx_acc)

    x = x_ref[...]
    wg, wu, wo = wg_ref[...], wu_ref[...], wo_ref[...]
    a, b = dot(x, wg), dot(x, wu)
    dg = dot_t(dy_ref[...], wo)
    square = a * a
    t = jnp.tanh(GELU_C * (a + GELU_A * (a * square)))
    half = 0.5 + 0.5 * t
    act = a * half
    slope = half + (0.5 * GELU_C) * a * (1.0 - t * t) * (1.0 + (3.0 * GELU_A) * square)
    g = (act * b).astype(BF16)
    da = (dg * b * slope).astype(BF16)
    db = (dg * act).astype(BF16)
    gt_ref[...] = g.T
    du_ref[0] = da
    du_ref[1] = db
    y_acc[...] += dot(g, wo)
    dx_acc[...] += dot_t(jnp.concatenate([da, db], axis=1), jnp.concatenate([wg, wu], axis=1))

    @pl.when(step == last)
    def _():
        y = y_acc[...].astype(BF16)
        y_ref[...] = y
        width = y.shape[1]
        dx_ref[:, :width] = dx_acc[...].astype(BF16)
        product = go_ref[...].astype(F32) * y.astype(F32)
        rest = jnp.sum(product, axis=-1, keepdims=True)
        lane = lax.broadcasted_iota(jnp.int32, (y.shape[0], 128), 1)
        terms = jnp.zeros(lane.shape, F32)
        for place in range(3):
            term = rest.astype(BF16).astype(F32)
            terms = jnp.where(lane == place, term, terms)
            rest = rest - term
        dx_ref[:, width:] = terms.astype(BF16)


def tile_of(size, most):
    return max(t for t in range(128, most + 1, 128) if size % t == 0)


def expert_call(batch, batches, mine, x, go, w_router, w_in, w_out, held):
    rows, width = x.shape
    inner = w_out.shape[0]
    tile = tile_of(inner, 256)
    tiles = inner // tile
    whole = lambda shape: pl.BlockSpec(shape, lambda j: (0,) * len(shape))
    in_specs = [
        pl.BlockSpec(memory_space=pltpu.SMEM),
        whole((rows, width)),
        whole((rows, width)),
        whole(w_router.shape),
        pl.BlockSpec((width, tile), lambda j: (0, j)),
        pl.BlockSpec((width, tile), lambda j: (0, tiles + j)),
        pl.BlockSpec((tile, width), lambda j: (j, 0)),
    ]
    args = [mine, x, go, w_router, w_in, w_in, w_out]
    aliases = {}
    if held is not None:
        in_specs += [pl.BlockSpec(memory_space=pl.ANY)] * 3
        aliases = {len(args): 2, len(args) + 1: 3, len(args) + 2: 4}
        args += list(held)
    flops = 12 * rows * width * inner
    return pl.pallas_call(
        expert_body,
        grid=(tiles,),
        in_specs=in_specs,
        out_specs=[
            whole((rows, width)),
            whole((rows, width + 128)),
            pl.BlockSpec((tile, rows), lambda j: (j, batch)),
            pl.BlockSpec((2, rows, tile), lambda j: (0, batch, j)),
            pl.BlockSpec((rows, width), lambda j: (batch, 0)),
        ],
        out_shape=[
            jax.ShapeDtypeStruct((rows, width), BF16),
            jax.ShapeDtypeStruct((rows, width + 128), BF16),
            jax.ShapeDtypeStruct((inner, batches * rows), BF16),
            jax.ShapeDtypeStruct((2, batches * rows, inner), BF16),
            jax.ShapeDtypeStruct((batches * rows, width), BF16),
        ],
        scratch_shapes=[pltpu.VMEM((rows, width), F32), pltpu.VMEM((rows, width), F32)],
        input_output_aliases=aliases,
        compiler_params=pltpu.CompilerParams(vmem_limit_bytes=56 << 20),
        cost_estimate=LIGHT,
        name="expert",
    )(*args)


def weight_in_body(*refs):
    xs, du_ref, out_ref, flipped = refs[:-3], refs[-3], refs[-2], refs[-1]
    rows = xs[0].shape[0]

    @pl.when(pl.program_id(0) == 0)
    def _():
        for n, x_ref in enumerate(xs):
            flipped[:, n * rows : (n + 1) * rows] = x_ref[...].T

    out_ref[...] = dot(flipped[...], du_ref[0]).astype(BF16).reshape(out_ref.shape)


def weight_in_call(size, xs, du):
    rows, width = xs[0].shape
    _, total, inner = du.shape
    tile = tile_of(inner, 256)
    tiles = inner // tile
    part = width // size
    space = 2 * tiles * part + (inner // size) * (width // tile)
    return pl.pallas_call(
        weight_in_body,
        grid=(2 * tiles,),
        in_specs=[pl.BlockSpec((rows, width), lambda j: (0, 0)) for _ in xs]
        + [pl.BlockSpec((1, total, tile), lambda j: (j // tiles, 0, j % tiles))],
        out_specs=pl.BlockSpec((size, part, tile), lambda j: (0, j, 0)),
        out_shape=jax.ShapeDtypeStruct((size, space, tile), BF16),
        scratch_shapes=[pltpu.VMEM((width, total), BF16)],
        compiler_params=pltpu.CompilerParams(vmem_limit_bytes=56 << 20),
        cost_estimate=LIGHT,
        name="weight_in",
    )(*xs, du)


def weight_out_body(gt_ref, dy_ref, _, out_ref):
    out_ref[...] = dot(gt_ref[...], dy_ref[...]).astype(BF16).reshape(out_ref.shape)


def weight_out_call(gt, dy, joined):
    inner, total = gt.shape
    width = dy.shape[1]
    size, space, tile = joined.shape
    part = inner // size
    first = (space - part * (width // tile)) // part
    assert first * part + part * (width // tile) == space
    return pl.pallas_call(
        weight_out_body,
        grid=(width // tile,),
        in_specs=[
            pl.BlockSpec((inner, total), lambda j: (0, 0)),
            pl.BlockSpec((total, tile), lambda j: (0, j)),
            pl.BlockSpec(memory_space=pl.ANY),
        ],
        out_specs=pl.BlockSpec((size, part, tile), lambda j: (0, first + j, 0)),
        out_shape=jax.ShapeDtypeStruct(joined.shape, BF16),
        input_output_aliases={2: 0},
        compiler_params=pltpu.CompilerParams(vmem_limit_bytes=56 << 20),
        cost_estimate=LIGHT,
        name="weight_out",
    )(gt, dy, joined)


def lane_below(shape, limit):
    return lax.broadcasted_iota(jnp.int32, shape, 1) < limit


def allowed_keys(rows, columns):
    segment_q, parent_q = rows[0:1], rows[1:2]
    segment_k, parent_k = columns[:, 0:1], columns[:, 1:2]
    return (segment_k == segment_q) | (segment_k == parent_q) | (parent_k == segment_q)


def pair_scores(h, head_size, scale, q, k, bias, allowed):
    low = lane_below(k.shape, head_size)
    mine = low if h % 2 == 0 else ~low
    raw = dot_t(jnp.where(mine, k, jnp.zeros_like(k)), q) * scale + bias
    return jnp.where(allowed, raw, NEG_BIG)


def piece_moves(me, pieces, rels, whole, arrived):
    moves = []
    for number, piece in enumerate(pieces):
        part, other = number % 2, number // 2
        half = piece.shape[1]
        for place, rel in enumerate(rels[part]):
            row = pl.multiple_of((me ^ rel ^ other) * (2 * half) + part * half, half)
            moves.append(
                pltpu.make_async_copy(
                    piece.at[place], whole.at[pl.ds(row, half)], arrived.at[len(moves)]
                )
            )
            moves[-1].start()
    return moves


def join_body(rels, me_ref, *refs):
    pieces, whole, arrived = refs[:-2], refs[-2], refs[-1]
    for move in piece_moves(me_ref[0], pieces, rels, whole, arrived):
        move.wait()


def join_call(me, pieces, rels):
    outside = pl.BlockSpec(memory_space=pl.ANY)
    count = 4 * len(rels[0])
    return pl.pallas_call(
        partial(join_body, rels),
        in_specs=[pl.BlockSpec(memory_space=pltpu.SMEM)] + [outside] * len(pieces),
        out_specs=pl.BlockSpec(memory_space=pltpu.VMEM),
        out_shape=jax.ShapeDtypeStruct((count * pieces[0].shape[1], pieces[0].shape[2]), BF16),
        scratch_shapes=[pltpu.SemaphoreType.DMA((count,))],
        cost_estimate=LIGHT,
        name="join",
    )(me, *pieces)


def forward_body(heads, experts, rels, *refs):
    if rels is None:
        weights_ref, refs = refs[0], refs[1:]
    else:
        me_ref, pieces, refs = refs[0], refs[1:5], refs[5:]
        refs, (full_ref, weights_ref, arrived, written) = refs[:-4], refs[-4:]
        moves = piece_moves(me_ref[0], pieces, rels, weights_ref, arrived)
    (
        tokens_ref,
        gain1_ref,
        bias_ref,
        rows_ref,
        columns_ref,
        gain2_ref,
        router_ref,
        targets_ref,
        x_ref,
        n1_ref,
        qkv_ref,
        lse_ref,
        o_ref,
        h1_ref,
        probs_ref,
    ) = refs
    length, width = tokens_ref.shape
    head_size = width // heads
    scale = head_size ** (-0.5)
    h0 = tokens_ref[...].astype(F32)
    n1 = (h0 * rms_scale(h0) * gain1_ref[...]).astype(BF16)
    n1_ref[...] = n1
    if rels is not None:
        for move in moves:
            move.wait()
        keep = pltpu.make_async_copy(weights_ref, full_ref, written)
        keep.start()
    for part in range(3):
        columns = slice(part * width, (part + 1) * width)
        qkv_ref[:, columns] = dot(n1, weights_ref[:, columns]).astype(BF16)
    allowed = allowed_keys(rows_ref[...], columns_ref[...])
    span = 2 * head_size
    for pair in range(heads // 2):
        at = pair * span
        q = qkv_ref[:, at : at + span]
        k = qkv_ref[:, width + at : width + at + span]
        flipped = qkv_ref[:, 2 * width + at : 2 * width + at + span].T
        parts = []
        for half in range(2):
            h = 2 * pair + half
            s = pair_scores(h, head_size, scale, q, k, bias_ref[h], allowed)
            top = jnp.max(s, axis=0, keepdims=True)
            e = jnp.exp(s - top)
            total = jnp.sum(e, axis=0, keepdims=True)
            lse_ref[h : h + 1] = top + jnp.log(total)
            p = (e * (1.0 / total)).astype(BF16)
            parts.append(dot(flipped[half * head_size : (half + 1) * head_size], p))
        o_ref[:, at : at + span] = jnp.concatenate(parts, axis=0).T.astype(BF16)
    h1 = h0 + dot(o_ref[...], weights_ref[:, 3 * width :])
    h1_ref[...] = h1
    n2 = (h1 * rms_scale(h1) * gain2_ref[...]).astype(BF16)
    logits = dot(n2, router_ref[...])
    logits = jnp.where(lane_below(logits.shape, experts), logits, NEG_BIG)
    top = jnp.max(logits, axis=-1, keepdims=True)
    e = jnp.exp(logits - top)
    probs_ref[...] = e / jnp.sum(e, axis=-1, keepdims=True)
    slots = lax.broadcasted_iota(jnp.int32, (x_ref.shape[0], length), 0)
    place = (slots == targets_ref[0:1]) | (slots == targets_ref[1:2])
    x_ref[...] = dot(place.astype(F32).astype(BF16), n2).astype(BF16)
    if rels is not None:
        keep.wait()


def forward_call(heads, experts, slot_count, weights, rels, *args):
    length, width = args[0].shape
    shapes = [
        ((slot_count, width), BF16),
        ((length, width), BF16),
        ((length, 3 * width), BF16),
        ((heads, length), F32),
        ((length, width), BF16),
        ((length, width), F32),
        ((length, 128), F32),
    ]
    inside = pl.BlockSpec(memory_space=pltpu.VMEM)
    outside = pl.BlockSpec(memory_space=pl.ANY)
    in_specs = [inside] * len(args)
    out_specs = [inside] * len(shapes)
    scratch = []
    if rels is None:
        args, in_specs = (weights,) + args, [inside] + in_specs
    else:
        me, pieces = weights
        args = (me, *pieces) + args
        in_specs = [pl.BlockSpec(memory_space=pltpu.SMEM)] + [outside] * len(pieces) + in_specs
        shapes.append(((width, 4 * width), BF16))
        out_specs.append(outside)
        scratch = [
            pltpu.VMEM((width, 4 * width), BF16),
            pltpu.SemaphoreType.DMA((4 * len(rels[0]),)),
            pltpu.SemaphoreType.DMA,
        ]
    return pl.pallas_call(
        partial(forward_body, heads, experts, rels),
        in_specs=in_specs,
        out_specs=out_specs,
        out_shape=[jax.ShapeDtypeStruct(*s) for s in shapes],
        scratch_shapes=scratch,
        compiler_params=pltpu.CompilerParams(vmem_limit_bytes=56 << 20),
        cost_estimate=LIGHT,
        name="attention_forward",
    )(*args)


def backward_body(
    heads,
    experts,
    dx_ref,
    targets_ref,
    routes_ref,
    probs_ref,
    h1_ref,
    go_ref,
    gain2_ref,
    router_ref,
    proj_ref,
    qkv_ref,
    lse_ref,
    bias_ref,
    rows_ref,
    columns_ref,
    dh1_ref,
    dbranch_ref,
    dqkv_ref,
    ds_ref,
    router_grad_ref,
    gain_grad_ref,
    do_ref,
):
    length, width = h1_ref.shape
    head_size = width // heads
    scale = head_size ** (-0.5)
    slots = lax.broadcasted_iota(jnp.int32, (length, dx_ref.shape[0]), 1)
    hot = [slots == targets_ref[:, j : j + 1] for j in range(2)]
    pick = [m.astype(F32).astype(BF16) for m in hot]
    dgate = [jnp.sum(dot(m, dx_ref[:, width:]), axis=-1, keepdims=True) for m in pick]
    probs = probs_ref[...]
    lane = lax.broadcasted_iota(jnp.int32, probs.shape, 1)
    dprobs = sum(jnp.where(lane == routes_ref[:, j : j + 1], dgate[j], 0.0) for j in range(2))
    dlogits = probs * (dprobs - jnp.sum(probs * dprobs, axis=-1, keepdims=True))
    dlogits = dlogits.astype(BF16)
    dn2 = dot(pick[0] + pick[1], dx_ref[:, :width]) + dot_t(dlogits, router_ref[...])
    h1 = h1_ref[...]
    r2 = rms_scale(h1)
    n2_hat = h1 * r2
    gain2 = gain2_ref[...]
    n2 = (n2_hat * gain2).astype(BF16)
    router_grad_ref[...] = t_dot(dlogits, n2)
    gain_grad_ref[...] = jnp.sum(dn2 * n2_hat, axis=0, keepdims=True)
    scaled = dn2 * gain2
    mean = jnp.mean(scaled * n2_hat, axis=-1, keepdims=True)
    dh1 = go_ref[...].astype(F32) + r2 * (scaled - n2_hat * mean)
    dh1_ref[...] = dh1
    dbranch = dh1.astype(BF16)
    dbranch_ref[...] = dbranch
    do_ref[...] = dot_t(dbranch, proj_ref[...]).astype(BF16)
    allowed = allowed_keys(rows_ref[...], columns_ref[...])
    span = 2 * head_size
    low = lane_below((length, span), head_size)
    for pair in range(heads // 2):
        at = pair * span
        q = qkv_ref[:, at : at + span]
        k = qkv_ref[:, width + at : width + at + span]
        v = qkv_ref[:, 2 * width + at : 2 * width + at + span]
        do = do_ref[:, at : at + span]
        flipped = k.T
        dq, dk, dv = [], [], []
        for half in range(2):
            h = 2 * pair + half
            s = pair_scores(h, head_size, scale, q, k, bias_ref[h], allowed)
            p = jnp.exp(s - lse_ref[h : h + 1])
            mine = low if half == 0 else ~low
            dp = dot_t(jnp.where(mine, v, jnp.zeros_like(v)), do)
            inner = jnp.sum(p * dp, axis=0, keepdims=True)
            ds = (p * (dp - inner)).astype(BF16)
            ds_ref[h] = ds
            dv.append(dot(p.astype(BF16), do))
            dk.append(dot(ds, q))
            dq.append(dot(flipped[half * head_size : (half + 1) * head_size], ds))
        dqkv_ref[:, at : at + span] = (jnp.concatenate(dq, axis=0).T * scale).astype(BF16)
        dqkv_ref[:, width + at : width + at + span] = (jnp.where(low, *dk) * scale).astype(BF16)
        dqkv_ref[:, 2 * width + at : 2 * width + at + span] = jnp.where(low, *dv).astype(BF16)


def backward_call(heads, experts, dx, targets, routes, probs, h1, go, gain2, router, proj, *rest):
    length, width = h1.shape
    shapes = [
        ((length, width), F32),
        ((length, width), BF16),
        ((length, 3 * width), BF16),
        ((heads, length, length), BF16),
        ((128, width), F32),
        ((1, width), F32),
    ]
    args = (dx, targets, routes, probs, h1, go, gain2, router, proj) + rest
    in_specs = [pl.BlockSpec(a.shape, lambda i, n=a.ndim: (0,) * n) for a in args]
    in_specs[8] = pl.BlockSpec((width, width), lambda i: (0, 3))
    return pl.pallas_call(
        partial(backward_body, heads, experts),
        grid=(1,),
        in_specs=in_specs,
        out_specs=[pl.BlockSpec(s, lambda i, n=len(s): (0,) * n) for s, _ in shapes],
        out_shape=[jax.ShapeDtypeStruct(*s) for s in shapes],
        scratch_shapes=[pltpu.VMEM((length, width), BF16)],
        compiler_params=pltpu.CompilerParams(vmem_limit_bytes=56 << 20),
        cost_estimate=LIGHT,
        name="attention_backward",
    )(*args)


def on_device(
    sizes,
    tokens,
    cotangent,
    segment_ids,
    parent_ids,
    routes,
    gain_attn,
    w_qkv,
    w_proj,
    rel_bias,
    gain_moe,
    w_router,
    w_in,
    w_out,
):
    dp, experts = sizes["dp"], sizes["expert"]
    batches, length, width = tokens.shape
    heads = rel_bias.shape[1]
    head_size = width // heads
    inner = w_in.shape[2] // 2
    capacity = (10 * length + 4 * experts - 1) // (4 * experts)
    slot_count = experts * capacity
    scale = head_size ** (-0.5)
    me_e = lax.axis_index("expert")

    attn_block = gather_expert(jnp.concatenate([w_qkv, w_proj], axis=1), experts)
    places = jax.vmap(partial(slot_positions, experts=experts))(routes)
    targets = routes * capacity + places
    hot = targets[..., None] == jnp.arange(slot_count, dtype=jnp.int32)
    select = hot.astype(BF16)
    both = select[:, :, 0] + select[:, :, 1]
    out_grads = [cotangent[n] for n in range(batches)]
    outgoing = [
        t_dot(both[n], out_grads[n]).astype(BF16).reshape(experts, capacity, width)
        for n in range(batches)
    ]
    go_slots = [all_to_all(after(v, attn_block)) for v in outgoing]

    positions = jnp.arange(length, dtype=jnp.int32)
    buckets = bucket_of(positions[:, None] - positions[None, :])
    bucket_hot = (buckets[:, :, None] == jnp.arange(rel_bias.shape[0], dtype=jnp.int32)).astype(F32)
    bias = jnp.einsum("kqc,ch->hkq", bucket_hot, rel_bias, precision=lax.Precision.HIGHEST)

    me_d = lax.axis_index("dp").astype(jnp.int32)[None]
    out_pieces, rels = gather_dp(w_out[0], dp, ())
    wout_full = join_call(me_d, out_pieces, rels)
    pieces, _ = gather_dp(after(attn_block, out_pieces[:2]), dp, (bias, outgoing))
    win_full = lax.all_gather(
        after(w_in[0], pieces[:2], go_slots[0]), "dp", axis=0, tiled=True
    )

    router_wide = jnp.pad(w_router, ((0, 0), (0, 128 - experts)))
    gain1, gain2 = gain_attn[None], gain_moe[None]
    saved = []
    for n in range(batches):
        id_rows = jnp.stack([segment_ids[n], parent_ids[n]])
        target_columns = targets[n]
        weights = attn_w if n else (me_d, pieces)
        outs = forward_call(
            heads,
            experts,
            slot_count,
            weights,
            None if n else rels,
            tokens[n],
            gain1,
            bias,
            id_rows,
            id_rows.T,
            gain2,
            router_wide,
            target_columns.T,
        )
        if n == 0:
            *outs, attn_w = outs
        x_slots = all_to_all(after(outs[0], go_slots).reshape(experts, capacity, width))
        saved.append((id_rows,) + tuple(outs[1:]) + (x_slots,))

    mine = jnp.stack([me_e, jnp.int32(experts)]).astype(jnp.int32)
    held, grads = [], None
    for n in range(batches):
        x = saved[n][-1].reshape(slot_count, width)
        go = go_slots[n].reshape(slot_count, width)
        y, dx, *grads = expert_call(
            n, batches, mine, x, go, router_wide, win_full, wout_full, grads
        )
        dx_back = all_to_all(dx.reshape(experts, capacity, width + 128))
        held.append((x, dx_back.reshape(slot_count, width + 128), y))
    y_back = all_to_all(
        jnp.stack([h[2].reshape(experts, capacity, width) for h in held], axis=1)
    )

    def backward(n, dx_back):
        id_rows, _, qkv, lse, _, h1, probs, _ = saved[n]
        return backward_call(
            heads,
            experts,
            dx_back,
            targets[n],
            routes[n],
            probs,
            h1,
            out_grads[n],
            gain2,
            router_wide,
            attn_w,
            qkv,
            lse,
            bias,
            id_rows,
            id_rows.T,
        )

    gt, du, dy = grads
    joined = weight_in_call(dp, [h[0] for h in held], after(du, held[0][1]))
    backs = []
    for n in range(batches):
        backs.append(backward(n, after(held[n][1], joined)))
        if n == 0:
            joined = weight_out_call(after(gt, held[-1][1], backs[0]), dy, joined)
    space, tile = joined.shape[1:]
    summed = lax.psum_scatter(
        joined.reshape(dp * space, tile), "dp", scatter_dimension=0, tiled=True
    )
    part_in, part_out = w_in.shape[1], w_out.shape[1]
    cut = (w_in.shape[2] // tile) * part_in
    in_total = summed[:cut].reshape(-1, part_in, tile).transpose(1, 0, 2)
    in_total = in_total.reshape(part_in, -1).astype(F32)
    out_total = summed[cut:].reshape(-1, part_out, tile).transpose(1, 0, 2)
    out_total = out_total.reshape(part_out, -1).astype(F32)

    outputs, input_grads = [], []
    full_qkv = attn_w[:, : 3 * width]
    n1_all, o_all, dbranch_all, dqkv_all = (
        jnp.concatenate(parts, axis=0)
        for parts in (
            [v[1] for v in saved],
            [v[4] for v in saved],
            [v[1] for v in backs],
            [v[2] for v in backs],
        )
    )
    qkv_part = t_dot(n1_all, dqkv_all)
    proj_part = t_dot(o_all, dbranch_all)
    attn_part = jnp.concatenate([qkv_part, proj_part], axis=1).astype(BF16)
    attn_core = scatter_core(attn_part, dp)
    attn_sum = scatter_dp(attn_core, dp)
    router_grad = sum(v[4] for v in backs)[:experts].T
    gain_moe_grad = sum(v[5] for v in backs)[0]
    table_grad = jnp.einsum(
        "nhkq,kqc->ch",
        after(jnp.stack([v[3] for v in backs]), attn_core),
        bucket_hot.astype(BF16),
        preferred_element_type=F32,
    )
    gain_attn_grad = 0.0
    for n in range(batches):
        _, n1, _, _, _, h1, probs, _ = saved[n]
        dh1, _, dqkv, _, _, _ = backs[n]
        y_n = after(y_back, attn_sum)[:, n].reshape(slot_count, width)
        route_hot = (routes[n][:, :, None] == jnp.arange(experts, dtype=jnp.int32)).astype(F32)
        gates = jnp.sum(probs[:, None, :experts] * route_hot, axis=-1)
        picked0, picked1 = dot(select[n][:, 0], y_n), dot(select[n][:, 1], y_n)
        moe = gates[:, :1] * picked0 + gates[:, 1:] * picked1
        outputs.append((h1 + moe).astype(BF16))
        h0 = tokens[n].astype(F32)
        r1 = rms_scale(h0)
        n1_hat = h0 * r1
        dn1 = dot_t(after(dqkv, attn_core), full_qkv)
        gain_attn_grad = gain_attn_grad + jnp.sum(dn1 * n1_hat, axis=0)
        scaled = dn1 * gain_attn
        input_grad = dh1 + r1 * (
            scaled - n1_hat * jnp.mean(scaled * n1_hat, axis=-1, keepdims=True)
        )
        input_grads.append(input_grad.astype(BF16))

    attn_total = scatter_expert(attn_sum, experts)
    qkv_total, proj_total = attn_total[:, : 3 * width], attn_total[:, 3 * width :]
    small = jnp.concatenate(
        [gain_attn_grad, table_grad.reshape(-1), gain_moe_grad, router_grad.reshape(-1)]
    )
    small = sum_all(after(small.reshape(-1, 128), attn_sum), sizes).reshape(-1)
    cuts = (width, width + table_grad.size, 2 * width + table_grad.size)
    return (
        jnp.stack(outputs),
        jnp.stack(input_grads),
        small[: cuts[0]],
        qkv_total,
        proj_total,
        small[cuts[0] : cuts[1]].reshape(table_grad.shape),
        small[cuts[1] : cuts[2]],
        small[cuts[2] :].reshape(router_grad.shape),
        in_total[None],
        out_total[None],
    )


def solution(mesh):
    rows = P(None, ("dp", "expert"), None)
    in_specs = (
        rows,
        rows,
        P(None, ("dp", "expert")),
        P(None, ("dp", "expert")),
        rows,
        P(),
        P(("dp", "expert"), None),
        P(("dp", "expert"), None),
        P(),
        P(),
        P(),
        P("expert", "dp", None),
        P("expert", "dp", None),
    )
    out_specs = (
        rows,
        rows,
        P(),
        P(("dp", "expert"), None),
        P(("dp", "expert"), None),
        P(),
        P(),
        P(),
        P("expert", "dp", None),
        P("expert", "dp", None),
    )
    return jax.shard_map(
        partial(on_device, dict(mesh.shape)),
        mesh=mesh,
        in_specs=in_specs,
        out_specs=out_specs,
        check_vma=False,
    )
```

```python
from functools import partial

import jax
import jax.numpy as jnp
from jax import lax
from jax.experimental import pallas as pl
from jax.experimental.pallas import tpu as pltpu
from jax.sharding import PartitionSpec as P

EPSILON = 1e-06
NEG_BIG = -1e30
LIMITS = (12, 16, 23, 32, 46, 64, 91)
F32 = jnp.float32
BF16 = jnp.bfloat16


def bucket_of(offset):
    distance = jnp.abs(offset)
    far_part = 8 + sum(((distance >= limit).astype(jnp.int32) for limit in LIMITS))
    near_far = jnp.where(distance < 8, distance, far_part)
    return jnp.where(offset > 0, 16, 0) + near_far


def slot_positions(routes, experts):
    order = jnp.concatenate([routes[:, 0], routes[:, 1]])
    chosen = (order[:, None] == jnp.arange(experts, dtype=jnp.int32)[None, :]).astype(jnp.int32)
    before = jnp.cumsum(chosen, axis=0) - chosen
    place = jnp.sum(before * chosen, axis=1)
    return place.reshape(2, -1).T


def tree_mask(segment, parent):
    same = segment[None, :] == segment[:, None]
    upward = segment[None, :] == parent[:, None]
    downward = parent[None, :] == segment[:, None]
    return same | upward | downward


def rms_scale(values):
    return lax.rsqrt(jnp.mean(values * values, axis=-1, keepdims=True) + EPSILON)


def gelu_product(gate_part, up_part):
    return jax.nn.gelu(gate_part, approximate=True) * up_part


def after(value, *others):
    return lax.optimization_barrier((value, others))[0]


def flip(value, axis, size, bit):
    return lax.ppermute(value, axis, [(i, i ^ bit) for i in range(size)])


def shift(value, axis, size, step):
    return lax.ppermute(value, axis, [(i, (i + step) % size) for i in range(size)])


def halving_orders(size):
    bits = [1 << k for k in range(1, size.bit_length() - 1)]
    return (bits, bits[::-1])


def gather_first(block, size, hold):
    half = block.shape[0] // 2
    out = []
    for part, order in enumerate(halving_orders(size)):
        have = after(block[None, part * half : (part + 1) * half], hold)
        out.append(jnp.concatenate([have, flip(have, "dp", size, order[0])], axis=0))
    return out


def gather_dp(first, size, hold):
    near, rels = [], []
    for have, order in zip(first, halving_orders(size)):
        have = after(have, hold)
        order_rels = [0, order[0]]
        for bit in order[1:]:
            have = jnp.concatenate([have, flip(have, "dp", size, bit)], axis=0)
            order_rels = order_rels + [rel ^ bit for rel in order_rels]
        near.append(have)
        rels.append(order_rels)
    far = [flip(have, "dp", size, 1) for have in near]
    return near + far, rels


def gather_expert(block, size):
    me = lax.axis_index("expert")
    full = jnp.zeros((size,) + block.shape, block.dtype)
    for step in range(size):
        piece = shift(block, "expert", size, step) if step else block
        full = lax.dynamic_update_slice(full, piece[None], ((me - step) % size, 0, 0))
    return full.reshape(size * block.shape[0], block.shape[1])


def all_to_all(value):
    return lax.all_to_all(value, "expert", split_axis=0, concat_axis=0, tiled=True)


def split_bit(value, me, bit):
    mine = (me // bit) % 2
    kept = lax.dynamic_index_in_dim(value, mine, 0, keepdims=False)
    sent = lax.dynamic_index_in_dim(value, 1 - mine, 0, keepdims=False)
    return kept, sent


def scatter_core(keep, send, size):
    return (keep.astype(F32) + flip(send, "dp", size, 1).astype(F32)).astype(BF16)


def scatter_dp(summed, size, hold):
    me = lax.axis_index("dp")
    _, rows, width = summed.shape
    half = rows // 2
    outs = []
    for part, order in enumerate(halving_orders(size)):
        value = summed[:, part * half : (part + 1) * half]
        left = [1 << k for k in range(1, size.bit_length() - 1)]
        for bit in order:
            place = left.index(bit)
            high, low = 1 << (len(left) - 1 - place), 1 << place
            shaped = value.astype(BF16).reshape(high, 2, low, half, width)
            kept, sent = split_bit(jnp.moveaxis(shaped, 1, 0), me, bit)
            value = kept.astype(F32) + after(flip(sent, "dp", size, bit), hold).astype(F32)
            left.remove(bit)
        outs.append(value.reshape(half, width))
    return jnp.concatenate(outs, axis=0)


def scatter_expert(total, size):
    rows = total.shape[0] // size
    low = total.astype(BF16).reshape(size, rows, total.shape[1])
    return jnp.sum(all_to_all(low).astype(F32), axis=0)


def sum_over(value, axis, size):
    bit = 1
    while bit < size:
        value = value + flip(value, axis, size, bit)
        bit *= 2
    return value


def sum_ring(value, axis, size):
    terms = [shift(value, axis, size, step) if step else value for step in range(size)]
    while len(terms) > 1:
        half = len(terms) // 2
        terms = [terms[k] + terms[k + half] for k in range(half)]
    return terms[0]


def dot(left, right):
    return jnp.dot(left, right, preferred_element_type=F32)


def dot_t(left, right):
    return lax.dot_general(left, right, (((1,), (1,)), ((), ())), preferred_element_type=F32)


def t_dot(left, right):
    return lax.dot_general(left, right, (((0,), (0,)), ((), ())), preferred_element_type=F32)

LIGHT = pl.CostEstimate(flops=1, bytes_accessed=1, transcendentals=0)


GELU_C = 0.7978845608028654
GELU_A = 0.044715


def expert_body(
    mine, x_ref, go_ref, wr_ref, wg_ref, wu_ref, wo_ref, *refs
):
    y_ref, dx_ref, gt_ref, du_ref, dy_ref, y_acc, dx_acc = refs[-7:]
    step, last = pl.program_id(0), pl.num_programs(0) - 1

    @pl.when(step == 0)
    def _():
        logits = dot(x_ref[...], wr_ref[...])
        lane = lax.broadcasted_iota(jnp.int32, logits.shape, 1)
        logits = jnp.where(lane < mine[1], logits, NEG_BIG)
        top = jnp.max(logits, axis=-1, keepdims=True)
        weights = jnp.exp(logits - top)
        total = jnp.sum(weights, axis=-1, keepdims=True)
        gate = jnp.sum(jnp.where(lane == mine[0], weights, 0.0), axis=-1, keepdims=True) / total
        dy_ref[...] = (gate * go_ref[...].astype(F32)).astype(BF16)
        y_acc[...] = jnp.zeros_like(y_acc)
        dx_acc[...] = jnp.zeros_like(dx_acc)

    x = x_ref[...]
    wg, wu, wo = wg_ref[...], wu_ref[...], wo_ref[...]
    a, b = dot(x, wg), dot(x, wu)
    dg = dot_t(dy_ref[...], wo)
    square = a * a
    t = jnp.tanh(GELU_C * (a + GELU_A * (a * square)))
    half = 0.5 + 0.5 * t
    act = a * half
    slope = half + (0.5 * GELU_C) * a * (1.0 - t * t) * (1.0 + (3.0 * GELU_A) * square)
    g = (act * b).astype(BF16)
    da = (dg * b * slope).astype(BF16)
    db = (dg * act).astype(BF16)
    gt_ref[...] = g.T
    du_ref[0] = da
    du_ref[1] = db
    y_acc[...] += dot(g, wo)
    dx_acc[...] += dot_t(jnp.concatenate([da, db], axis=1), jnp.concatenate([wg, wu], axis=1))

    @pl.when(step == last)
    def _():
        y = y_acc[...].astype(BF16)
        y_ref[:, 0] = y.reshape(-1, *y_ref.shape[2:])
        width = y.shape[1]
        dx_ref[:, :width] = dx_acc[...].astype(BF16)
        product = go_ref[...].astype(F32) * y.astype(F32)
        rest = jnp.sum(product, axis=-1, keepdims=True)
        lane = lax.broadcasted_iota(jnp.int32, (y.shape[0], 128), 1)
        terms = jnp.zeros(lane.shape, F32)
        for place in range(3):
            term = rest.astype(BF16).astype(F32)
            terms = jnp.where(lane == place, term, terms)
            rest = rest - term
        dx_ref[:, width:] = terms.astype(BF16)


def tile_of(size, most):
    return max(t for t in range(128, most + 1, 128) if size % t == 0)


def expert_call(batch, batches, experts, mine, x, go, w_router, w_in, w_out, held):
    rows, width = x.shape
    inner = w_out.shape[0]
    tile = tile_of(inner, 256)
    tiles = inner // tile
    whole = lambda shape: pl.BlockSpec(shape, lambda j: (0,) * len(shape))
    in_specs = [
        pl.BlockSpec(memory_space=pltpu.SMEM),
        whole((rows, width)),
        whole((rows, width)),
        whole(w_router.shape),
        pl.BlockSpec((width, tile), lambda j: (0, j)),
        pl.BlockSpec((width, tile), lambda j: (0, tiles + j)),
        pl.BlockSpec((tile, width), lambda j: (j, 0)),
    ]
    args = [mine, x, go, w_router, w_in, w_in, w_out]
    aliases = {}
    if held is not None:
        in_specs += [pl.BlockSpec(memory_space=pl.ANY)] * 4
        aliases = {len(args): 0, len(args) + 1: 2, len(args) + 2: 3, len(args) + 3: 4}
        args += list(held)
    flops = 12 * rows * width * inner
    return pl.pallas_call(
        expert_body,
        grid=(tiles,),
        in_specs=in_specs,
        out_specs=[
            pl.BlockSpec((experts, 1, rows // experts, width), lambda j: (0, batch, 0, 0)),
            whole((rows, width + 128)),
            pl.BlockSpec((tile, rows), lambda j: (j, batch)),
            pl.BlockSpec((2, rows, tile), lambda j: (0, batch, j)),
            pl.BlockSpec((rows, width), lambda j: (batch, 0)),
        ],
        out_shape=[
            jax.ShapeDtypeStruct((experts, batches, rows // experts, width), BF16),
            jax.ShapeDtypeStruct((rows, width + 128), BF16),
            jax.ShapeDtypeStruct((inner, batches * rows), BF16),
            jax.ShapeDtypeStruct((2, batches * rows, inner), BF16),
            jax.ShapeDtypeStruct((batches * rows, width), BF16),
        ],
        scratch_shapes=[pltpu.VMEM((rows, width), F32), pltpu.VMEM((rows, width), F32)],
        input_output_aliases=aliases,
        compiler_params=pltpu.CompilerParams(vmem_limit_bytes=56 << 20),
        cost_estimate=LIGHT,
        name="expert",
    )(*args)


def keep_and_send(value, core, keep_ref, send_ref, place):
    value = value.reshape((-1, 2) + value.shape[1:])
    even, odd = value[:, 0], value[:, 1]
    keep_ref[place] = jnp.where(core == 0, even, odd)
    send_ref[place] = jnp.where(core == 0, odd, even)


def weight_in_body(*refs):
    xs, du_ref, out_ref, flipped = refs[:-3], refs[-3], refs[-2], refs[-1]
    rows = xs[0].shape[0]

    @pl.when(pl.program_id(0) == 0)
    def _():
        for n, x_ref in enumerate(xs):
            flipped[:, n * rows : (n + 1) * rows] = x_ref[...].T

    tile = out_ref.shape[2]
    part = flipped.shape[0] // out_ref.shape[0]
    for place in range(out_ref.shape[1] // part):
        value = dot(flipped[...], du_ref[0, :, place * tile : (place + 1) * tile]).astype(BF16)
        out_ref[:, place * part : (place + 1) * part] = value.reshape(-1, part, tile)


def weight_in_call(size, xs, du):
    rows, width = xs[0].shape
    _, total, inner = du.shape
    tile = tile_of(inner, 256)
    tiles = inner // tile
    part = width // size
    space = 2 * tiles * part + (inner // size) * (width // tile)
    return pl.pallas_call(
        weight_in_body,
        grid=(2,),
        in_specs=[pl.BlockSpec((rows, width), lambda j: (0, 0)) for _ in xs]
        + [pl.BlockSpec((1, total, inner), lambda j: (j, 0, 0))],
        out_specs=pl.BlockSpec((size, tiles * part, tile), lambda j: (0, j, 0)),
        out_shape=jax.ShapeDtypeStruct((size, space, tile), BF16),
        scratch_shapes=[pltpu.VMEM((width, total), BF16)],
        compiler_params=pltpu.CompilerParams(vmem_limit_bytes=56 << 20),
        cost_estimate=LIGHT,
        name="weight_in",
    )(*xs, du)


def weight_out_body(gt_ref, dy_ref, _, out_ref):
    out_ref[...] = dot(gt_ref[...], dy_ref[...]).astype(BF16).reshape(out_ref.shape)


def weight_out_call(gt, dy, joined):
    inner, total = gt.shape
    width = dy.shape[1]
    size, space, tile = joined.shape
    part = inner // size
    first = (space - part * (width // tile)) // part
    assert first * part + part * (width // tile) == space
    return pl.pallas_call(
        weight_out_body,
        grid=(width // tile,),
        in_specs=[
            pl.BlockSpec((inner, total), lambda j: (0, 0)),
            pl.BlockSpec((total, tile), lambda j: (0, j)),
            pl.BlockSpec(memory_space=pl.ANY),
        ],
        out_specs=pl.BlockSpec((size, part, tile), lambda j: (0, first + j, 0)),
        out_shape=jax.ShapeDtypeStruct(joined.shape, BF16),
        input_output_aliases={2: 0},
        compiler_params=pltpu.CompilerParams(vmem_limit_bytes=56 << 20),
        cost_estimate=LIGHT,
        name="weight_out",
    )(gt, dy, joined)


def spread_body(count, summed_ref, in_ref, out_ref):
    part, tile = in_ref.shape[0], summed_ref.shape[1]
    for place in range(count):
        piece = summed_ref[place * part : (place + 1) * part]
        in_ref[:, place * tile : (place + 1) * tile] = piece.astype(F32)
    base, part = count * part, out_ref.shape[0]
    for place in range(out_ref.shape[1] // tile):
        piece = summed_ref[base + place * part : base + (place + 1) * part]
        out_ref[:, place * tile : (place + 1) * tile] = piece.astype(F32)


def spread_call(summed, in_shape, out_shape):
    return pl.pallas_call(
        partial(spread_body, in_shape[1] // summed.shape[1]),
        out_shape=[jax.ShapeDtypeStruct(shape, F32) for shape in (in_shape, out_shape)],
        compiler_params=pltpu.CompilerParams(vmem_limit_bytes=56 << 20),
        cost_estimate=LIGHT,
        name="spread",
    )(summed)


def weight_attn_body(count, core_ref, *refs):
    n1s, os, dqkvs, dbranches = (refs[k * count : (k + 1) * count] for k in range(4))
    keep_ref, send_ref, flipped, right = refs[4 * count :]
    step, last = pl.program_id(0), pl.num_programs(0) - 1
    length = n1s[0].shape[0]
    blocks = 2 * keep_ref.shape[0]

    def fill(lefts, rights):
        for n in range(count):
            if lefts is not None:
                flipped[:, n * length : (n + 1) * length] = lefts[n][...].T
            right[n * length : (n + 1) * length] = rights[n][...]

    @pl.when(step == 0)
    def _():
        fill(n1s, dqkvs)

    @pl.when((step > 0) & (step < last))
    def _():
        fill(None, dqkvs)

    @pl.when(step == last)
    def _():
        fill(os, dbranches)

    value = dot(flipped[...], right[...]).astype(BF16)
    value = value.reshape(blocks, -1, value.shape[1])
    keep_and_send(value, core_ref[0], keep_ref, send_ref, slice(None))


def weight_attn_call(size, core, n1s, os, dqkvs, dbranches):
    count = len(n1s)
    length, width = n1s[0].shape
    whole = pl.BlockSpec((length, width), lambda j: (0, 0))
    half = pl.BlockSpec((size // 2, width // size, width), lambda j: (0, 0, j))
    return pl.pallas_call(
        partial(weight_attn_body, count),
        grid=(4,),
        in_specs=[pl.BlockSpec(memory_space=pltpu.SMEM)]
        + [whole] * (2 * count)
        + [pl.BlockSpec((length, width), lambda j: (0, jnp.minimum(j, 2)))] * count
        + [whole] * count,
        out_specs=[half, half],
        out_shape=[jax.ShapeDtypeStruct((size // 2, width // size, 4 * width), BF16)] * 2,
        scratch_shapes=[
            pltpu.VMEM((width, count * length), BF16),
            pltpu.VMEM((count * length, width), BF16),
        ],
        compiler_params=pltpu.CompilerParams(vmem_limit_bytes=56 << 20),
        cost_estimate=LIGHT,
        name="weight_attn",
    )(core, *n1s, *os, *dqkvs, *dbranches)


def lane_below(shape, limit):
    return lax.broadcasted_iota(jnp.int32, shape, 1) < limit


def allowed_keys(rows, columns):
    segment_q, parent_q = rows[0:1], rows[1:2]
    segment_k, parent_k = columns[:, 0:1], columns[:, 1:2]
    return (segment_k == segment_q) | (segment_k == parent_q) | (parent_k == segment_q)


def pair_scores(h, head_size, scale, q, k, bias, allowed):
    low = lane_below(k.shape, head_size)
    mine = low if h % 2 == 0 else ~low
    raw = dot_t(jnp.where(mine, k, jnp.zeros_like(k)), q) * scale + bias
    return jnp.where(allowed, raw, NEG_BIG)


def piece_moves(me, pieces, rels, whole, arrived):
    moves = []
    for number, piece in enumerate(pieces):
        part, other = number % 2, number // 2
        half = piece.shape[1]
        for place, rel in enumerate(rels[part]):
            row = pl.multiple_of((me ^ rel ^ other) * (2 * half) + part * half, half)
            moves.append(
                pltpu.make_async_copy(
                    piece.at[place], whole.at[pl.ds(row, half)], arrived.at[len(moves)]
                )
            )
            moves[-1].start()
    return moves


def join_body(rels, me_ref, *refs):
    pieces, whole, arrived = refs[:-2], refs[-2], refs[-1]
    for move in piece_moves(me_ref[0], pieces, rels, whole, arrived):
        move.wait()


def join_call(me, pieces, rels):
    outside = pl.BlockSpec(memory_space=pl.ANY)
    count = 4 * len(rels[0])
    return pl.pallas_call(
        partial(join_body, rels),
        in_specs=[pl.BlockSpec(memory_space=pltpu.SMEM)] + [outside] * len(pieces),
        out_specs=pl.BlockSpec(memory_space=pltpu.VMEM),
        out_shape=jax.ShapeDtypeStruct((count * pieces[0].shape[1], pieces[0].shape[2]), BF16),
        scratch_shapes=[pltpu.SemaphoreType.DMA((count,))],
        cost_estimate=LIGHT,
        name="join",
    )(me, *pieces)


def forward_body(heads, experts, rels, *refs):
    if rels is None:
        weights_ref, refs = refs[0], refs[1:]
    else:
        me_ref, pieces, refs = refs[0], refs[1:5], refs[5:]
        refs, (full_ref, weights_ref, arrived, written) = refs[:-4], refs[-4:]
        moves = piece_moves(me_ref[0], pieces, rels, weights_ref, arrived)
    (
        tokens_ref,
        gain1_ref,
        bias_ref,
        rows_ref,
        columns_ref,
        gain2_ref,
        router_ref,
        targets_ref,
        x_ref,
        n1_ref,
        qkv_ref,
        lse_ref,
        o_ref,
        h1_ref,
        probs_ref,
    ) = refs
    length, width = tokens_ref.shape
    head_size = width // heads
    scale = head_size ** (-0.5)
    h0 = tokens_ref[...].astype(F32)
    n1 = (h0 * rms_scale(h0) * gain1_ref[...]).astype(BF16)
    n1_ref[...] = n1
    if rels is not None:
        for move in moves:
            move.wait()
        keep = pltpu.make_async_copy(weights_ref, full_ref, written)
        keep.start()
    for part in range(3):
        columns = slice(part * width, (part + 1) * width)
        qkv_ref[:, columns] = dot(n1, weights_ref[:, columns]).astype(BF16)
    allowed = allowed_keys(rows_ref[...], columns_ref[...])
    span = 2 * head_size
    for pair in range(heads // 2):
        at = pair * span
        q = qkv_ref[:, at : at + span]
        k = qkv_ref[:, width + at : width + at + span]
        flipped = qkv_ref[:, 2 * width + at : 2 * width + at + span].T
        parts = []
        for half in range(2):
            h = 2 * pair + half
            s = pair_scores(h, head_size, scale, q, k, bias_ref[h], allowed)
            top = jnp.max(s, axis=0, keepdims=True)
            e = jnp.exp(s - top)
            total = jnp.sum(e, axis=0, keepdims=True)
            lse_ref[h : h + 1] = top + jnp.log(total)
            p = (e * (1.0 / total)).astype(BF16)
            parts.append(dot(flipped[half * head_size : (half + 1) * head_size], p))
        o_ref[:, at : at + span] = jnp.concatenate(parts, axis=0).T.astype(BF16)
    h1 = h0 + dot(o_ref[...], weights_ref[:, 3 * width :])
    h1_ref[...] = h1
    n2 = (h1 * rms_scale(h1) * gain2_ref[...]).astype(BF16)
    logits = dot(n2, router_ref[...])
    logits = jnp.where(lane_below(logits.shape, experts), logits, NEG_BIG)
    top = jnp.max(logits, axis=-1, keepdims=True)
    e = jnp.exp(logits - top)
    probs_ref[...] = e / jnp.sum(e, axis=-1, keepdims=True)
    slots = lax.broadcasted_iota(jnp.int32, (x_ref.shape[0], length), 0)
    place = (slots == targets_ref[0:1]) | (slots == targets_ref[1:2])
    x_ref[...] = dot(place.astype(F32).astype(BF16), n2).astype(BF16)
    if rels is not None:
        keep.wait()


def forward_call(heads, experts, slot_count, weights, rels, *args):
    length, width = args[0].shape
    shapes = [
        ((slot_count, width), BF16),
        ((length, width), BF16),
        ((length, 3 * width), BF16),
        ((heads, length), F32),
        ((length, width), BF16),
        ((length, width), F32),
        ((length, 128), F32),
    ]
    inside = pl.BlockSpec(memory_space=pltpu.VMEM)
    outside = pl.BlockSpec(memory_space=pl.ANY)
    in_specs = [inside] * len(args)
    out_specs = [inside] * len(shapes)
    scratch = []
    if rels is None:
        args, in_specs = (weights,) + args, [inside] + in_specs
    else:
        me, pieces = weights
        args = (me, *pieces) + args
        in_specs = [pl.BlockSpec(memory_space=pltpu.SMEM)] + [outside] * len(pieces) + in_specs
        shapes.append(((width, 4 * width), BF16))
        out_specs.append(outside)
        scratch = [
            pltpu.VMEM((width, 4 * width), BF16),
            pltpu.SemaphoreType.DMA((4 * len(rels[0]),)),
            pltpu.SemaphoreType.DMA,
        ]
    return pl.pallas_call(
        partial(forward_body, heads, experts, rels),
        in_specs=in_specs,
        out_specs=out_specs,
        out_shape=[jax.ShapeDtypeStruct(*s) for s in shapes],
        scratch_shapes=scratch,
        compiler_params=pltpu.CompilerParams(vmem_limit_bytes=56 << 20),
        cost_estimate=LIGHT,
        name="attention_forward",
    )(*args)


def backward_body(
    heads,
    experts,
    dx_ref,
    targets_ref,
    routes_ref,
    probs_ref,
    h1_ref,
    go_ref,
    gain2_ref,
    router_ref,
    proj_ref,
    qkv_ref,
    lse_ref,
    bias_ref,
    rows_ref,
    columns_ref,
    dh1_ref,
    dbranch_ref,
    dqkv_ref,
    ds_ref,
    router_grad_ref,
    gain_grad_ref,
    do_ref,
):
    length, width = h1_ref.shape
    head_size = width // heads
    scale = head_size ** (-0.5)
    slots = lax.broadcasted_iota(jnp.int32, (length, dx_ref.shape[0]), 1)
    hot = [slots == targets_ref[:, j : j + 1] for j in range(2)]
    pick = [m.astype(F32).astype(BF16) for m in hot]
    dgate = [jnp.sum(dot(m, dx_ref[:, width:]), axis=-1, keepdims=True) for m in pick]
    probs = probs_ref[...]
    lane = lax.broadcasted_iota(jnp.int32, probs.shape, 1)
    dprobs = sum(jnp.where(lane == routes_ref[:, j : j + 1], dgate[j], 0.0) for j in range(2))
    dlogits = probs * (dprobs - jnp.sum(probs * dprobs, axis=-1, keepdims=True))
    dlogits = dlogits.astype(BF16)
    dn2 = dot(pick[0] + pick[1], dx_ref[:, :width]) + dot_t(dlogits, router_ref[...])
    h1 = h1_ref[...]
    r2 = rms_scale(h1)
    n2_hat = h1 * r2
    gain2 = gain2_ref[...]
    n2 = (n2_hat * gain2).astype(BF16)
    router_grad_ref[...] = t_dot(dlogits, n2)
    gain_grad_ref[...] = jnp.sum(dn2 * n2_hat, axis=0, keepdims=True)
    scaled = dn2 * gain2
    mean = jnp.mean(scaled * n2_hat, axis=-1, keepdims=True)
    dh1 = go_ref[...].astype(F32) + r2 * (scaled - n2_hat * mean)
    dh1_ref[...] = dh1
    dbranch = dh1.astype(BF16)
    dbranch_ref[...] = dbranch
    do_ref[...] = dot_t(dbranch, proj_ref[...]).astype(BF16)
    allowed = allowed_keys(rows_ref[...], columns_ref[...])
    span = 2 * head_size
    low = lane_below((length, span), head_size)
    for pair in range(heads // 2):
        at = pair * span
        q = qkv_ref[:, at : at + span]
        k = qkv_ref[:, width + at : width + at + span]
        v = qkv_ref[:, 2 * width + at : 2 * width + at + span]
        do = do_ref[:, at : at + span]
        flipped = k.T
        dq, dk, dv = [], [], []
        for half in range(2):
            h = 2 * pair + half
            s = pair_scores(h, head_size, scale, q, k, bias_ref[h], allowed)
            p = jnp.exp(s - lse_ref[h : h + 1])
            mine = low if half == 0 else ~low
            dp = dot_t(jnp.where(mine, v, jnp.zeros_like(v)), do)
            inner = jnp.sum(p * dp, axis=0, keepdims=True)
            ds = (p * (dp - inner)).astype(BF16)
            ds_ref[h] = ds
            dv.append(dot(p.astype(BF16), do))
            dk.append(dot(ds, q))
            dq.append(dot(flipped[half * head_size : (half + 1) * head_size], ds))
        dqkv_ref[:, at : at + span] = (jnp.concatenate(dq, axis=0).T * scale).astype(BF16)
        dqkv_ref[:, width + at : width + at + span] = (jnp.where(low, *dk) * scale).astype(BF16)
        dqkv_ref[:, 2 * width + at : 2 * width + at + span] = jnp.where(low, *dv).astype(BF16)


def backward_call(heads, experts, dx, targets, routes, probs, h1, go, gain2, router, proj, *rest):
    length, width = h1.shape
    shapes = [
        ((length, width), F32),
        ((length, width), BF16),
        ((length, 3 * width), BF16),
        ((heads, length, length), BF16),
        ((128, width), F32),
        ((1, width), F32),
    ]
    args = (dx, targets, routes, probs, h1, go, gain2, router, proj) + rest
    in_specs = [pl.BlockSpec(a.shape, lambda i, n=a.ndim: (0,) * n) for a in args]
    in_specs[8] = pl.BlockSpec((width, width), lambda i: (0, 3))
    return pl.pallas_call(
        partial(backward_body, heads, experts),
        grid=(1,),
        in_specs=in_specs,
        out_specs=[pl.BlockSpec(s, lambda i, n=len(s): (0,) * n) for s, _ in shapes],
        out_shape=[jax.ShapeDtypeStruct(*s) for s in shapes],
        scratch_shapes=[pltpu.VMEM((length, width), BF16)],
        compiler_params=pltpu.CompilerParams(vmem_limit_bytes=56 << 20),
        cost_estimate=LIGHT,
        name="attention_backward",
    )(*args)


def on_device(
    sizes,
    tokens,
    cotangent,
    segment_ids,
    parent_ids,
    routes,
    gain_attn,
    w_qkv,
    w_proj,
    rel_bias,
    gain_moe,
    w_router,
    w_in,
    w_out,
):
    dp, experts = sizes["dp"], sizes["expert"]
    batches, length, width = tokens.shape
    heads = rel_bias.shape[1]
    head_size = width // heads
    inner = w_in.shape[2] // 2
    capacity = (10 * length + 4 * experts - 1) // (4 * experts)
    slot_count = experts * capacity
    scale = head_size ** (-0.5)
    me_e = lax.axis_index("expert")

    attn_block = gather_expert(jnp.concatenate([w_qkv, w_proj], axis=1), experts)
    places = jax.vmap(partial(slot_positions, experts=experts))(routes)
    targets = routes * capacity + places
    hot = targets[..., None] == jnp.arange(slot_count, dtype=jnp.int32)
    select = hot.astype(BF16)
    both = select[:, :, 0] + select[:, :, 1]
    out_grads = [cotangent[n] for n in range(batches)]
    outgoing = [
        t_dot(both[n], out_grads[n]).astype(BF16).reshape(experts, capacity, width)
        for n in range(batches)
    ]
    go_slots = [all_to_all(after(v, attn_block)) for v in outgoing]

    positions = jnp.arange(length, dtype=jnp.int32)
    buckets = bucket_of(positions[:, None] - positions[None, :])
    bucket_hot = (buckets[:, :, None] == jnp.arange(rel_bias.shape[0], dtype=jnp.int32)).astype(F32)
    bias = jnp.einsum("kqc,ch->hkq", bucket_hot, rel_bias, precision=lax.Precision.HIGHEST)

    me_d = lax.axis_index("dp").astype(jnp.int32)[None]
    out_first = gather_first(w_out[0], dp, ())
    attn_first = gather_first(attn_block, dp, (bias, outgoing, out_first))
    pieces, rels = gather_dp(attn_first, dp, ())
    out_pieces, _ = gather_dp(out_first, dp, pieces[:2])
    wout_full = join_call(me_d, out_pieces, rels)
    win_full = lax.all_gather(
        after(w_in[0], pieces[:2], go_slots[0]), "dp", axis=0, tiled=True
    )

    router_wide = jnp.pad(w_router, ((0, 0), (0, 128 - experts)))
    gain1, gain2 = gain_attn[None], gain_moe[None]
    saved = []
    for n in range(batches):
        id_rows = jnp.stack([segment_ids[n], parent_ids[n]])
        target_columns = targets[n]
        weights = attn_w if n else (me_d, pieces)
        outs = forward_call(
            heads,
            experts,
            slot_count,
            weights,
            None if n else rels,
            after(tokens[n], wout_full) if n else tokens[n],
            gain1,
            bias,
            id_rows,
            id_rows.T,
            gain2,
            router_wide,
            target_columns.T,
        )
        if n == 0:
            *outs, attn_w = outs
        x_slots = all_to_all(after(outs[0], go_slots).reshape(experts, capacity, width))
        saved.append((id_rows,) + tuple(outs[1:]) + (x_slots,))

    mine = jnp.stack([me_e, jnp.int32(experts)]).astype(jnp.int32)
    held, grads = [], None
    for n in range(batches):
        x = saved[n][-1].reshape(slot_count, width)
        go = go_slots[n].reshape(slot_count, width)
        y, dx, *grads = expert_call(
            n, batches, experts, mine, x, go, router_wide, win_full, wout_full, grads
        )
        grads = [y] + grads
        dx_back = all_to_all(dx.reshape(experts, capacity, width + 128))
        held.append((x, dx_back.reshape(slot_count, width + 128)))

    def backward(n, dx_back):
        id_rows, _, qkv, lse, _, h1, probs, _ = saved[n]
        return backward_call(
            heads,
            experts,
            dx_back,
            targets[n],
            routes[n],
            probs,
            h1,
            out_grads[n],
            gain2,
            router_wide,
            attn_w,
            qkv,
            lse,
            bias,
            id_rows,
            id_rows.T,
        )

    core = me_d % 2
    _, gt, du, dy = grads
    joined = weight_in_call(dp, [h[0] for h in held], after(du, held[0][1]))
    backs = [backward(0, after(held[0][1], joined))]
    joined = weight_out_call(after(gt, held[1][1], backs[0]), dy, joined)
    backs.append(backward(1, after(held[1][1], joined)))
    attn_keep, attn_send = weight_attn_call(
        dp,
        core,
        [v[1] for v in saved],
        [v[4] for v in saved],
        [v[2] for v in backs],
        [v[1] for v in backs],
    )
    y_back = all_to_all(after(grads[0], attn_keep))
    attn_core = scatter_core(attn_keep, attn_send, dp)
    attn_sum = scatter_dp(attn_core, dp, ())
    space, tile = joined.shape[1:]
    summed = lax.psum_scatter(
        joined.reshape(dp * space, tile), "dp", scatter_dimension=0, tiled=True
    )
    in_total, out_total = spread_call(summed, w_in.shape[1:], w_out.shape[1:])

    outputs, input_grads = [], []
    full_qkv = attn_w[:, : 3 * width]
    router_grad = sum(v[4] for v in backs)[:experts].T
    gain_moe_grad = sum(v[5] for v in backs)[0]
    table_grad = jnp.einsum(
        "nhkq,kqc->ch",
        after(jnp.stack([v[3] for v in backs]), attn_keep),
        bucket_hot.astype(BF16),
        preferred_element_type=F32,
    )
    gain_attn_grad = 0.0
    for n in range(batches):
        _, n1, _, _, _, h1, probs, _ = saved[n]
        dh1, _, dqkv, _, _, _ = backs[n]
        y_n = after(y_back, attn_sum)[:, n].reshape(slot_count, width)
        route_hot = (routes[n][:, :, None] == jnp.arange(experts, dtype=jnp.int32)).astype(F32)
        gates = jnp.sum(probs[:, None, :experts] * route_hot, axis=-1)
        picked0, picked1 = dot(select[n][:, 0], y_n), dot(select[n][:, 1], y_n)
        moe = gates[:, :1] * picked0 + gates[:, 1:] * picked1
        outputs.append((h1 + moe).astype(BF16))
        h0 = tokens[n].astype(F32)
        r1 = rms_scale(h0)
        n1_hat = h0 * r1
        dn1 = dot_t(after(dqkv, attn_keep), full_qkv)
        gain_attn_grad = gain_attn_grad + jnp.sum(dn1 * n1_hat, axis=0)
        scaled = dn1 * gain_attn
        input_grad = dh1 + r1 * (
            scaled - n1_hat * jnp.mean(scaled * n1_hat, axis=-1, keepdims=True)
        )
        input_grads.append(input_grad.astype(BF16))

    attn_total = scatter_expert(attn_sum, experts)
    qkv_total, proj_total = attn_total[:, : 3 * width], attn_total[:, 3 * width :]
    small = jnp.concatenate(
        [gain_attn_grad, table_grad.reshape(-1), gain_moe_grad, router_grad.reshape(-1)]
    )
    small = sum_over(small.reshape(-1, 128), "dp", dp)
    small = sum_ring(after(small, attn_sum), "expert", experts).reshape(-1)
    cuts = (width, width + table_grad.size, 2 * width + table_grad.size)
    return (
        jnp.stack(outputs),
        jnp.stack(input_grads),
        small[: cuts[0]],
        qkv_total,
        proj_total,
        small[cuts[0] : cuts[1]].reshape(table_grad.shape),
        small[cuts[1] : cuts[2]],
        small[cuts[2] :].reshape(router_grad.shape),
        in_total[None],
        out_total[None],
    )


def solution(mesh):
    rows = P(None, ("dp", "expert"), None)
    in_specs = (
        rows,
        rows,
        P(None, ("dp", "expert")),
        P(None, ("dp", "expert")),
        rows,
        P(),
        P(("dp", "expert"), None),
        P(("dp", "expert"), None),
        P(),
        P(),
        P(),
        P("expert", "dp", None),
        P("expert", "dp", None),
    )
    out_specs = (
        rows,
        rows,
        P(),
        P(("dp", "expert"), None),
        P(("dp", "expert"), None),
        P(),
        P(),
        P(),
        P("expert", "dp", None),
        P("expert", "dp", None),
    )
    return jax.shard_map(
        partial(on_device, dict(mesh.shape)),
        mesh=mesh,
        in_specs=in_specs,
        out_specs=out_specs,
        check_vma=False,
    )
```

```python
from functools import partial

import jax
import jax.numpy as jnp
from jax import lax
from jax.experimental import pallas as pl
from jax.experimental.pallas import tpu as pltpu
from jax.sharding import PartitionSpec as P

EPSILON = 1e-06
NEG_BIG = -1e30
LIMITS = (12, 16, 23, 32, 46, 64, 91)
F32 = jnp.float32
BF16 = jnp.bfloat16


def bucket_of(offset):
    distance = jnp.abs(offset)
    far_part = 8 + sum(((distance >= limit).astype(jnp.int32) for limit in LIMITS))
    near_far = jnp.where(distance < 8, distance, far_part)
    return jnp.where(offset > 0, 16, 0) + near_far


def slot_positions(routes, experts):
    order = jnp.concatenate([routes[:, 0], routes[:, 1]])
    chosen = (order[:, None] == jnp.arange(experts, dtype=jnp.int32)[None, :]).astype(jnp.int32)
    before = jnp.cumsum(chosen, axis=0) - chosen
    place = jnp.sum(before * chosen, axis=1)
    return place.reshape(2, -1).T


def tree_mask(segment, parent):
    same = segment[None, :] == segment[:, None]
    upward = segment[None, :] == parent[:, None]
    downward = parent[None, :] == segment[:, None]
    return same | upward | downward


def rms_scale(values):
    return lax.rsqrt(jnp.mean(values * values, axis=-1, keepdims=True) + EPSILON)


def gelu_product(gate_part, up_part):
    return jax.nn.gelu(gate_part, approximate=True) * up_part


def after(value, *others):
    return lax.optimization_barrier((value, others))[0]


def flip(value, axis, size, bit):
    return lax.ppermute(value, axis, [(i, i ^ bit) for i in range(size)])


def shift(value, axis, size, step):
    return lax.ppermute(value, axis, [(i, (i + step) % size) for i in range(size)])


def halving_orders(size):
    bits = [1 << k for k in range(1, size.bit_length() - 1)]
    return (bits, bits[::-1])


def gather_first(block, size, hold):
    half = block.shape[0] // 2
    out = []
    for part, order in enumerate(halving_orders(size)):
        have = after(block[None, part * half : (part + 1) * half], hold)
        out.append(jnp.concatenate([have, flip(have, "dp", size, order[0])], axis=0))
    return out


def gather_dp(first, size, hold):
    near, rels = [], []
    for have, order in zip(first, halving_orders(size)):
        have = after(have, hold)
        order_rels = [0, order[0]]
        for bit in order[1:]:
            have = jnp.concatenate([have, flip(have, "dp", size, bit)], axis=0)
            order_rels = order_rels + [rel ^ bit for rel in order_rels]
        near.append(have)
        rels.append(order_rels)
    far = [flip(have, "dp", size, 1) for have in near]
    return near + far, rels


def gather_expert(block, size):
    me = lax.axis_index("expert")
    full = jnp.zeros((size,) + block.shape, block.dtype)
    for step in range(size):
        piece = shift(block, "expert", size, step) if step else block
        full = lax.dynamic_update_slice(full, piece[None], ((me - step) % size, 0, 0))
    return full.reshape(size * block.shape[0], block.shape[1])


def all_to_all(value):
    return lax.all_to_all(value, "expert", split_axis=0, concat_axis=0, tiled=True)


def split_bit(value, me, bit):
    mine = (me // bit) % 2
    kept = lax.dynamic_index_in_dim(value, mine, 0, keepdims=False)
    sent = lax.dynamic_index_in_dim(value, 1 - mine, 0, keepdims=False)
    return kept, sent


def scatter_core(keep, send, size):
    return (keep.astype(F32) + flip(send, "dp", size, 1).astype(F32)).astype(BF16)


def scatter_dp(summed, size, hold):
    me = lax.axis_index("dp")
    _, rows, width = summed.shape
    half = rows // 2
    outs = []
    for part, order in enumerate(halving_orders(size)):
        value = summed[:, part * half : (part + 1) * half]
        left = [1 << k for k in range(1, size.bit_length() - 1)]
        for bit in order:
            place = left.index(bit)
            high, low = 1 << (len(left) - 1 - place), 1 << place
            shaped = value.astype(BF16).reshape(high, 2, low, half, width)
            kept, sent = split_bit(jnp.moveaxis(shaped, 1, 0), me, bit)
            got = flip(sent, "dp", size, bit)
            value = kept.astype(F32) + after(got, hold).astype(F32)
            left.remove(bit)
        outs.append(value.reshape(half, width))
    return jnp.concatenate(outs, axis=0)


def scatter_expert(total, size):
    rows = total.shape[0] // size
    low = total.astype(BF16).reshape(size, rows, total.shape[1])
    return jnp.sum(all_to_all(low).astype(F32), axis=0)


def sum_over(value, axis, size):
    bit = 1
    while bit < size:
        value = value + flip(value, axis, size, bit)
        bit *= 2
    return value


def sum_ring(value, axis, size):
    terms = [shift(value, axis, size, step) if step else value for step in range(size)]
    while len(terms) > 1:
        half = len(terms) // 2
        terms = [terms[k] + terms[k + half] for k in range(half)]
    return terms[0]


def dot(left, right):
    return jnp.dot(left, right, preferred_element_type=F32)


def dot_t(left, right):
    return lax.dot_general(left, right, (((1,), (1,)), ((), ())), preferred_element_type=F32)


def t_dot(left, right):
    return lax.dot_general(left, right, (((0,), (0,)), ((), ())), preferred_element_type=F32)

LIGHT = pl.CostEstimate(flops=1, bytes_accessed=1, transcendentals=0)


GELU_C = 0.7978845608028654
GELU_A = 0.044715


def expert_body(
    mine, x_ref, go_ref, wr_ref, wg_ref, wu_ref, wo_ref, *refs
):
    y_ref, dx_ref, gt_ref, du_ref, dy_ref, y_acc, dx_acc = refs[-7:]
    step, last = pl.program_id(0), pl.num_programs(0) - 1

    @pl.when(step == 0)
    def _():
        logits = dot(x_ref[...], wr_ref[...])
        lane = lax.broadcasted_iota(jnp.int32, logits.shape, 1)
        logits = jnp.where(lane < mine[1], logits, NEG_BIG)
        top = jnp.max(logits, axis=-1, keepdims=True)
        weights = jnp.exp(logits - top)
        total = jnp.sum(weights, axis=-1, keepdims=True)
        gate = jnp.sum(jnp.where(lane == mine[0], weights, 0.0), axis=-1, keepdims=True) / total
        dy_ref[...] = (gate * go_ref[...].astype(F32)).astype(BF16)
        y_acc[...] = jnp.zeros_like(y_acc)
        dx_acc[...] = jnp.zeros_like(dx_acc)

    x = x_ref[...]
    wg, wu, wo = wg_ref[...], wu_ref[...], wo_ref[...]
    a, b = dot(x, wg), dot(x, wu)
    dg = dot_t(dy_ref[...], wo)
    square = a * a
    t = jnp.tanh(GELU_C * (a + GELU_A * (a * square)))
    half = 0.5 + 0.5 * t
    act = a * half
    slope = half + (0.5 * GELU_C) * a * (1.0 - t * t) * (1.0 + (3.0 * GELU_A) * square)
    g = (act * b).astype(BF16)
    da = (dg * b * slope).astype(BF16)
    db = (dg * act).astype(BF16)
    gt_ref[...] = g.T
    du_ref[0] = da
    du_ref[1] = db
    y_acc[...] += dot(g, wo)
    dx_acc[...] += dot_t(jnp.concatenate([da, db], axis=1), jnp.concatenate([wg, wu], axis=1))

    @pl.when(step == last)
    def _():
        y = y_acc[...].astype(BF16)
        y_ref[:, 0] = y.reshape(-1, *y_ref.shape[2:])
        width = y.shape[1]
        dx_ref[:, :width] = dx_acc[...].astype(BF16)
        product = go_ref[...].astype(F32) * y.astype(F32)
        rest = jnp.sum(product, axis=-1, keepdims=True)
        lane = lax.broadcasted_iota(jnp.int32, (y.shape[0], 128), 1)
        terms = jnp.zeros(lane.shape, F32)
        for place in range(3):
            term = rest.astype(BF16).astype(F32)
            terms = jnp.where(lane == place, term, terms)
            rest = rest - term
        dx_ref[:, width:] = terms.astype(BF16)


def tile_of(size, most):
    return max(t for t in range(128, most + 1, 128) if size % t == 0)


def expert_call(batch, batches, experts, mine, x, go, w_router, w_in, w_out, held):
    rows, width = x.shape
    inner = w_out.shape[0]
    tile = tile_of(inner, 256)
    tiles = inner // tile
    whole = lambda shape: pl.BlockSpec(shape, lambda j: (0,) * len(shape))
    in_specs = [
        pl.BlockSpec(memory_space=pltpu.SMEM),
        whole((rows, width)),
        whole((rows, width)),
        whole(w_router.shape),
        pl.BlockSpec((width, tile), lambda j: (0, j)),
        pl.BlockSpec((width, tile), lambda j: (0, tiles + j)),
        pl.BlockSpec((tile, width), lambda j: (j, 0)),
    ]
    args = [mine, x, go, w_router, w_in, w_in, w_out]
    aliases = {}
    if held is not None:
        in_specs += [pl.BlockSpec(memory_space=pl.ANY)] * 4
        aliases = {len(args): 0, len(args) + 1: 2, len(args) + 2: 3, len(args) + 3: 4}
        args += list(held)
    flops = 12 * rows * width * inner
    return pl.pallas_call(
        expert_body,
        grid=(tiles,),
        in_specs=in_specs,
        out_specs=[
            pl.BlockSpec((experts, 1, rows // experts, width), lambda j: (0, batch, 0, 0)),
            whole((rows, width + 128)),
            pl.BlockSpec((tile, rows), lambda j: (j, batch)),
            pl.BlockSpec((2, rows, tile), lambda j: (0, batch, j)),
            pl.BlockSpec((rows, width), lambda j: (batch, 0)),
        ],
        out_shape=[
            jax.ShapeDtypeStruct((experts, batches, rows // experts, width), BF16),
            jax.ShapeDtypeStruct((rows, width + 128), BF16),
            jax.ShapeDtypeStruct((inner, batches * rows), BF16),
            jax.ShapeDtypeStruct((2, batches * rows, inner), BF16),
            jax.ShapeDtypeStruct((batches * rows, width), BF16),
        ],
        scratch_shapes=[pltpu.VMEM((rows, width), F32), pltpu.VMEM((rows, width), F32)],
        input_output_aliases=aliases,
        compiler_params=pltpu.CompilerParams(vmem_limit_bytes=56 << 20),
        cost_estimate=LIGHT,
        name="expert",
    )(*args)


def keep_and_send(value, core, keep_ref, send_ref, place):
    value = value.reshape((-1, 2) + value.shape[1:])
    even, odd = value[:, 0], value[:, 1]
    keep_ref[place] = jnp.where(core == 0, even, odd)
    send_ref[place] = jnp.where(core == 0, odd, even)


def weight_in_body(*refs):
    xs, du_ref, out_ref, flipped = refs[:-3], refs[-3], refs[-2], refs[-1]
    rows = xs[0].shape[0]

    @pl.when(pl.program_id(0) == 0)
    def _():
        for n, x_ref in enumerate(xs):
            flipped[:, n * rows : (n + 1) * rows] = x_ref[...].T

    tile = out_ref.shape[2]
    part = flipped.shape[0] // out_ref.shape[0]
    for place in range(out_ref.shape[1] // part):
        value = dot(flipped[...], du_ref[0, :, place * tile : (place + 1) * tile]).astype(BF16)
        out_ref[:, place * part : (place + 1) * part] = value.reshape(-1, part, tile)


def weight_in_call(size, xs, du):
    rows, width = xs[0].shape
    _, total, inner = du.shape
    tile = tile_of(inner, 256)
    tiles = inner // tile
    part = width // size
    space = 2 * tiles * part + (inner // size) * (width // tile)
    return pl.pallas_call(
        weight_in_body,
        grid=(2,),
        in_specs=[pl.BlockSpec((rows, width), lambda j: (0, 0)) for _ in xs]
        + [pl.BlockSpec((1, total, inner), lambda j: (j, 0, 0))],
        out_specs=pl.BlockSpec((size, tiles * part, tile), lambda j: (0, j, 0)),
        out_shape=jax.ShapeDtypeStruct((size, space, tile), BF16),
        scratch_shapes=[pltpu.VMEM((width, total), BF16)],
        compiler_params=pltpu.CompilerParams(vmem_limit_bytes=56 << 20),
        cost_estimate=LIGHT,
        name="weight_in",
    )(*xs, du)


def weight_out_body(gt_ref, dy_ref, _, out_ref):
    out_ref[...] = dot(gt_ref[...], dy_ref[...]).astype(BF16).reshape(out_ref.shape)


def weight_out_call(gt, dy, joined):
    inner, total = gt.shape
    width = dy.shape[1]
    size, space, tile = joined.shape
    part = inner // size
    first = (space - part * (width // tile)) // part
    assert first * part + part * (width // tile) == space
    return pl.pallas_call(
        weight_out_body,
        grid=(width // tile,),
        in_specs=[
            pl.BlockSpec((inner, total), lambda j: (0, 0)),
            pl.BlockSpec((total, tile), lambda j: (0, j)),
            pl.BlockSpec(memory_space=pl.ANY),
        ],
        out_specs=pl.BlockSpec((size, part, tile), lambda j: (0, first + j, 0)),
        out_shape=jax.ShapeDtypeStruct(joined.shape, BF16),
        input_output_aliases={2: 0},
        compiler_params=pltpu.CompilerParams(vmem_limit_bytes=56 << 20),
        cost_estimate=LIGHT,
        name="weight_out",
    )(gt, dy, joined)


def spread_body(count, summed_ref, in_ref, out_ref):
    part, tile = in_ref.shape[0], summed_ref.shape[1]
    for place in range(count):
        piece = summed_ref[place * part : (place + 1) * part]
        in_ref[:, place * tile : (place + 1) * tile] = piece.astype(F32)
    base, part = count * part, out_ref.shape[0]
    for place in range(out_ref.shape[1] // tile):
        piece = summed_ref[base + place * part : base + (place + 1) * part]
        out_ref[:, place * tile : (place + 1) * tile] = piece.astype(F32)


def spread_call(summed, in_shape, out_shape):
    return pl.pallas_call(
        partial(spread_body, in_shape[1] // summed.shape[1]),
        out_shape=[jax.ShapeDtypeStruct(shape, F32) for shape in (in_shape, out_shape)],
        compiler_params=pltpu.CompilerParams(vmem_limit_bytes=56 << 20),
        cost_estimate=LIGHT,
        name="spread",
    )(summed)


def weight_attn_body(count, core_ref, *refs):
    n1s, os, dqkvs, dbranches = (refs[k * count : (k + 1) * count] for k in range(4))
    keep_ref, send_ref, flipped, right = refs[4 * count :]
    step, last = pl.program_id(0), pl.num_programs(0) - 1
    length = n1s[0].shape[0]
    blocks = 2 * keep_ref.shape[0]

    def fill(lefts, rights):
        for n in range(count):
            if lefts is not None:
                flipped[:, n * length : (n + 1) * length] = lefts[n][...].T
            right[n * length : (n + 1) * length] = rights[n][...]

    @pl.when(step == 0)
    def _():
        fill(n1s, dqkvs)

    @pl.when((step > 0) & (step < last))
    def _():
        fill(None, dqkvs)

    @pl.when(step == last)
    def _():
        fill(os, dbranches)

    value = dot(flipped[...], right[...]).astype(BF16)
    value = value.reshape(blocks, -1, value.shape[1])
    keep_and_send(value, core_ref[0], keep_ref, send_ref, slice(None))


def weight_attn_call(size, core, n1s, os, dqkvs, dbranches):
    count = len(n1s)
    length, width = n1s[0].shape
    whole = pl.BlockSpec((length, width), lambda j: (0, 0))
    half = pl.BlockSpec((size // 2, width // size, width), lambda j: (0, 0, j))
    return pl.pallas_call(
        partial(weight_attn_body, count),
        grid=(4,),
        in_specs=[pl.BlockSpec(memory_space=pltpu.SMEM)]
        + [whole] * (2 * count)
        + [pl.BlockSpec((length, width), lambda j: (0, jnp.minimum(j, 2)))] * count
        + [whole] * count,
        out_specs=[half, half],
        out_shape=[jax.ShapeDtypeStruct((size // 2, width // size, 4 * width), BF16)] * 2,
        scratch_shapes=[
            pltpu.VMEM((width, count * length), BF16),
            pltpu.VMEM((count * length, width), BF16),
        ],
        compiler_params=pltpu.CompilerParams(vmem_limit_bytes=56 << 20),
        cost_estimate=LIGHT,
        name="weight_attn",
    )(core, *n1s, *os, *dqkvs, *dbranches)


def lane_below(shape, limit):
    return lax.broadcasted_iota(jnp.int32, shape, 1) < limit


def allowed_keys(rows, columns):
    segment_q, parent_q = rows[0:1], rows[1:2]
    segment_k, parent_k = columns[:, 0:1], columns[:, 1:2]
    return (segment_k == segment_q) | (segment_k == parent_q) | (parent_k == segment_q)


def pair_scores(h, head_size, scale, q, k, bias, allowed):
    low = lane_below(k.shape, head_size)
    mine = low if h % 2 == 0 else ~low
    raw = dot_t(jnp.where(mine, k, jnp.zeros_like(k)), q) * scale + bias
    return jnp.where(allowed, raw, NEG_BIG)


def piece_moves(me, pieces, rels, whole, arrived):
    moves = []
    for number, piece in enumerate(pieces):
        part, other = number % 2, number // 2
        half = piece.shape[1]
        for place, rel in enumerate(rels[part]):
            row = pl.multiple_of((me ^ rel ^ other) * (2 * half) + part * half, half)
            moves.append(
                pltpu.make_async_copy(
                    piece.at[place], whole.at[pl.ds(row, half)], arrived.at[len(moves)]
                )
            )
            moves[-1].start()
    return moves


def join_body(rels, me_ref, *refs):
    pieces, whole, arrived = refs[:-2], refs[-2], refs[-1]
    for move in piece_moves(me_ref[0], pieces, rels, whole, arrived):
        move.wait()


def join_call(me, pieces, rels):
    outside = pl.BlockSpec(memory_space=pl.ANY)
    count = 4 * len(rels[0])
    return pl.pallas_call(
        partial(join_body, rels),
        in_specs=[pl.BlockSpec(memory_space=pltpu.SMEM)] + [outside] * len(pieces),
        out_specs=pl.BlockSpec(memory_space=pltpu.VMEM),
        out_shape=jax.ShapeDtypeStruct((count * pieces[0].shape[1], pieces[0].shape[2]), BF16),
        scratch_shapes=[pltpu.SemaphoreType.DMA((count,))],
        cost_estimate=LIGHT,
        name="join",
    )(me, *pieces)


def forward_body(heads, experts, rels, *refs):
    if rels is None:
        weights_ref, refs = refs[0], refs[1:]
    else:
        me_ref, pieces, refs = refs[0], refs[1:5], refs[5:]
        refs, (full_ref, weights_ref, arrived, written) = refs[:-4], refs[-4:]
        moves = piece_moves(me_ref[0], pieces, rels, weights_ref, arrived)
    (
        tokens_ref,
        gain1_ref,
        bias_ref,
        rows_ref,
        columns_ref,
        gain2_ref,
        router_ref,
        targets_ref,
        x_ref,
        n1_ref,
        qkv_ref,
        lse_ref,
        o_ref,
        h1_ref,
        probs_ref,
    ) = refs
    length, width = tokens_ref.shape
    head_size = width // heads
    scale = head_size ** (-0.5)
    h0 = tokens_ref[...].astype(F32)
    n1 = (h0 * rms_scale(h0) * gain1_ref[...]).astype(BF16)
    n1_ref[...] = n1
    if rels is not None:
        for move in moves:
            move.wait()
        keep = pltpu.make_async_copy(weights_ref, full_ref, written)
        keep.start()
    for part in range(3):
        columns = slice(part * width, (part + 1) * width)
        qkv_ref[:, columns] = dot(n1, weights_ref[:, columns]).astype(BF16)
    allowed = allowed_keys(rows_ref[...], columns_ref[...])
    span = 2 * head_size
    for pair in range(heads // 2):
        at = pair * span
        q = qkv_ref[:, at : at + span]
        k = qkv_ref[:, width + at : width + at + span]
        flipped = qkv_ref[:, 2 * width + at : 2 * width + at + span].T
        parts = []
        for half in range(2):
            h = 2 * pair + half
            s = pair_scores(h, head_size, scale, q, k, bias_ref[h], allowed)
            top = jnp.max(s, axis=0, keepdims=True)
            e = jnp.exp(s - top)
            total = jnp.sum(e, axis=0, keepdims=True)
            lse_ref[h : h + 1] = top + jnp.log(total)
            p = (e * (1.0 / total)).astype(BF16)
            parts.append(dot(flipped[half * head_size : (half + 1) * head_size], p))
        o_ref[:, at : at + span] = jnp.concatenate(parts, axis=0).T.astype(BF16)
    h1 = h0 + dot(o_ref[...], weights_ref[:, 3 * width :])
    h1_ref[...] = h1
    n2 = (h1 * rms_scale(h1) * gain2_ref[...]).astype(BF16)
    logits = dot(n2, router_ref[...])
    logits = jnp.where(lane_below(logits.shape, experts), logits, NEG_BIG)
    top = jnp.max(logits, axis=-1, keepdims=True)
    e = jnp.exp(logits - top)
    probs_ref[...] = e / jnp.sum(e, axis=-1, keepdims=True)
    slots = lax.broadcasted_iota(jnp.int32, (x_ref.shape[0], length), 0)
    place = (slots == targets_ref[0:1]) | (slots == targets_ref[1:2])
    x_ref[...] = dot(place.astype(F32).astype(BF16), n2).astype(BF16)
    if rels is not None:
        keep.wait()


def forward_call(heads, experts, slot_count, weights, rels, *args):
    length, width = args[0].shape
    shapes = [
        ((slot_count, width), BF16),
        ((length, width), BF16),
        ((length, 3 * width), BF16),
        ((heads, length), F32),
        ((length, width), BF16),
        ((length, width), F32),
        ((length, 128), F32),
    ]
    inside = pl.BlockSpec(memory_space=pltpu.VMEM)
    outside = pl.BlockSpec(memory_space=pl.ANY)
    in_specs = [inside] * len(args)
    out_specs = [inside] * len(shapes)
    scratch = []
    if rels is None:
        args, in_specs = (weights,) + args, [inside] + in_specs
    else:
        me, pieces = weights
        args = (me, *pieces) + args
        in_specs = [pl.BlockSpec(memory_space=pltpu.SMEM)] + [outside] * len(pieces) + in_specs
        shapes.append(((width, 4 * width), BF16))
        out_specs.append(outside)
        scratch = [
            pltpu.VMEM((width, 4 * width), BF16),
            pltpu.SemaphoreType.DMA((4 * len(rels[0]),)),
            pltpu.SemaphoreType.DMA,
        ]
    return pl.pallas_call(
        partial(forward_body, heads, experts, rels),
        in_specs=in_specs,
        out_specs=out_specs,
        out_shape=[jax.ShapeDtypeStruct(*s) for s in shapes],
        scratch_shapes=scratch,
        compiler_params=pltpu.CompilerParams(vmem_limit_bytes=56 << 20),
        cost_estimate=LIGHT,
        name="attention_forward",
    )(*args)


def backward_body(
    heads,
    experts,
    dx_ref,
    targets_ref,
    routes_ref,
    probs_ref,
    h1_ref,
    go_ref,
    gain2_ref,
    router_ref,
    proj_ref,
    qkv_ref,
    lse_ref,
    bias_ref,
    rows_ref,
    columns_ref,
    dh1_ref,
    dbranch_ref,
    dqkv_ref,
    ds_ref,
    router_grad_ref,
    gain_grad_ref,
    do_ref,
):
    length, width = h1_ref.shape
    head_size = width // heads
    scale = head_size ** (-0.5)
    slots = lax.broadcasted_iota(jnp.int32, (length, dx_ref.shape[0]), 1)
    hot = [slots == targets_ref[:, j : j + 1] for j in range(2)]
    pick = [m.astype(F32).astype(BF16) for m in hot]
    dgate = [jnp.sum(dot(m, dx_ref[:, width:]), axis=-1, keepdims=True) for m in pick]
    probs = probs_ref[...]
    lane = lax.broadcasted_iota(jnp.int32, probs.shape, 1)
    dprobs = sum(jnp.where(lane == routes_ref[:, j : j + 1], dgate[j], 0.0) for j in range(2))
    dlogits = probs * (dprobs - jnp.sum(probs * dprobs, axis=-1, keepdims=True))
    dlogits = dlogits.astype(BF16)
    dn2 = dot(pick[0] + pick[1], dx_ref[:, :width]) + dot_t(dlogits, router_ref[...])
    h1 = h1_ref[...]
    r2 = rms_scale(h1)
    n2_hat = h1 * r2
    gain2 = gain2_ref[...]
    n2 = (n2_hat * gain2).astype(BF16)
    router_grad_ref[...] = t_dot(dlogits, n2)
    gain_grad_ref[...] = jnp.sum(dn2 * n2_hat, axis=0, keepdims=True)
    scaled = dn2 * gain2
    mean = jnp.mean(scaled * n2_hat, axis=-1, keepdims=True)
    dh1 = go_ref[...].astype(F32) + r2 * (scaled - n2_hat * mean)
    dh1_ref[...] = dh1
    dbranch = dh1.astype(BF16)
    dbranch_ref[...] = dbranch
    do_ref[...] = dot_t(dbranch, proj_ref[...]).astype(BF16)
    allowed = allowed_keys(rows_ref[...], columns_ref[...])
    span = 2 * head_size
    low = lane_below((length, span), head_size)
    for pair in range(heads // 2):
        at = pair * span
        q = qkv_ref[:, at : at + span]
        k = qkv_ref[:, width + at : width + at + span]
        v = qkv_ref[:, 2 * width + at : 2 * width + at + span]
        do = do_ref[:, at : at + span]
        flipped = k.T
        dq, dk, dv = [], [], []
        for half in range(2):
            h = 2 * pair + half
            s = pair_scores(h, head_size, scale, q, k, bias_ref[h], allowed)
            p = jnp.exp(s - lse_ref[h : h + 1])
            mine = low if half == 0 else ~low
            dp = dot_t(jnp.where(mine, v, jnp.zeros_like(v)), do)
            inner = jnp.sum(p * dp, axis=0, keepdims=True)
            ds = (p * (dp - inner)).astype(BF16)
            ds_ref[h] = ds
            dv.append(dot(p.astype(BF16), do))
            dk.append(dot(ds, q))
            dq.append(dot(flipped[half * head_size : (half + 1) * head_size], ds))
        dqkv_ref[:, at : at + span] = (jnp.concatenate(dq, axis=0).T * scale).astype(BF16)
        dqkv_ref[:, width + at : width + at + span] = (jnp.where(low, *dk) * scale).astype(BF16)
        dqkv_ref[:, 2 * width + at : 2 * width + at + span] = jnp.where(low, *dv).astype(BF16)


def backward_call(heads, experts, dx, targets, routes, probs, h1, go, gain2, router, proj, *rest):
    length, width = h1.shape
    shapes = [
        ((length, width), F32),
        ((length, width), BF16),
        ((length, 3 * width), BF16),
        ((heads, length, length), BF16),
        ((128, width), F32),
        ((1, width), F32),
    ]
    args = (dx, targets, routes, probs, h1, go, gain2, router, proj) + rest
    in_specs = [pl.BlockSpec(a.shape, lambda i, n=a.ndim: (0,) * n) for a in args]
    in_specs[8] = pl.BlockSpec((width, width), lambda i: (0, 3))
    return pl.pallas_call(
        partial(backward_body, heads, experts),
        grid=(1,),
        in_specs=in_specs,
        out_specs=[pl.BlockSpec(s, lambda i, n=len(s): (0,) * n) for s, _ in shapes],
        out_shape=[jax.ShapeDtypeStruct(*s) for s in shapes],
        scratch_shapes=[pltpu.VMEM((length, width), BF16)],
        compiler_params=pltpu.CompilerParams(vmem_limit_bytes=56 << 20),
        cost_estimate=LIGHT,
        name="attention_backward",
    )(*args)


def finish_body(count, tokens_ref, gain_ref, weights_ref, *refs):
    dqkvs, dh1s = refs[:count], refs[count : 2 * count]
    out_ref, gain_grad_ref = refs[2 * count :]
    gain = gain_ref[...]
    total = jnp.zeros(gain.shape, F32)
    for n in range(count):
        h0 = tokens_ref[n].astype(F32)
        r1 = rms_scale(h0)
        n1_hat = h0 * r1
        dn1 = dot_t(dqkvs[n][...], weights_ref[...])
        total = total + jnp.sum(dn1 * n1_hat, axis=0, keepdims=True)
        scaled = dn1 * gain
        mean = jnp.mean(scaled * n1_hat, axis=-1, keepdims=True)
        out_ref[n] = (dh1s[n][...] + r1 * (scaled - n1_hat * mean)).astype(BF16)
    gain_grad_ref[...] = total


def finish_call(tokens, gain, weights, dqkvs, dh1s):
    args = (tokens, gain, weights, *dqkvs, *dh1s)
    in_specs = [pl.BlockSpec(a.shape, lambda i, n=a.ndim: (0,) * n) for a in args]
    in_specs[2] = pl.BlockSpec((tokens.shape[2], 3 * tokens.shape[2]), lambda i: (0, 0))
    return pl.pallas_call(
        partial(finish_body, len(dqkvs)),
        grid=(1,),
        in_specs=in_specs,
        out_specs=[
            pl.BlockSpec(tokens.shape, lambda i: (0, 0, 0)),
            pl.BlockSpec(gain.shape, lambda i: (0, 0)),
        ],
        out_shape=[
            jax.ShapeDtypeStruct(tokens.shape, BF16),
            jax.ShapeDtypeStruct(gain.shape, F32),
        ],
        compiler_params=pltpu.CompilerParams(vmem_limit_bytes=56 << 20),
        cost_estimate=LIGHT,
        name="finish",
    )(*args)


def output_body(count, y_ref, targets_ref, routes_ref, *refs):
    probs, h1s, out_ref = refs[:count], refs[count : 2 * count], refs[-1]
    width = out_ref.shape[2]
    for n in range(count):
        y = y_ref[:, n].reshape(-1, width)
        slots = lax.broadcasted_iota(jnp.int32, (out_ref.shape[1], y.shape[0]), 1)
        total = h1s[n][...]
        moe = 0.0
        for j in range(2):
            weights = probs[n][...]
            lane = lax.broadcasted_iota(jnp.int32, weights.shape, 1)
            mine = lane == routes_ref[n, :, j : j + 1]
            gate = jnp.sum(jnp.where(mine, weights, 0.0), axis=-1, keepdims=True)
            pick = (slots == targets_ref[n, :, j : j + 1]).astype(F32).astype(BF16)
            moe = moe + gate * dot(pick, y)
        out_ref[n] = (total + moe).astype(BF16)


def output_call(y, targets, routes, probs, h1s):
    length, width = h1s[0].shape
    return pl.pallas_call(
        partial(output_body, len(h1s)),
        out_shape=jax.ShapeDtypeStruct((len(h1s), length, width), BF16),
        compiler_params=pltpu.CompilerParams(vmem_limit_bytes=56 << 20),
        cost_estimate=LIGHT,
        name="output",
    )(y, targets, routes, *probs, *h1s)


def on_device(
    sizes,
    tokens,
    cotangent,
    segment_ids,
    parent_ids,
    routes,
    gain_attn,
    w_qkv,
    w_proj,
    rel_bias,
    gain_moe,
    w_router,
    w_in,
    w_out,
):
    dp, experts = sizes["dp"], sizes["expert"]
    batches, length, width = tokens.shape
    heads = rel_bias.shape[1]
    head_size = width // heads
    inner = w_in.shape[2] // 2
    capacity = (10 * length + 4 * experts - 1) // (4 * experts)
    slot_count = experts * capacity
    scale = head_size ** (-0.5)
    me_e = lax.axis_index("expert")

    attn_block = gather_expert(jnp.concatenate([w_qkv, w_proj], axis=1), experts)
    places = jax.vmap(partial(slot_positions, experts=experts))(routes)
    targets = routes * capacity + places
    hot = targets[..., None] == jnp.arange(slot_count, dtype=jnp.int32)
    select = hot.astype(BF16)
    both = select[:, :, 0] + select[:, :, 1]
    out_grads = [cotangent[n] for n in range(batches)]
    outgoing = [
        t_dot(both[n], out_grads[n]).astype(BF16).reshape(experts, capacity, width)
        for n in range(batches)
    ]
    go_joint = all_to_all(after(jnp.stack(outgoing, axis=1), attn_block))
    go_slots = [go_joint[:, n] for n in range(batches)]

    positions = jnp.arange(length, dtype=jnp.int32)
    buckets = bucket_of(positions[:, None] - positions[None, :])
    bucket_hot = (buckets[:, :, None] == jnp.arange(rel_bias.shape[0], dtype=jnp.int32)).astype(F32)
    bias = jnp.einsum("kqc,ch->hkq", bucket_hot, rel_bias, precision=lax.Precision.HIGHEST)

    me_d = lax.axis_index("dp").astype(jnp.int32)[None]
    attn_first = gather_first(attn_block, dp, outgoing)
    pieces, rels = gather_dp(attn_first, dp, bias)
    wout_full = lax.all_gather(w_out[0], "dp", axis=0, tiled=True)
    win_full = lax.all_gather(
        after(w_in[0], pieces[:2], go_slots[0]), "dp", axis=0, tiled=True
    )

    router_wide = jnp.pad(w_router, ((0, 0), (0, 128 - experts)))
    gain1, gain2 = gain_attn[None], gain_moe[None]
    saved = []
    for n in range(batches):
        id_rows = jnp.stack([segment_ids[n], parent_ids[n]])
        target_columns = targets[n]
        weights = attn_w if n else (me_d, pieces)
        outs = forward_call(
            heads,
            experts,
            slot_count,
            weights,
            None if n else rels,
            tokens[n],
            gain1,
            bias,
            id_rows,
            id_rows.T,
            gain2,
            router_wide,
            target_columns.T,
        )
        if n == 0:
            *outs, attn_w = outs
        x_slots = all_to_all(after(outs[0], go_slots).reshape(experts, capacity, width))
        saved.append((id_rows,) + tuple(outs[1:]) + (x_slots,))

    mine = jnp.stack([me_e, jnp.int32(experts)]).astype(jnp.int32)
    held, grads = [], None
    for n in range(batches):
        x = saved[n][-1].reshape(slot_count, width)
        go = go_slots[n].reshape(slot_count, width)
        y, dx, *grads = expert_call(
            n, batches, experts, mine, x, go, router_wide, win_full, wout_full, grads
        )
        grads = [y] + grads
        dx_back = all_to_all(dx.reshape(experts, capacity, width + 128))
        held.append((x, dx_back.reshape(slot_count, width + 128)))

    def backward(n, dx_back):
        id_rows, _, qkv, lse, _, h1, probs, _ = saved[n]
        return backward_call(
            heads,
            experts,
            dx_back,
            targets[n],
            routes[n],
            probs,
            h1,
            out_grads[n],
            gain2,
            router_wide,
            attn_w,
            qkv,
            lse,
            bias,
            id_rows,
            id_rows.T,
        )

    core = me_d % 2
    _, gt, du, dy = grads
    joined = weight_in_call(dp, [h[0] for h in held], after(du, held[0][1]))
    backs = [backward(0, after(held[0][1], joined))]
    joined = weight_out_call(after(gt, held[1][1], backs[0]), dy, joined)
    backs.append(backward(1, after(held[1][1], joined)))
    attn_keep, attn_send = weight_attn_call(
        dp,
        core,
        [v[1] for v in saved],
        [v[4] for v in saved],
        [v[2] for v in backs],
        [v[1] for v in backs],
    )
    y_back = all_to_all(after(grads[0], attn_keep))
    attn_core = scatter_core(attn_keep, attn_send, dp)
    space, tile = joined.shape[1:]
    summed = lax.psum_scatter(
        joined.reshape(dp * space, tile), "dp", scatter_dimension=0, tiled=True
    )
    in_total, out_total = spread_call(summed, w_in.shape[1:], w_out.shape[1:])

    router_grad = sum(v[4] for v in backs)[:experts].T
    gain_moe_grad = sum(v[5] for v in backs)[0]
    table_grad = jnp.einsum(
        "nhkq,kqc->ch",
        after(jnp.stack([v[3] for v in backs]), attn_core),
        bucket_hot.astype(BF16),
        preferred_element_type=F32,
    )
    input_grads, gain_attn_grad = finish_call(
        tokens, gain1, attn_w, [after(v[2], attn_core) for v in backs], [v[0] for v in backs]
    )
    small = jnp.concatenate(
        [gain_attn_grad[0], table_grad.reshape(-1), gain_moe_grad, router_grad.reshape(-1)]
    )
    small = sum_over(small.reshape(-1, 128), "dp", dp)
    attn_sum = scatter_dp(attn_core, dp, (input_grads, table_grad))
    small = sum_ring(after(small, attn_sum), "expert", experts).reshape(-1)
    attn_total = scatter_expert(attn_sum, experts)
    qkv_total, proj_total = attn_total[:, : 3 * width], attn_total[:, 3 * width :]
    outputs = output_call(
        after(y_back, attn_sum), targets, routes, [v[6] for v in saved], [v[5] for v in saved]
    )
    cuts = (width, width + table_grad.size, 2 * width + table_grad.size)
    return (
        outputs,
        input_grads,
        small[: cuts[0]],
        qkv_total,
        proj_total,
        small[cuts[0] : cuts[1]].reshape(table_grad.shape),
        small[cuts[1] : cuts[2]],
        small[cuts[2] :].reshape(router_grad.shape),
        in_total[None],
        out_total[None],
    )


def solution(mesh):
    rows = P(None, ("dp", "expert"), None)
    in_specs = (
        rows,
        rows,
        P(None, ("dp", "expert")),
        P(None, ("dp", "expert")),
        rows,
        P(),
        P(("dp", "expert"), None),
        P(("dp", "expert"), None),
        P(),
        P(),
        P(),
        P("expert", "dp", None),
        P("expert", "dp", None),
    )
    out_specs = (
        rows,
        rows,
        P(),
        P(("dp", "expert"), None),
        P(("dp", "expert"), None),
        P(),
        P(),
        P(),
        P("expert", "dp", None),
        P("expert", "dp", None),
    )
    return jax.shard_map(
        partial(on_device, dict(mesh.shape)),
        mesh=mesh,
        in_specs=in_specs,
        out_specs=out_specs,
        check_vma=False,
    )
```

```python
from functools import partial

import jax
import jax.numpy as jnp
from jax import lax
from jax.experimental import pallas as pl
from jax.experimental.pallas import tpu as pltpu
from jax.sharding import PartitionSpec as P

EPSILON = 1e-06
NEG_BIG = -1e30
LIMITS = (12, 16, 23, 32, 46, 64, 91)
F32 = jnp.float32
BF16 = jnp.bfloat16


def bucket_of(offset):
    distance = jnp.abs(offset)
    far_part = 8 + sum(((distance >= limit).astype(jnp.int32) for limit in LIMITS))
    near_far = jnp.where(distance < 8, distance, far_part)
    return jnp.where(offset > 0, 16, 0) + near_far


def slot_positions(routes, experts):
    order = jnp.concatenate([routes[:, 0], routes[:, 1]])
    chosen = (order[:, None] == jnp.arange(experts, dtype=jnp.int32)[None, :]).astype(jnp.int32)
    before = jnp.cumsum(chosen, axis=0) - chosen
    place = jnp.sum(before * chosen, axis=1)
    return place.reshape(2, -1).T


def tree_mask(segment, parent):
    same = segment[None, :] == segment[:, None]
    upward = segment[None, :] == parent[:, None]
    downward = parent[None, :] == segment[:, None]
    return same | upward | downward


def rms_scale(values):
    return lax.rsqrt(jnp.mean(values * values, axis=-1, keepdims=True) + EPSILON)


def gelu_product(gate_part, up_part):
    return jax.nn.gelu(gate_part, approximate=True) * up_part


def after(value, *others):
    return lax.optimization_barrier((value, others))[0]


def flip(value, axis, size, bit):
    return lax.ppermute(value, axis, [(i, i ^ bit) for i in range(size)])


def shift(value, axis, size, step):
    return lax.ppermute(value, axis, [(i, (i + step) % size) for i in range(size)])


def halving_orders(size):
    bits = [1 << k for k in range(1, size.bit_length() - 1)]
    return (bits, bits[::-1])


def gather_first(block, size, hold):
    half = block.shape[0] // 2
    out = []
    for part, order in enumerate(halving_orders(size)):
        have = after(block[None, part * half : (part + 1) * half], hold)
        out.append(jnp.concatenate([have, flip(have, "dp", size, order[0])], axis=0))
    return out


def gather_dp(first, size, hold):
    near, rels = [], []
    for have, order in zip(first, halving_orders(size)):
        have = after(have, hold)
        order_rels = [0, order[0]]
        for bit in order[1:]:
            have = jnp.concatenate([have, flip(have, "dp", size, bit)], axis=0)
            order_rels = order_rels + [rel ^ bit for rel in order_rels]
        near.append(have)
        rels.append(order_rels)
    far = [flip(have, "dp", size, 1) for have in near]
    return near + far, rels


def gather_expert(block, size):
    me = lax.axis_index("expert")
    full = jnp.zeros((size,) + block.shape, block.dtype)
    for step in range(size):
        piece = shift(block, "expert", size, step) if step else block
        full = lax.dynamic_update_slice(full, piece[None], ((me - step) % size, 0, 0))
    return full.reshape(size * block.shape[0], block.shape[1])


def all_to_all(value):
    return lax.all_to_all(value, "expert", split_axis=0, concat_axis=0, tiled=True)


def split_bit(value, me, bit):
    mine = (me // bit) % 2
    kept = lax.dynamic_index_in_dim(value, mine, 0, keepdims=False)
    sent = lax.dynamic_index_in_dim(value, 1 - mine, 0, keepdims=False)
    return kept, sent


def scatter_core(keep, send, size):
    return (keep.astype(F32) + flip(send, "dp", size, 1).astype(F32)).astype(BF16)


def scatter_dp(summed, size, hold):
    me = lax.axis_index("dp")
    _, rows, width = summed.shape
    half = rows // 2
    outs = []
    for part, order in enumerate(halving_orders(size)):
        value = summed[:, part * half : (part + 1) * half]
        left = [1 << k for k in range(1, size.bit_length() - 1)]
        for bit in order:
            place = left.index(bit)
            high, low = 1 << (len(left) - 1 - place), 1 << place
            shaped = value.astype(BF16).reshape(high, 2, low, half, width)
            kept, sent = split_bit(jnp.moveaxis(shaped, 1, 0), me, bit)
            got = flip(sent, "dp", size, bit)
            value = kept.astype(F32) + after(got, hold).astype(F32)
            left.remove(bit)
        outs.append(value.reshape(half, width))
    return jnp.concatenate(outs, axis=0)


def scatter_expert(total, size):
    rows = total.shape[0] // size
    low = total.astype(BF16).reshape(size, rows, total.shape[1])
    return jnp.sum(all_to_all(low).astype(F32), axis=0)


def sum_over(value, axis, size):
    bit = 1
    while bit < size:
        value = value + flip(value, axis, size, bit)
        bit *= 2
    return value


def sum_ring(value, axis, size):
    terms = [shift(value, axis, size, step) if step else value for step in range(size)]
    while len(terms) > 1:
        half = len(terms) // 2
        terms = [terms[k] + terms[k + half] for k in range(half)]
    return terms[0]


def dot(left, right):
    return jnp.dot(left, right, preferred_element_type=F32)


def dot_t(left, right):
    return lax.dot_general(left, right, (((1,), (1,)), ((), ())), preferred_element_type=F32)


def t_dot(left, right):
    return lax.dot_general(left, right, (((0,), (0,)), ((), ())), preferred_element_type=F32)

LIGHT = pl.CostEstimate(flops=1, bytes_accessed=1, transcendentals=0)


GELU_C = 0.7978845608028654
GELU_A = 0.044715


def expert_body(
    mine, x_ref, go_ref, wr_ref, wg_ref, wu_ref, wo_ref, *refs
):
    y_ref, dx_ref, gt_ref, du_ref, dy_ref, y_acc, dx_acc = refs[-7:]
    step, last = pl.program_id(0), pl.num_programs(0) - 1

    @pl.when(step == 0)
    def _():
        logits = dot(x_ref[...], wr_ref[...])
        lane = lax.broadcasted_iota(jnp.int32, logits.shape, 1)
        logits = jnp.where(lane < mine[1], logits, NEG_BIG)
        top = jnp.max(logits, axis=-1, keepdims=True)
        weights = jnp.exp(logits - top)
        total = jnp.sum(weights, axis=-1, keepdims=True)
        gate = jnp.sum(jnp.where(lane == mine[0], weights, 0.0), axis=-1, keepdims=True) / total
        dy_ref[...] = (gate * go_ref[...].astype(F32)).astype(BF16)
        y_acc[...] = jnp.zeros_like(y_acc)
        dx_acc[...] = jnp.zeros_like(dx_acc)

    x = x_ref[...]
    wg, wu, wo = wg_ref[...], wu_ref[...], wo_ref[...]
    a, b = dot(x, wg), dot(x, wu)
    dg = dot_t(dy_ref[...], wo)
    square = a * a
    t = jnp.tanh(GELU_C * (a + GELU_A * (a * square)))
    half = 0.5 + 0.5 * t
    act = a * half
    slope = half + (0.5 * GELU_C) * a * (1.0 - t * t) * (1.0 + (3.0 * GELU_A) * square)
    g = (act * b).astype(BF16)
    da = (dg * b * slope).astype(BF16)
    db = (dg * act).astype(BF16)
    gt_ref[...] = g.T
    du_ref[0] = da
    du_ref[1] = db
    y_acc[...] += dot(g, wo)
    dx_acc[...] += dot_t(jnp.concatenate([da, db], axis=1), jnp.concatenate([wg, wu], axis=1))

    @pl.when(step == last)
    def _():
        y = y_acc[...].astype(BF16)
        y_ref[:, 0] = y.reshape(-1, *y_ref.shape[2:])
        width = y.shape[1]
        dx_ref[:, :width] = dx_acc[...].astype(BF16)
        product = go_ref[...].astype(F32) * y.astype(F32)
        rest = jnp.sum(product, axis=-1, keepdims=True)
        lane = lax.broadcasted_iota(jnp.int32, (y.shape[0], 128), 1)
        terms = jnp.zeros(lane.shape, F32)
        for place in range(3):
            term = rest.astype(BF16).astype(F32)
            terms = jnp.where(lane == place, term, terms)
            rest = rest - term
        dx_ref[:, width:] = terms.astype(BF16)


def tile_of(size, most):
    return max(t for t in range(128, most + 1, 128) if size % t == 0)


def expert_call(batch, batches, experts, mine, x, go, w_router, w_in, w_out, held):
    rows, width = x.shape
    inner = w_out.shape[0]
    tile = tile_of(inner, 256)
    tiles = inner // tile
    whole = lambda shape: pl.BlockSpec(shape, lambda j: (0,) * len(shape))
    in_specs = [
        pl.BlockSpec(memory_space=pltpu.SMEM),
        whole((rows, width)),
        whole((rows, width)),
        whole(w_router.shape),
        pl.BlockSpec((width, tile), lambda j: (0, j)),
        pl.BlockSpec((width, tile), lambda j: (0, tiles + j)),
        pl.BlockSpec((tile, width), lambda j: (j, 0)),
    ]
    args = [mine, x, go, w_router, w_in, w_in, w_out]
    aliases = {}
    if held is not None:
        in_specs += [pl.BlockSpec(memory_space=pl.ANY)] * 4
        aliases = {len(args): 0, len(args) + 1: 2, len(args) + 2: 3, len(args) + 3: 4}
        args += list(held)
    flops = 12 * rows * width * inner
    return pl.pallas_call(
        expert_body,
        grid=(tiles,),
        in_specs=in_specs,
        out_specs=[
            pl.BlockSpec((experts, 1, rows // experts, width), lambda j: (0, batch, 0, 0)),
            whole((rows, width + 128)),
            pl.BlockSpec((tile, rows), lambda j: (j, batch)),
            pl.BlockSpec((2, rows, tile), lambda j: (0, batch, j)),
            pl.BlockSpec((rows, width), lambda j: (batch, 0)),
        ],
        out_shape=[
            jax.ShapeDtypeStruct((experts, batches, rows // experts, width), BF16),
            jax.ShapeDtypeStruct((rows, width + 128), BF16),
            jax.ShapeDtypeStruct((inner, batches * rows), BF16),
            jax.ShapeDtypeStruct((2, batches * rows, inner), BF16),
            jax.ShapeDtypeStruct((batches * rows, width), BF16),
        ],
        scratch_shapes=[pltpu.VMEM((rows, width), F32), pltpu.VMEM((rows, width), F32)],
        input_output_aliases=aliases,
        compiler_params=pltpu.CompilerParams(vmem_limit_bytes=56 << 20),
        cost_estimate=LIGHT,
        name="expert",
    )(*args)


def keep_and_send(value, core, keep_ref, send_ref, place):
    value = value.reshape((-1, 2) + value.shape[1:])
    even, odd = value[:, 0], value[:, 1]
    keep_ref[place] = jnp.where(core == 0, even, odd)
    send_ref[place] = jnp.where(core == 0, odd, even)


def weight_in_body(*refs):
    xs, du_ref, out_ref, flipped = refs[:-3], refs[-3], refs[-2], refs[-1]
    rows = xs[0].shape[0]

    @pl.when(pl.program_id(0) == 0)
    def _():
        for n, x_ref in enumerate(xs):
            flipped[:, n * rows : (n + 1) * rows] = x_ref[...].T

    tile = out_ref.shape[2]
    part = flipped.shape[0] // out_ref.shape[0]
    for place in range(out_ref.shape[1] // part):
        value = dot(flipped[...], du_ref[0, :, place * tile : (place + 1) * tile]).astype(BF16)
        out_ref[:, place * part : (place + 1) * part] = value.reshape(-1, part, tile)


def weight_in_call(size, xs, du):
    rows, width = xs[0].shape
    _, total, inner = du.shape
    tile = tile_of(inner, 256)
    tiles = inner // tile
    part = width // size
    space = 2 * tiles * part + (inner // size) * (width // tile)
    return pl.pallas_call(
        weight_in_body,
        grid=(2,),
        in_specs=[pl.BlockSpec((rows, width), lambda j: (0, 0)) for _ in xs]
        + [pl.BlockSpec((1, total, inner), lambda j: (j, 0, 0))],
        out_specs=pl.BlockSpec((size, tiles * part, tile), lambda j: (0, j, 0)),
        out_shape=jax.ShapeDtypeStruct((size, space, tile), BF16),
        scratch_shapes=[pltpu.VMEM((width, total), BF16)],
        compiler_params=pltpu.CompilerParams(vmem_limit_bytes=56 << 20),
        cost_estimate=LIGHT,
        name="weight_in",
    )(*xs, du)


def weight_out_body(gt_ref, dy_ref, _, out_ref):
    out_ref[...] = dot(gt_ref[...], dy_ref[...]).astype(BF16).reshape(out_ref.shape)


def weight_out_call(gt, dy, joined):
    inner, total = gt.shape
    width = dy.shape[1]
    size, space, tile = joined.shape
    part = inner // size
    first = (space - part * (width // tile)) // part
    assert first * part + part * (width // tile) == space
    return pl.pallas_call(
        weight_out_body,
        grid=(width // tile,),
        in_specs=[
            pl.BlockSpec((inner, total), lambda j: (0, 0)),
            pl.BlockSpec((total, tile), lambda j: (0, j)),
            pl.BlockSpec(memory_space=pl.ANY),
        ],
        out_specs=pl.BlockSpec((size, part, tile), lambda j: (0, first + j, 0)),
        out_shape=jax.ShapeDtypeStruct(joined.shape, BF16),
        input_output_aliases={2: 0},
        compiler_params=pltpu.CompilerParams(vmem_limit_bytes=56 << 20),
        cost_estimate=LIGHT,
        name="weight_out",
    )(gt, dy, joined)


def spread_body(count, summed_ref, in_ref, out_ref):
    part, tile = in_ref.shape[0], summed_ref.shape[1]
    for place in range(count):
        piece = summed_ref[place * part : (place + 1) * part]
        in_ref[:, place * tile : (place + 1) * tile] = piece.astype(F32)
    base, part = count * part, out_ref.shape[0]
    for place in range(out_ref.shape[1] // tile):
        piece = summed_ref[base + place * part : base + (place + 1) * part]
        out_ref[:, place * tile : (place + 1) * tile] = piece.astype(F32)


def spread_call(summed, in_shape, out_shape):
    return pl.pallas_call(
        partial(spread_body, in_shape[1] // summed.shape[1]),
        out_shape=[jax.ShapeDtypeStruct(shape, F32) for shape in (in_shape, out_shape)],
        compiler_params=pltpu.CompilerParams(vmem_limit_bytes=56 << 20),
        cost_estimate=LIGHT,
        name="spread",
    )(summed)


def weight_attn_body(count, core_ref, *refs):
    n1s, os, dqkvs, dbranches = (refs[k * count : (k + 1) * count] for k in range(4))
    keep_ref, send_ref, flipped, right = refs[4 * count :]
    step, last = pl.program_id(0), pl.num_programs(0) - 1
    length = n1s[0].shape[0]
    blocks = 2 * keep_ref.shape[0]

    def fill(lefts, rights):
        for n in range(count):
            if lefts is not None:
                flipped[:, n * length : (n + 1) * length] = lefts[n][...].T
            right[n * length : (n + 1) * length] = rights[n][...]

    @pl.when(step == 0)
    def _():
        fill(n1s, dqkvs)

    @pl.when((step > 0) & (step < last))
    def _():
        fill(None, dqkvs)

    @pl.when(step == last)
    def _():
        fill(os, dbranches)

    value = dot(flipped[...], right[...]).astype(BF16)
    value = value.reshape(blocks, -1, value.shape[1])
    keep_and_send(value, core_ref[0], keep_ref, send_ref, slice(None))


def weight_attn_call(size, core, n1s, os, dqkvs, dbranches):
    count = len(n1s)
    length, width = n1s[0].shape
    whole = pl.BlockSpec((length, width), lambda j: (0, 0))
    half = pl.BlockSpec((size // 2, width // size, width), lambda j: (0, 0, j))
    return pl.pallas_call(
        partial(weight_attn_body, count),
        grid=(4,),
        in_specs=[pl.BlockSpec(memory_space=pltpu.SMEM)]
        + [whole] * (2 * count)
        + [pl.BlockSpec((length, width), lambda j: (0, jnp.minimum(j, 2)))] * count
        + [whole] * count,
        out_specs=[half, half],
        out_shape=[jax.ShapeDtypeStruct((size // 2, width // size, 4 * width), BF16)] * 2,
        scratch_shapes=[
            pltpu.VMEM((width, count * length), BF16),
            pltpu.VMEM((count * length, width), BF16),
        ],
        compiler_params=pltpu.CompilerParams(vmem_limit_bytes=56 << 20),
        cost_estimate=LIGHT,
        name="weight_attn",
    )(core, *n1s, *os, *dqkvs, *dbranches)


def lane_below(shape, limit):
    return lax.broadcasted_iota(jnp.int32, shape, 1) < limit


def allowed_keys(rows, columns):
    segment_q, parent_q = rows[0:1], rows[1:2]
    segment_k, parent_k = columns[:, 0:1], columns[:, 1:2]
    return (segment_k == segment_q) | (segment_k == parent_q) | (parent_k == segment_q)


def pair_scores(h, head_size, scale, q, k, bias, allowed):
    low = lane_below(k.shape, head_size)
    mine = low if h % 2 == 0 else ~low
    raw = dot_t(jnp.where(mine, k, jnp.zeros_like(k)), q) * scale + bias
    return jnp.where(allowed, raw, NEG_BIG)


def piece_moves(me, pieces, rels, whole, arrived):
    moves = []
    for number, piece in enumerate(pieces):
        part, other = number % 2, number // 2
        half = piece.shape[1]
        for place, rel in enumerate(rels[part]):
            row = pl.multiple_of((me ^ rel ^ other) * (2 * half) + part * half, half)
            moves.append(
                pltpu.make_async_copy(
                    piece.at[place], whole.at[pl.ds(row, half)], arrived.at[len(moves)]
                )
            )
            moves[-1].start()
    return moves


def join_body(rels, me_ref, *refs):
    pieces, whole, arrived = refs[:-2], refs[-2], refs[-1]
    for move in piece_moves(me_ref[0], pieces, rels, whole, arrived):
        move.wait()


def join_call(me, pieces, rels):
    outside = pl.BlockSpec(memory_space=pl.ANY)
    count = 4 * len(rels[0])
    return pl.pallas_call(
        partial(join_body, rels),
        in_specs=[pl.BlockSpec(memory_space=pltpu.SMEM)] + [outside] * len(pieces),
        out_specs=pl.BlockSpec(memory_space=pltpu.VMEM),
        out_shape=jax.ShapeDtypeStruct((count * pieces[0].shape[1], pieces[0].shape[2]), BF16),
        scratch_shapes=[pltpu.SemaphoreType.DMA((count,))],
        cost_estimate=LIGHT,
        name="join",
    )(me, *pieces)


def forward_body(heads, experts, rels, *refs):
    if rels is None:
        weights_ref, refs = refs[0], refs[1:]
    else:
        me_ref, pieces, refs = refs[0], refs[1:5], refs[5:]
        refs, (full_ref, weights_ref, arrived, written) = refs[:-4], refs[-4:]
        moves = piece_moves(me_ref[0], pieces, rels, weights_ref, arrived)
    (
        tokens_ref,
        gain1_ref,
        bias_ref,
        rows_ref,
        columns_ref,
        gain2_ref,
        router_ref,
        targets_ref,
        x_ref,
        n1_ref,
        qkv_ref,
        lse_ref,
        o_ref,
        h1_ref,
        probs_ref,
    ) = refs
    length, width = tokens_ref.shape
    head_size = width // heads
    scale = head_size ** (-0.5)
    h0 = tokens_ref[...].astype(F32)
    n1 = (h0 * rms_scale(h0) * gain1_ref[...]).astype(BF16)
    n1_ref[...] = n1
    if rels is not None:
        for move in moves:
            move.wait()
        keep = pltpu.make_async_copy(weights_ref, full_ref, written)
        keep.start()
    for part in range(3):
        columns = slice(part * width, (part + 1) * width)
        qkv_ref[:, columns] = dot(n1, weights_ref[:, columns]).astype(BF16)
    allowed = allowed_keys(rows_ref[...], columns_ref[...])
    span = 2 * head_size
    for pair in range(heads // 2):
        at = pair * span
        q = qkv_ref[:, at : at + span]
        k = qkv_ref[:, width + at : width + at + span]
        flipped = qkv_ref[:, 2 * width + at : 2 * width + at + span].T
        parts = []
        for half in range(2):
            h = 2 * pair + half
            s = pair_scores(h, head_size, scale, q, k, bias_ref[h], allowed)
            top = jnp.max(s, axis=0, keepdims=True)
            e = jnp.exp(s - top)
            total = jnp.sum(e, axis=0, keepdims=True)
            lse_ref[h : h + 1] = top + jnp.log(total)
            p = (e * (1.0 / total)).astype(BF16)
            parts.append(dot(flipped[half * head_size : (half + 1) * head_size], p))
        o_ref[:, at : at + span] = jnp.concatenate(parts, axis=0).T.astype(BF16)
    h1 = h0 + dot(o_ref[...], weights_ref[:, 3 * width :])
    h1_ref[...] = h1
    n2 = (h1 * rms_scale(h1) * gain2_ref[...]).astype(BF16)
    logits = dot(n2, router_ref[...])
    logits = jnp.where(lane_below(logits.shape, experts), logits, NEG_BIG)
    top = jnp.max(logits, axis=-1, keepdims=True)
    e = jnp.exp(logits - top)
    probs_ref[...] = e / jnp.sum(e, axis=-1, keepdims=True)
    slots = lax.broadcasted_iota(jnp.int32, (x_ref.shape[0], length), 0)
    place = (slots == targets_ref[0:1]) | (slots == targets_ref[1:2])
    x_ref[...] = dot(place.astype(F32).astype(BF16), n2).astype(BF16)
    if rels is not None:
        keep.wait()


def forward_call(heads, experts, slot_count, weights, rels, *args):
    length, width = args[0].shape
    shapes = [
        ((slot_count, width), BF16),
        ((length, width), BF16),
        ((length, 3 * width), BF16),
        ((heads, length), F32),
        ((length, width), BF16),
        ((length, width), F32),
        ((length, 128), F32),
    ]
    inside = pl.BlockSpec(memory_space=pltpu.VMEM)
    outside = pl.BlockSpec(memory_space=pl.ANY)
    in_specs = [inside] * len(args)
    out_specs = [inside] * len(shapes)
    scratch = []
    if rels is None:
        args, in_specs = (weights,) + args, [inside] + in_specs
    else:
        me, pieces = weights
        args = (me, *pieces) + args
        in_specs = [pl.BlockSpec(memory_space=pltpu.SMEM)] + [outside] * len(pieces) + in_specs
        shapes.append(((width, 4 * width), BF16))
        out_specs.append(outside)
        scratch = [
            pltpu.VMEM((width, 4 * width), BF16),
            pltpu.SemaphoreType.DMA((4 * len(rels[0]),)),
            pltpu.SemaphoreType.DMA,
        ]
    return pl.pallas_call(
        partial(forward_body, heads, experts, rels),
        in_specs=in_specs,
        out_specs=out_specs,
        out_shape=[jax.ShapeDtypeStruct(*s) for s in shapes],
        scratch_shapes=scratch,
        compiler_params=pltpu.CompilerParams(vmem_limit_bytes=56 << 20),
        cost_estimate=LIGHT,
        name="attention_forward",
    )(*args)


def backward_body(
    heads,
    experts,
    dx_ref,
    targets_ref,
    routes_ref,
    probs_ref,
    h1_ref,
    go_ref,
    gain2_ref,
    router_ref,
    proj_ref,
    qkv_ref,
    lse_ref,
    bias_ref,
    rows_ref,
    columns_ref,
    dh1_ref,
    dbranch_ref,
    dqkv_ref,
    ds_ref,
    router_grad_ref,
    gain_grad_ref,
    do_ref,
):
    length, width = h1_ref.shape
    head_size = width // heads
    scale = head_size ** (-0.5)
    slots = lax.broadcasted_iota(jnp.int32, (length, dx_ref.shape[0]), 1)
    hot = [slots == targets_ref[:, j : j + 1] for j in range(2)]
    pick = [m.astype(F32).astype(BF16) for m in hot]
    dgate = [jnp.sum(dot(m, dx_ref[:, width:]), axis=-1, keepdims=True) for m in pick]
    probs = probs_ref[...]
    lane = lax.broadcasted_iota(jnp.int32, probs.shape, 1)
    dprobs = sum(jnp.where(lane == routes_ref[:, j : j + 1], dgate[j], 0.0) for j in range(2))
    dlogits = probs * (dprobs - jnp.sum(probs * dprobs, axis=-1, keepdims=True))
    dlogits = dlogits.astype(BF16)
    dn2 = dot(pick[0] + pick[1], dx_ref[:, :width]) + dot_t(dlogits, router_ref[...])
    h1 = h1_ref[...]
    r2 = rms_scale(h1)
    n2_hat = h1 * r2
    gain2 = gain2_ref[...]
    n2 = (n2_hat * gain2).astype(BF16)
    router_grad_ref[...] = t_dot(dlogits, n2)
    gain_grad_ref[...] = jnp.sum(dn2 * n2_hat, axis=0, keepdims=True)
    scaled = dn2 * gain2
    mean = jnp.mean(scaled * n2_hat, axis=-1, keepdims=True)
    dh1 = go_ref[...].astype(F32) + r2 * (scaled - n2_hat * mean)
    dh1_ref[...] = dh1
    dbranch = dh1.astype(BF16)
    dbranch_ref[...] = dbranch
    do_ref[...] = dot_t(dbranch, proj_ref[...]).astype(BF16)
    allowed = allowed_keys(rows_ref[...], columns_ref[...])
    span = 2 * head_size
    low = lane_below((length, span), head_size)
    for pair in range(heads // 2):
        at = pair * span
        q = qkv_ref[:, at : at + span]
        k = qkv_ref[:, width + at : width + at + span]
        v = qkv_ref[:, 2 * width + at : 2 * width + at + span]
        do = do_ref[:, at : at + span]
        flipped = k.T
        dq, dk, dv = [], [], []
        for half in range(2):
            h = 2 * pair + half
            s = pair_scores(h, head_size, scale, q, k, bias_ref[h], allowed)
            p = jnp.exp(s - lse_ref[h : h + 1])
            mine = low if half == 0 else ~low
            dp = dot_t(jnp.where(mine, v, jnp.zeros_like(v)), do)
            inner = jnp.sum(p * dp, axis=0, keepdims=True)
            ds = (p * (dp - inner)).astype(BF16)
            ds_ref[h] = ds
            dv.append(dot(p.astype(BF16), do))
            dk.append(dot(ds, q))
            dq.append(dot(flipped[half * head_size : (half + 1) * head_size], ds))
        dqkv_ref[:, at : at + span] = (jnp.concatenate(dq, axis=0).T * scale).astype(BF16)
        dqkv_ref[:, width + at : width + at + span] = (jnp.where(low, *dk) * scale).astype(BF16)
        dqkv_ref[:, 2 * width + at : 2 * width + at + span] = jnp.where(low, *dv).astype(BF16)


def backward_call(heads, experts, dx, targets, routes, probs, h1, go, gain2, router, proj, *rest):
    length, width = h1.shape
    shapes = [
        ((length, width), F32),
        ((length, width), BF16),
        ((length, 3 * width), BF16),
        ((heads, length, length), BF16),
        ((128, width), F32),
        ((1, width), F32),
    ]
    args = (dx, targets, routes, probs, h1, go, gain2, router, proj) + rest
    in_specs = [pl.BlockSpec(a.shape, lambda i, n=a.ndim: (0,) * n) for a in args]
    in_specs[8] = pl.BlockSpec((width, width), lambda i: (0, 3))
    return pl.pallas_call(
        partial(backward_body, heads, experts),
        grid=(1,),
        in_specs=in_specs,
        out_specs=[pl.BlockSpec(s, lambda i, n=len(s): (0,) * n) for s, _ in shapes],
        out_shape=[jax.ShapeDtypeStruct(*s) for s in shapes],
        scratch_shapes=[pltpu.VMEM((length, width), BF16)],
        compiler_params=pltpu.CompilerParams(vmem_limit_bytes=56 << 20),
        cost_estimate=LIGHT,
        name="attention_backward",
    )(*args)


def finish_body(count, tokens_ref, gain_ref, weights_ref, *refs):
    dqkvs, dh1s = refs[:count], refs[count : 2 * count]
    out_ref, gain_grad_ref = refs[2 * count :]
    gain = gain_ref[...]
    total = jnp.zeros(gain.shape, F32)
    for n in range(count):
        h0 = tokens_ref[n].astype(F32)
        r1 = rms_scale(h0)
        n1_hat = h0 * r1
        dn1 = dot_t(dqkvs[n][...], weights_ref[...])
        total = total + jnp.sum(dn1 * n1_hat, axis=0, keepdims=True)
        scaled = dn1 * gain
        mean = jnp.mean(scaled * n1_hat, axis=-1, keepdims=True)
        out_ref[n] = (dh1s[n][...] + r1 * (scaled - n1_hat * mean)).astype(BF16)
    gain_grad_ref[...] = total


def finish_call(tokens, gain, weights, dqkvs, dh1s):
    args = (tokens, gain, weights, *dqkvs, *dh1s)
    in_specs = [pl.BlockSpec(a.shape, lambda i, n=a.ndim: (0,) * n) for a in args]
    in_specs[2] = pl.BlockSpec((tokens.shape[2], 3 * tokens.shape[2]), lambda i: (0, 0))
    return pl.pallas_call(
        partial(finish_body, len(dqkvs)),
        grid=(1,),
        in_specs=in_specs,
        out_specs=[
            pl.BlockSpec(tokens.shape, lambda i: (0, 0, 0)),
            pl.BlockSpec(gain.shape, lambda i: (0, 0)),
        ],
        out_shape=[
            jax.ShapeDtypeStruct(tokens.shape, BF16),
            jax.ShapeDtypeStruct(gain.shape, F32),
        ],
        compiler_params=pltpu.CompilerParams(vmem_limit_bytes=56 << 20),
        cost_estimate=LIGHT,
        name="finish",
    )(*args)


def output_body(count, y_ref, targets_ref, routes_ref, *refs):
    probs, h1s, out_ref = refs[:count], refs[count : 2 * count], refs[-1]
    width = out_ref.shape[2]
    for n in range(count):
        y = y_ref[:, n].reshape(-1, width)
        slots = lax.broadcasted_iota(jnp.int32, (out_ref.shape[1], y.shape[0]), 1)
        total = h1s[n][...]
        moe = 0.0
        for j in range(2):
            weights = probs[n][...]
            lane = lax.broadcasted_iota(jnp.int32, weights.shape, 1)
            mine = lane == routes_ref[n, :, j : j + 1]
            gate = jnp.sum(jnp.where(mine, weights, 0.0), axis=-1, keepdims=True)
            pick = (slots == targets_ref[n, :, j : j + 1]).astype(F32).astype(BF16)
            moe = moe + gate * dot(pick, y)
        out_ref[n] = (total + moe).astype(BF16)


def output_call(y, targets, routes, probs, h1s):
    length, width = h1s[0].shape
    return pl.pallas_call(
        partial(output_body, len(h1s)),
        out_shape=jax.ShapeDtypeStruct((len(h1s), length, width), BF16),
        compiler_params=pltpu.CompilerParams(vmem_limit_bytes=56 << 20),
        cost_estimate=LIGHT,
        name="output",
    )(y, targets, routes, *probs, *h1s)


def on_device(
    sizes,
    tokens,
    cotangent,
    segment_ids,
    parent_ids,
    routes,
    gain_attn,
    w_qkv,
    w_proj,
    rel_bias,
    gain_moe,
    w_router,
    w_in,
    w_out,
):
    dp, experts = sizes["dp"], sizes["expert"]
    batches, length, width = tokens.shape
    heads = rel_bias.shape[1]
    head_size = width // heads
    inner = w_in.shape[2] // 2
    capacity = (10 * length + 4 * experts - 1) // (4 * experts)
    slot_count = experts * capacity
    scale = head_size ** (-0.5)
    me_e = lax.axis_index("expert")

    attn_block = gather_expert(jnp.concatenate([w_qkv, w_proj], axis=1), experts)
    places = jax.vmap(partial(slot_positions, experts=experts))(routes)
    targets = routes * capacity + places
    hot = targets[..., None] == jnp.arange(slot_count, dtype=jnp.int32)
    select = hot.astype(BF16)
    both = select[:, :, 0] + select[:, :, 1]
    out_grads = [cotangent[n] for n in range(batches)]
    outgoing = [
        t_dot(both[n], out_grads[n]).astype(BF16).reshape(experts, capacity, width)
        for n in range(batches)
    ]
    go_joint = all_to_all(after(jnp.stack(outgoing, axis=1), attn_block))
    go_slots = [go_joint[:, n] for n in range(batches)]

    positions = jnp.arange(length, dtype=jnp.int32)
    buckets = bucket_of(positions[:, None] - positions[None, :])
    bucket_hot = (buckets[:, :, None] == jnp.arange(rel_bias.shape[0], dtype=jnp.int32)).astype(F32)
    bias = jnp.einsum("kqc,ch->hkq", bucket_hot, rel_bias, precision=lax.Precision.HIGHEST)

    me_d = lax.axis_index("dp").astype(jnp.int32)[None]
    attn_first = gather_first(attn_block, dp, outgoing)
    pieces, rels = gather_dp(attn_first, dp, bias)
    wout_full = lax.all_gather(w_out[0], "dp", axis=0, tiled=True)
    win_full = lax.all_gather(
        after(w_in[0], pieces[:2], go_slots[0]), "dp", axis=0, tiled=True
    )

    router_wide = jnp.pad(w_router, ((0, 0), (0, 128 - experts)))
    gain1, gain2 = gain_attn[None], gain_moe[None]
    saved = []
    for n in range(batches):
        id_rows = jnp.stack([segment_ids[n], parent_ids[n]])
        target_columns = targets[n]
        weights = attn_w if n else (me_d, pieces)
        outs = forward_call(
            heads,
            experts,
            slot_count,
            weights,
            None if n else rels,
            tokens[n],
            gain1,
            bias,
            id_rows,
            id_rows.T,
            gain2,
            router_wide,
            target_columns.T,
        )
        if n == 0:
            *outs, attn_w = outs
        x_slots = all_to_all(after(outs[0], go_slots).reshape(experts, capacity, width))
        saved.append((id_rows,) + tuple(outs[1:]) + (x_slots,))

    mine = jnp.stack([me_e, jnp.int32(experts)]).astype(jnp.int32)
    held, grads = [], None
    for n in range(batches):
        x = saved[n][-1].reshape(slot_count, width)
        go = go_slots[n].reshape(slot_count, width)
        y, dx, *grads = expert_call(
            n, batches, experts, mine, x, go, router_wide, win_full, wout_full, grads
        )
        grads = [y] + grads
        dx_back = all_to_all(dx.reshape(experts, capacity, width + 128))
        held.append((x, dx_back.reshape(slot_count, width + 128)))

    def backward(n, dx_back):
        id_rows, _, qkv, lse, _, h1, probs, _ = saved[n]
        return backward_call(
            heads,
            experts,
            dx_back,
            targets[n],
            routes[n],
            probs,
            h1,
            out_grads[n],
            gain2,
            router_wide,
            attn_w,
            qkv,
            lse,
            bias,
            id_rows,
            id_rows.T,
        )

    core = me_d % 2
    _, gt, du, dy = grads
    joined = weight_in_call(dp, [h[0] for h in held], after(du, held[0][1]))
    joined = after(weight_out_call(gt, dy, joined), held[1][1])
    backs = [backward(n, after(held[n][1], joined)) for n in range(batches)]
    attn_keep, attn_send = weight_attn_call(
        dp,
        core,
        [v[1] for v in saved],
        [v[4] for v in saved],
        [v[2] for v in backs],
        [v[1] for v in backs],
    )
    y_back = all_to_all(after(grads[0], attn_keep))
    attn_core = scatter_core(attn_keep, attn_send, dp)
    space, tile = joined.shape[1:]
    summed = lax.psum_scatter(
        joined.reshape(dp * space, tile), "dp", scatter_dimension=0, tiled=True
    )
    in_total, out_total = spread_call(summed, w_in.shape[1:], w_out.shape[1:])

    router_grad = sum(v[4] for v in backs)[:experts].T
    gain_moe_grad = sum(v[5] for v in backs)[0]
    table_grad = jnp.einsum(
        "nhkq,kqc->ch",
        after(jnp.stack([v[3] for v in backs]), attn_core),
        bucket_hot.astype(BF16),
        preferred_element_type=F32,
    )
    input_grads, gain_attn_grad = finish_call(
        tokens, gain1, attn_w, [after(v[2], attn_core) for v in backs], [v[0] for v in backs]
    )
    small = jnp.concatenate(
        [gain_attn_grad[0], table_grad.reshape(-1), gain_moe_grad, router_grad.reshape(-1)]
    )
    small = sum_over(small.reshape(-1, 128), "dp", dp)
    attn_sum = scatter_dp(attn_core, dp, (input_grads, table_grad))
    small = sum_ring(after(small, attn_sum), "expert", experts).reshape(-1)
    attn_total = scatter_expert(attn_sum, experts)
    qkv_total, proj_total = attn_total[:, : 3 * width], attn_total[:, 3 * width :]
    outputs = output_call(
        after(y_back, attn_sum), targets, routes, [v[6] for v in saved], [v[5] for v in saved]
    )
    cuts = (width, width + table_grad.size, 2 * width + table_grad.size)
    return (
        outputs,
        input_grads,
        small[: cuts[0]],
        qkv_total,
        proj_total,
        small[cuts[0] : cuts[1]].reshape(table_grad.shape),
        small[cuts[1] : cuts[2]],
        small[cuts[2] :].reshape(router_grad.shape),
        in_total[None],
        out_total[None],
    )


def solution(mesh):
    rows = P(None, ("dp", "expert"), None)
    in_specs = (
        rows,
        rows,
        P(None, ("dp", "expert")),
        P(None, ("dp", "expert")),
        rows,
        P(),
        P(("dp", "expert"), None),
        P(("dp", "expert"), None),
        P(),
        P(),
        P(),
        P("expert", "dp", None),
        P("expert", "dp", None),
    )
    out_specs = (
        rows,
        rows,
        P(),
        P(("dp", "expert"), None),
        P(("dp", "expert"), None),
        P(),
        P(),
        P(),
        P("expert", "dp", None),
        P("expert", "dp", None),
    )
    return jax.shard_map(
        partial(on_device, dict(mesh.shape)),
        mesh=mesh,
        in_specs=in_specs,
        out_specs=out_specs,
        check_vma=False,
    )
```

```python
from functools import partial

import jax
import jax.numpy as jnp
from jax import lax
from jax.experimental import pallas as pl
from jax.experimental.pallas import tpu as pltpu
from jax.sharding import PartitionSpec as P

EPSILON = 1e-06
NEG_BIG = -1e30
LIMITS = (12, 16, 23, 32, 46, 64, 91)
F32 = jnp.float32
BF16 = jnp.bfloat16


def bucket_of(offset):
    distance = jnp.abs(offset)
    far_part = 8 + sum(((distance >= limit).astype(jnp.int32) for limit in LIMITS))
    near_far = jnp.where(distance < 8, distance, far_part)
    return jnp.where(offset > 0, 16, 0) + near_far


def slot_positions(routes, experts):
    order = jnp.concatenate([routes[:, 0], routes[:, 1]])
    chosen = (order[:, None] == jnp.arange(experts, dtype=jnp.int32)[None, :]).astype(jnp.int32)
    before = jnp.cumsum(chosen, axis=0) - chosen
    place = jnp.sum(before * chosen, axis=1)
    return place.reshape(2, -1).T


def tree_mask(segment, parent):
    same = segment[None, :] == segment[:, None]
    upward = segment[None, :] == parent[:, None]
    downward = parent[None, :] == segment[:, None]
    return same | upward | downward


def rms_scale(values):
    return lax.rsqrt(jnp.mean(values * values, axis=-1, keepdims=True) + EPSILON)


def gelu_product(gate_part, up_part):
    return jax.nn.gelu(gate_part, approximate=True) * up_part


def after(value, *others):
    return lax.optimization_barrier((value, others))[0]


def flip(value, axis, size, bit):
    return lax.ppermute(value, axis, [(i, i ^ bit) for i in range(size)])


def shift(value, axis, size, step):
    return lax.ppermute(value, axis, [(i, (i + step) % size) for i in range(size)])


def halving_orders(size):
    bits = [1 << k for k in range(1, size.bit_length() - 1)]
    return (bits, bits[::-1])


def gather_first(block, size, hold):
    half = block.shape[0] // 2
    out = []
    for part, order in enumerate(halving_orders(size)):
        have = after(block[None, part * half : (part + 1) * half], hold)
        out.append(jnp.concatenate([have, flip(have, "dp", size, order[0])], axis=0))
    return out


def gather_dp(first, size, hold):
    near, rels = [], []
    for have, order in zip(first, halving_orders(size)):
        have = after(have, hold)
        order_rels = [0, order[0]]
        for bit in order[1:]:
            have = jnp.concatenate([have, flip(have, "dp", size, bit)], axis=0)
            order_rels = order_rels + [rel ^ bit for rel in order_rels]
        near.append(have)
        rels.append(order_rels)
    far = [flip(have, "dp", size, 1) for have in near]
    return near + far, rels


def gather_expert(block, size):
    me = lax.axis_index("expert")
    full = jnp.zeros((size,) + block.shape, block.dtype)
    for step in range(size):
        piece = shift(block, "expert", size, step) if step else block
        full = lax.dynamic_update_slice(full, piece[None], ((me - step) % size, 0, 0))
    return full.reshape(size * block.shape[0], block.shape[1])


def all_to_all(value):
    return lax.all_to_all(value, "expert", split_axis=0, concat_axis=0, tiled=True)


def split_bit(value, me, bit):
    mine = (me // bit) % 2
    kept = lax.dynamic_index_in_dim(value, mine, 0, keepdims=False)
    sent = lax.dynamic_index_in_dim(value, 1 - mine, 0, keepdims=False)
    return kept, sent


def scatter_core(keep, send, size):
    return (keep.astype(F32) + flip(send, "dp", size, 1).astype(F32)).astype(BF16)


def scatter_dp(summed, size, hold):
    me = lax.axis_index("dp")
    _, rows, width = summed.shape
    half = rows // 2
    outs = []
    for part, order in enumerate(halving_orders(size)):
        value = summed[:, part * half : (part + 1) * half]
        left = [1 << k for k in range(1, size.bit_length() - 1)]
        for bit in order:
            place = left.index(bit)
            high, low = 1 << (len(left) - 1 - place), 1 << place
            shaped = value.astype(BF16).reshape(high, 2, low, half, width)
            kept, sent = split_bit(jnp.moveaxis(shaped, 1, 0), me, bit)
            got = flip(sent, "dp", size, bit)
            value = kept.astype(F32) + after(got, hold).astype(F32)
            left.remove(bit)
        outs.append(value.reshape(half, width))
    return jnp.concatenate(outs, axis=0)


def scatter_expert(total, size):
    rows = total.shape[0] // size
    low = total.astype(BF16).reshape(size, rows, total.shape[1])
    return jnp.sum(all_to_all(low).astype(F32), axis=0)


def sum_over(value, axis, size):
    bit = 1
    while bit < size:
        value = value + flip(value, axis, size, bit)
        bit *= 2
    return value


def sum_ring(value, axis, size):
    terms = [shift(value, axis, size, step) if step else value for step in range(size)]
    while len(terms) > 1:
        half = len(terms) // 2
        terms = [terms[k] + terms[k + half] for k in range(half)]
    return terms[0]


def dot(left, right):
    return jnp.dot(left, right, preferred_element_type=F32)


def dot_t(left, right):
    return lax.dot_general(left, right, (((1,), (1,)), ((), ())), preferred_element_type=F32)


def t_dot(left, right):
    return lax.dot_general(left, right, (((0,), (0,)), ((), ())), preferred_element_type=F32)

LIGHT = pl.CostEstimate(flops=1, bytes_accessed=1, transcendentals=0)


GELU_C = 0.7978845608028654
GELU_A = 0.044715


def expert_body(
    mine, x_ref, go_ref, wr_ref, wg_ref, wu_ref, wo_ref, *refs
):
    y_ref, dx_ref, gt_ref, du_ref, dy_ref, y_acc, dx_acc = refs[-7:]
    step, last = pl.program_id(0), pl.num_programs(0) - 1

    @pl.when(step == 0)
    def _():
        logits = dot(x_ref[...], wr_ref[...])
        lane = lax.broadcasted_iota(jnp.int32, logits.shape, 1)
        logits = jnp.where(lane < mine[1], logits, NEG_BIG)
        top = jnp.max(logits, axis=-1, keepdims=True)
        weights = jnp.exp(logits - top)
        total = jnp.sum(weights, axis=-1, keepdims=True)
        gate = jnp.sum(jnp.where(lane == mine[0], weights, 0.0), axis=-1, keepdims=True) / total
        dy_ref[...] = (gate * go_ref[...].astype(F32)).astype(BF16)
        y_acc[...] = jnp.zeros_like(y_acc)
        dx_acc[...] = jnp.zeros_like(dx_acc)

    x = x_ref[...]
    wg, wu, wo = wg_ref[...], wu_ref[...], wo_ref[...]
    a, b = dot(x, wg), dot(x, wu)
    dg = dot_t(dy_ref[...], wo)
    square = a * a
    t = jnp.tanh(GELU_C * (a + GELU_A * (a * square)))
    half = 0.5 + 0.5 * t
    act = a * half
    slope = half + (0.5 * GELU_C) * a * (1.0 - t * t) * (1.0 + (3.0 * GELU_A) * square)
    g = (act * b).astype(BF16)
    da = (dg * b * slope).astype(BF16)
    db = (dg * act).astype(BF16)
    gt_ref[...] = g.T
    du_ref[0] = da
    du_ref[1] = db
    y_acc[...] += dot(g, wo)
    dx_acc[...] += dot_t(jnp.concatenate([da, db], axis=1), jnp.concatenate([wg, wu], axis=1))

    @pl.when(step == last)
    def _():
        y = y_acc[...].astype(BF16)
        y_ref[:, 0] = y.reshape(-1, *y_ref.shape[2:])
        width = y.shape[1]
        dx_ref[:, :width] = dx_acc[...].astype(BF16)
        product = go_ref[...].astype(F32) * y.astype(F32)
        rest = jnp.sum(product, axis=-1, keepdims=True)
        lane = lax.broadcasted_iota(jnp.int32, (y.shape[0], 128), 1)
        terms = jnp.zeros(lane.shape, F32)
        for place in range(3):
            term = rest.astype(BF16).astype(F32)
            terms = jnp.where(lane == place, term, terms)
            rest = rest - term
        dx_ref[:, width:] = terms.astype(BF16)


def tile_of(size, most):
    return max(t for t in range(128, most + 1, 128) if size % t == 0)


def expert_call(batch, batches, experts, mine, x, go, w_router, w_in, w_out, held):
    rows, width = x.shape
    inner = w_out.shape[0]
    tile = tile_of(inner, 256)
    tiles = inner // tile
    whole = lambda shape: pl.BlockSpec(shape, lambda j: (0,) * len(shape))
    in_specs = [
        pl.BlockSpec(memory_space=pltpu.SMEM),
        whole((rows, width)),
        whole((rows, width)),
        whole(w_router.shape),
        pl.BlockSpec((width, tile), lambda j: (0, j)),
        pl.BlockSpec((width, tile), lambda j: (0, tiles + j)),
        pl.BlockSpec((tile, width), lambda j: (j, 0)),
    ]
    args = [mine, x, go, w_router, w_in, w_in, w_out]
    aliases = {}
    if held is not None:
        in_specs += [pl.BlockSpec(memory_space=pl.ANY)] * 4
        aliases = {len(args): 0, len(args) + 1: 2, len(args) + 2: 3, len(args) + 3: 4}
        args += list(held)
    flops = 12 * rows * width * inner
    return pl.pallas_call(
        expert_body,
        grid=(tiles,),
        in_specs=in_specs,
        out_specs=[
            pl.BlockSpec((experts, 1, rows // experts, width), lambda j: (0, batch, 0, 0)),
            whole((rows, width + 128)),
            pl.BlockSpec((tile, rows), lambda j: (j, batch)),
            pl.BlockSpec((2, rows, tile), lambda j: (0, batch, j)),
            pl.BlockSpec((rows, width), lambda j: (batch, 0)),
        ],
        out_shape=[
            jax.ShapeDtypeStruct((experts, batches, rows // experts, width), BF16),
            jax.ShapeDtypeStruct((rows, width + 128), BF16),
            jax.ShapeDtypeStruct((inner, batches * rows), BF16),
            jax.ShapeDtypeStruct((2, batches * rows, inner), BF16),
            jax.ShapeDtypeStruct((batches * rows, width), BF16),
        ],
        scratch_shapes=[pltpu.VMEM((rows, width), F32), pltpu.VMEM((rows, width), F32)],
        input_output_aliases=aliases,
        compiler_params=pltpu.CompilerParams(vmem_limit_bytes=56 << 20),
        cost_estimate=LIGHT,
        name="expert",
    )(*args)


def keep_and_send(value, core, keep_ref, send_ref, place):
    value = value.reshape((-1, 2) + value.shape[1:])
    even, odd = value[:, 0], value[:, 1]
    keep_ref[place] = jnp.where(core == 0, even, odd)
    send_ref[place] = jnp.where(core == 0, odd, even)


def weight_in_body(*refs):
    xs, du_ref, out_ref, flipped = refs[:-3], refs[-3], refs[-2], refs[-1]
    rows = xs[0].shape[0]

    @pl.when(pl.program_id(0) == 0)
    def _():
        for n, x_ref in enumerate(xs):
            flipped[:, n * rows : (n + 1) * rows] = x_ref[...].T

    tile = out_ref.shape[2]
    part = flipped.shape[0] // out_ref.shape[0]
    for place in range(out_ref.shape[1] // part):
        value = dot(flipped[...], du_ref[0, :, place * tile : (place + 1) * tile]).astype(BF16)
        out_ref[:, place * part : (place + 1) * part] = value.reshape(-1, part, tile)


def weight_in_call(size, xs, du):
    rows, width = xs[0].shape
    _, total, inner = du.shape
    tile = tile_of(inner, 256)
    tiles = inner // tile
    part = width // size
    space = 2 * tiles * part + (inner // size) * (width // tile)
    return pl.pallas_call(
        weight_in_body,
        grid=(2,),
        in_specs=[pl.BlockSpec((rows, width), lambda j: (0, 0)) for _ in xs]
        + [pl.BlockSpec((1, total, inner), lambda j: (j, 0, 0))],
        out_specs=pl.BlockSpec((size, tiles * part, tile), lambda j: (0, j, 0)),
        out_shape=jax.ShapeDtypeStruct((size, space, tile), BF16),
        scratch_shapes=[pltpu.VMEM((width, total), BF16)],
        compiler_params=pltpu.CompilerParams(vmem_limit_bytes=56 << 20),
        cost_estimate=LIGHT,
        name="weight_in",
    )(*xs, du)


def weight_out_body(gt_ref, dy_ref, _, out_ref):
    out_ref[...] = dot(gt_ref[...], dy_ref[...]).astype(BF16).reshape(out_ref.shape)


def weight_out_call(gt, dy, joined):
    inner, total = gt.shape
    width = dy.shape[1]
    size, space, tile = joined.shape
    part = inner // size
    first = (space - part * (width // tile)) // part
    assert first * part + part * (width // tile) == space
    return pl.pallas_call(
        weight_out_body,
        grid=(width // tile,),
        in_specs=[
            pl.BlockSpec((inner, total), lambda j: (0, 0)),
            pl.BlockSpec((total, tile), lambda j: (0, j)),
            pl.BlockSpec(memory_space=pl.ANY),
        ],
        out_specs=pl.BlockSpec((size, part, tile), lambda j: (0, first + j, 0)),
        out_shape=jax.ShapeDtypeStruct(joined.shape, BF16),
        input_output_aliases={2: 0},
        compiler_params=pltpu.CompilerParams(vmem_limit_bytes=56 << 20),
        cost_estimate=LIGHT,
        name="weight_out",
    )(gt, dy, joined)


def spread_body(count, summed_ref, in_ref, out_ref):
    part, tile = in_ref.shape[0], summed_ref.shape[1]
    for place in range(count):
        piece = summed_ref[place * part : (place + 1) * part]
        in_ref[:, place * tile : (place + 1) * tile] = piece.astype(F32)
    base, part = count * part, out_ref.shape[0]
    for place in range(out_ref.shape[1] // tile):
        piece = summed_ref[base + place * part : base + (place + 1) * part]
        out_ref[:, place * tile : (place + 1) * tile] = piece.astype(F32)


def spread_call(summed, in_shape, out_shape):
    return pl.pallas_call(
        partial(spread_body, in_shape[1] // summed.shape[1]),
        out_shape=[jax.ShapeDtypeStruct(shape, F32) for shape in (in_shape, out_shape)],
        compiler_params=pltpu.CompilerParams(vmem_limit_bytes=32 << 20),
        cost_estimate=LIGHT,
        name="spread",
    )(summed)


def weight_attn_body(count, core_ref, *refs):
    n1s, os, dqkvs, dbranches = (refs[k * count : (k + 1) * count] for k in range(4))
    keep_ref, send_ref, flipped, right = refs[4 * count :]
    step, last = pl.program_id(0), pl.num_programs(0) - 1
    length = n1s[0].shape[0]
    blocks = 2 * keep_ref.shape[0]

    def fill(lefts, rights):
        for n in range(count):
            if lefts is not None:
                flipped[:, n * length : (n + 1) * length] = lefts[n][...].T
            right[n * length : (n + 1) * length] = rights[n][...]

    @pl.when(step == 0)
    def _():
        fill(n1s, dqkvs)

    @pl.when((step > 0) & (step < last))
    def _():
        fill(None, dqkvs)

    @pl.when(step == last)
    def _():
        fill(os, dbranches)

    value = dot(flipped[...], right[...]).astype(BF16)
    value = value.reshape(blocks, -1, value.shape[1])
    keep_and_send(value, core_ref[0], keep_ref, send_ref, slice(None))


def weight_attn_call(size, core, n1s, os, dqkvs, dbranches):
    count = len(n1s)
    length, width = n1s[0].shape
    whole = pl.BlockSpec((length, width), lambda j: (0, 0))
    half = pl.BlockSpec((size // 2, width // size, width), lambda j: (0, 0, j))
    return pl.pallas_call(
        partial(weight_attn_body, count),
        grid=(4,),
        in_specs=[pl.BlockSpec(memory_space=pltpu.SMEM)]
        + [whole] * (2 * count)
        + [pl.BlockSpec((length, width), lambda j: (0, jnp.minimum(j, 2)))] * count
        + [whole] * count,
        out_specs=[half, half],
        out_shape=[jax.ShapeDtypeStruct((size // 2, width // size, 4 * width), BF16)] * 2,
        scratch_shapes=[
            pltpu.VMEM((width, count * length), BF16),
            pltpu.VMEM((count * length, width), BF16),
        ],
        compiler_params=pltpu.CompilerParams(vmem_limit_bytes=32 << 20),
        cost_estimate=LIGHT,
        name="weight_attn",
    )(core, *n1s, *os, *dqkvs, *dbranches)


def lane_below(shape, limit):
    return lax.broadcasted_iota(jnp.int32, shape, 1) < limit


def allowed_keys(rows, columns):
    segment_q, parent_q = rows[0:1], rows[1:2]
    segment_k, parent_k = columns[:, 0:1], columns[:, 1:2]
    return (segment_k == segment_q) | (segment_k == parent_q) | (parent_k == segment_q)


def pair_scores(h, head_size, scale, q, k, bias, allowed):
    low = lane_below(k.shape, head_size)
    mine = low if h % 2 == 0 else ~low
    raw = dot_t(jnp.where(mine, k, jnp.zeros_like(k)), q) * scale + bias
    return jnp.where(allowed, raw, NEG_BIG)


def piece_moves(me, pieces, rels, whole, arrived):
    moves = []
    for number, piece in enumerate(pieces):
        part, other = number % 2, number // 2
        half = piece.shape[1]
        for place, rel in enumerate(rels[part]):
            row = pl.multiple_of((me ^ rel ^ other) * (2 * half) + part * half, half)
            moves.append(
                pltpu.make_async_copy(
                    piece.at[place], whole.at[pl.ds(row, half)], arrived.at[len(moves)]
                )
            )
            moves[-1].start()
    return moves


def join_body(rels, me_ref, *refs):
    pieces, whole, arrived = refs[:-2], refs[-2], refs[-1]
    for move in piece_moves(me_ref[0], pieces, rels, whole, arrived):
        move.wait()


def join_call(me, pieces, rels):
    outside = pl.BlockSpec(memory_space=pl.ANY)
    count = 4 * len(rels[0])
    return pl.pallas_call(
        partial(join_body, rels),
        in_specs=[pl.BlockSpec(memory_space=pltpu.SMEM)] + [outside] * len(pieces),
        out_specs=pl.BlockSpec(memory_space=pltpu.VMEM),
        out_shape=jax.ShapeDtypeStruct((count * pieces[0].shape[1], pieces[0].shape[2]), BF16),
        scratch_shapes=[pltpu.SemaphoreType.DMA((count,))],
        cost_estimate=LIGHT,
        name="join",
    )(me, *pieces)


def forward_body(heads, experts, rels, *refs):
    if rels is None:
        weights_ref, refs = refs[0], refs[1:]
    else:
        me_ref, pieces, refs = refs[0], refs[1:5], refs[5:]
        refs, (full_ref, weights_ref, arrived, written) = refs[:-4], refs[-4:]
        moves = piece_moves(me_ref[0], pieces, rels, weights_ref, arrived)
    (
        tokens_ref,
        gain1_ref,
        bias_ref,
        rows_ref,
        columns_ref,
        gain2_ref,
        router_ref,
        targets_ref,
        x_ref,
        n1_ref,
        qkv_ref,
        lse_ref,
        o_ref,
        h1_ref,
        probs_ref,
    ) = refs
    length, width = tokens_ref.shape
    head_size = width // heads
    scale = head_size ** (-0.5)
    h0 = tokens_ref[...].astype(F32)
    n1 = (h0 * rms_scale(h0) * gain1_ref[...]).astype(BF16)
    n1_ref[...] = n1
    if rels is not None:
        for move in moves:
            move.wait()
        keep = pltpu.make_async_copy(weights_ref, full_ref, written)
        keep.start()
    for part in range(3):
        columns = slice(part * width, (part + 1) * width)
        qkv_ref[:, columns] = dot(n1, weights_ref[:, columns]).astype(BF16)
    allowed = allowed_keys(rows_ref[...], columns_ref[...])
    span = 2 * head_size
    for pair in range(heads // 2):
        at = pair * span
        q = qkv_ref[:, at : at + span]
        k = qkv_ref[:, width + at : width + at + span]
        flipped = qkv_ref[:, 2 * width + at : 2 * width + at + span].T
        parts = []
        for half in range(2):
            h = 2 * pair + half
            s = pair_scores(h, head_size, scale, q, k, bias_ref[h], allowed)
            top = jnp.max(s, axis=0, keepdims=True)
            e = jnp.exp(s - top)
            total = jnp.sum(e, axis=0, keepdims=True)
            lse_ref[h : h + 1] = top + jnp.log(total)
            p = (e * (1.0 / total)).astype(BF16)
            parts.append(dot(flipped[half * head_size : (half + 1) * head_size], p))
        o_ref[:, at : at + span] = jnp.concatenate(parts, axis=0).T.astype(BF16)
    h1 = h0 + dot(o_ref[...], weights_ref[:, 3 * width :])
    h1_ref[...] = h1
    n2 = (h1 * rms_scale(h1) * gain2_ref[...]).astype(BF16)
    logits = dot(n2, router_ref[...])
    logits = jnp.where(lane_below(logits.shape, experts), logits, NEG_BIG)
    top = jnp.max(logits, axis=-1, keepdims=True)
    e = jnp.exp(logits - top)
    probs_ref[...] = e / jnp.sum(e, axis=-1, keepdims=True)
    slots = lax.broadcasted_iota(jnp.int32, (x_ref.shape[0], length), 0)
    place = (slots == targets_ref[0:1]) | (slots == targets_ref[1:2])
    x_ref[...] = dot(place.astype(F32).astype(BF16), n2).astype(BF16)
    if rels is not None:
        keep.wait()


def forward_call(heads, experts, slot_count, weights, rels, *args):
    length, width = args[0].shape
    shapes = [
        ((slot_count, width), BF16),
        ((length, width), BF16),
        ((length, 3 * width), BF16),
        ((heads, length), F32),
        ((length, width), BF16),
        ((length, width), F32),
        ((length, 128), F32),
    ]
    inside = pl.BlockSpec(memory_space=pltpu.VMEM)
    outside = pl.BlockSpec(memory_space=pl.ANY)
    in_specs = [inside] * len(args)
    out_specs = [inside] * len(shapes)
    scratch = []
    if rels is None:
        args, in_specs = (weights,) + args, [inside] + in_specs
    else:
        me, pieces = weights
        args = (me, *pieces) + args
        in_specs = [pl.BlockSpec(memory_space=pltpu.SMEM)] + [outside] * len(pieces) + in_specs
        shapes.append(((width, 4 * width), BF16))
        out_specs.append(outside)
        scratch = [
            pltpu.VMEM((width, 4 * width), BF16),
            pltpu.SemaphoreType.DMA((4 * len(rels[0]),)),
            pltpu.SemaphoreType.DMA,
        ]
    return pl.pallas_call(
        partial(forward_body, heads, experts, rels),
        in_specs=in_specs,
        out_specs=out_specs,
        out_shape=[jax.ShapeDtypeStruct(*s) for s in shapes],
        scratch_shapes=scratch,
        compiler_params=pltpu.CompilerParams(vmem_limit_bytes=32 << 20),
        cost_estimate=LIGHT,
        name="attention_forward",
    )(*args)


def backward_body(
    heads,
    experts,
    dx_ref,
    targets_ref,
    routes_ref,
    probs_ref,
    h1_ref,
    go_ref,
    gain2_ref,
    router_ref,
    proj_ref,
    qkv_ref,
    lse_ref,
    bias_ref,
    rows_ref,
    columns_ref,
    dh1_ref,
    dbranch_ref,
    dqkv_ref,
    ds_ref,
    router_grad_ref,
    gain_grad_ref,
    do_ref,
):
    length, width = h1_ref.shape
    head_size = width // heads
    scale = head_size ** (-0.5)
    slots = lax.broadcasted_iota(jnp.int32, (length, dx_ref.shape[0]), 1)
    hot = [slots == targets_ref[:, j : j + 1] for j in range(2)]
    pick = [m.astype(F32).astype(BF16) for m in hot]
    dgate = [jnp.sum(dot(m, dx_ref[:, width:]), axis=-1, keepdims=True) for m in pick]
    probs = probs_ref[...]
    lane = lax.broadcasted_iota(jnp.int32, probs.shape, 1)
    dprobs = sum(jnp.where(lane == routes_ref[:, j : j + 1], dgate[j], 0.0) for j in range(2))
    dlogits = probs * (dprobs - jnp.sum(probs * dprobs, axis=-1, keepdims=True))
    dlogits = dlogits.astype(BF16)
    dn2 = dot(pick[0] + pick[1], dx_ref[:, :width]) + dot_t(dlogits, router_ref[...])
    h1 = h1_ref[...]
    r2 = rms_scale(h1)
    n2_hat = h1 * r2
    gain2 = gain2_ref[...]
    n2 = (n2_hat * gain2).astype(BF16)
    router_grad_ref[...] = t_dot(dlogits, n2)
    gain_grad_ref[...] = jnp.sum(dn2 * n2_hat, axis=0, keepdims=True)
    scaled = dn2 * gain2
    mean = jnp.mean(scaled * n2_hat, axis=-1, keepdims=True)
    dh1 = go_ref[...].astype(F32) + r2 * (scaled - n2_hat * mean)
    dh1_ref[...] = dh1
    dbranch = dh1.astype(BF16)
    dbranch_ref[...] = dbranch
    do_ref[...] = dot_t(dbranch, proj_ref[...]).astype(BF16)
    allowed = allowed_keys(rows_ref[...], columns_ref[...])
    span = 2 * head_size
    low = lane_below((length, span), head_size)
    for pair in range(heads // 2):
        at = pair * span
        q = qkv_ref[:, at : at + span]
        k = qkv_ref[:, width + at : width + at + span]
        v = qkv_ref[:, 2 * width + at : 2 * width + at + span]
        do = do_ref[:, at : at + span]
        flipped = k.T
        dq, dk, dv = [], [], []
        for half in range(2):
            h = 2 * pair + half
            s = pair_scores(h, head_size, scale, q, k, bias_ref[h], allowed)
            p = jnp.exp(s - lse_ref[h : h + 1])
            mine = low if half == 0 else ~low
            dp = dot_t(jnp.where(mine, v, jnp.zeros_like(v)), do)
            inner = jnp.sum(p * dp, axis=0, keepdims=True)
            ds = (p * (dp - inner)).astype(BF16)
            ds_ref[h] = ds
            dv.append(dot(p.astype(BF16), do))
            dk.append(dot(ds, q))
            dq.append(dot(flipped[half * head_size : (half + 1) * head_size], ds))
        dqkv_ref[:, at : at + span] = (jnp.concatenate(dq, axis=0).T * scale).astype(BF16)
        dqkv_ref[:, width + at : width + at + span] = (jnp.where(low, *dk) * scale).astype(BF16)
        dqkv_ref[:, 2 * width + at : 2 * width + at + span] = jnp.where(low, *dv).astype(BF16)


def backward_call(heads, experts, dx, targets, routes, probs, h1, go, gain2, router, proj, *rest):
    length, width = h1.shape
    shapes = [
        ((length, width), F32),
        ((length, width), BF16),
        ((length, 3 * width), BF16),
        ((heads, length, length), BF16),
        ((128, width), F32),
        ((1, width), F32),
    ]
    args = (dx, targets, routes, probs, h1, go, gain2, router, proj) + rest
    in_specs = [pl.BlockSpec(a.shape, lambda i, n=a.ndim: (0,) * n) for a in args]
    in_specs[8] = pl.BlockSpec((width, width), lambda i: (0, 3))
    return pl.pallas_call(
        partial(backward_body, heads, experts),
        grid=(1,),
        in_specs=in_specs,
        out_specs=[pl.BlockSpec(s, lambda i, n=len(s): (0,) * n) for s, _ in shapes],
        out_shape=[jax.ShapeDtypeStruct(*s) for s in shapes],
        scratch_shapes=[pltpu.VMEM((length, width), BF16)],
        compiler_params=pltpu.CompilerParams(vmem_limit_bytes=32 << 20),
        cost_estimate=LIGHT,
        name="attention_backward",
    )(*args)


def finish_body(count, tokens_ref, gain_ref, weights_ref, *refs):
    dqkvs, dh1s = refs[:count], refs[count : 2 * count]
    out_ref, gain_grad_ref = refs[2 * count :]
    gain = gain_ref[...]
    total = jnp.zeros(gain.shape, F32)
    for n in range(count):
        h0 = tokens_ref[n].astype(F32)
        r1 = rms_scale(h0)
        n1_hat = h0 * r1
        dn1 = dot_t(dqkvs[n][...], weights_ref[...])
        total = total + jnp.sum(dn1 * n1_hat, axis=0, keepdims=True)
        scaled = dn1 * gain
        mean = jnp.mean(scaled * n1_hat, axis=-1, keepdims=True)
        out_ref[n] = (dh1s[n][...] + r1 * (scaled - n1_hat * mean)).astype(BF16)
    gain_grad_ref[...] = total


def finish_call(tokens, gain, weights, dqkvs, dh1s):
    args = (tokens, gain, weights, *dqkvs, *dh1s)
    in_specs = [pl.BlockSpec(a.shape, lambda i, n=a.ndim: (0,) * n) for a in args]
    in_specs[2] = pl.BlockSpec((tokens.shape[2], 3 * tokens.shape[2]), lambda i: (0, 0))
    return pl.pallas_call(
        partial(finish_body, len(dqkvs)),
        grid=(1,),
        in_specs=in_specs,
        out_specs=[
            pl.BlockSpec(tokens.shape, lambda i: (0, 0, 0)),
            pl.BlockSpec(gain.shape, lambda i: (0, 0)),
        ],
        out_shape=[
            jax.ShapeDtypeStruct(tokens.shape, BF16),
            jax.ShapeDtypeStruct(gain.shape, F32),
        ],
        compiler_params=pltpu.CompilerParams(vmem_limit_bytes=32 << 20),
        cost_estimate=LIGHT,
        name="finish",
    )(*args)


def output_body(count, y_ref, targets_ref, routes_ref, *refs):
    probs, h1s, out_ref = refs[:count], refs[count : 2 * count], refs[-1]
    width = out_ref.shape[2]
    for n in range(count):
        y = y_ref[:, n].reshape(-1, width)
        slots = lax.broadcasted_iota(jnp.int32, (out_ref.shape[1], y.shape[0]), 1)
        total = h1s[n][...]
        moe = 0.0
        for j in range(2):
            weights = probs[n][...]
            lane = lax.broadcasted_iota(jnp.int32, weights.shape, 1)
            mine = lane == routes_ref[n, :, j : j + 1]
            gate = jnp.sum(jnp.where(mine, weights, 0.0), axis=-1, keepdims=True)
            pick = (slots == targets_ref[n, :, j : j + 1]).astype(F32).astype(BF16)
            moe = moe + gate * dot(pick, y)
        out_ref[n] = (total + moe).astype(BF16)


def output_call(y, targets, routes, probs, h1s):
    length, width = h1s[0].shape
    return pl.pallas_call(
        partial(output_body, len(h1s)),
        out_shape=jax.ShapeDtypeStruct((len(h1s), length, width), BF16),
        compiler_params=pltpu.CompilerParams(vmem_limit_bytes=32 << 20),
        cost_estimate=LIGHT,
        name="output",
    )(y, targets, routes, *probs, *h1s)


def on_device(
    sizes,
    tokens,
    cotangent,
    segment_ids,
    parent_ids,
    routes,
    gain_attn,
    w_qkv,
    w_proj,
    rel_bias,
    gain_moe,
    w_router,
    w_in,
    w_out,
):
    dp, experts = sizes["dp"], sizes["expert"]
    batches, length, width = tokens.shape
    heads = rel_bias.shape[1]
    head_size = width // heads
    inner = w_in.shape[2] // 2
    capacity = (10 * length + 4 * experts - 1) // (4 * experts)
    slot_count = experts * capacity
    scale = head_size ** (-0.5)
    me_e = lax.axis_index("expert")

    attn_block = gather_expert(jnp.concatenate([w_qkv, w_proj], axis=1), experts)
    places = jax.vmap(partial(slot_positions, experts=experts))(routes)
    targets = routes * capacity + places
    hot = targets[..., None] == jnp.arange(slot_count, dtype=jnp.int32)
    select = hot.astype(BF16)
    both = select[:, :, 0] + select[:, :, 1]
    out_grads = [cotangent[n] for n in range(batches)]
    outgoing = [
        t_dot(both[n], out_grads[n]).astype(BF16).reshape(experts, capacity, width)
        for n in range(batches)
    ]
    go_joint = all_to_all(after(jnp.stack(outgoing, axis=1), attn_block))
    go_slots = [go_joint[:, n] for n in range(batches)]

    positions = jnp.arange(length, dtype=jnp.int32)
    buckets = bucket_of(positions[:, None] - positions[None, :])
    bucket_hot = (buckets[:, :, None] == jnp.arange(rel_bias.shape[0], dtype=jnp.int32)).astype(F32)
    bias = jnp.einsum("kqc,ch->hkq", bucket_hot, rel_bias, precision=lax.Precision.HIGHEST)

    me_d = lax.axis_index("dp").astype(jnp.int32)[None]
    attn_first = gather_first(attn_block, dp, outgoing)
    pieces, rels = gather_dp(attn_first, dp, bias)
    wout_full = lax.all_gather(w_out[0], "dp", axis=0, tiled=True)
    win_full = lax.all_gather(
        after(w_in[0], pieces[:2], go_slots[0]), "dp", axis=0, tiled=True
    )

    router_wide = jnp.pad(w_router, ((0, 0), (0, 128 - experts)))
    gain1, gain2 = gain_attn[None], gain_moe[None]
    saved = []
    for n in range(batches):
        id_rows = jnp.stack([segment_ids[n], parent_ids[n]])
        target_columns = targets[n]
        weights = attn_w if n else (me_d, pieces)
        outs = forward_call(
            heads,
            experts,
            slot_count,
            weights,
            None if n else rels,
            tokens[n],
            gain1,
            bias,
            id_rows,
            id_rows.T,
            gain2,
            router_wide,
            target_columns.T,
        )
        if n == 0:
            *outs, attn_w = outs
        x_slots = all_to_all(after(outs[0], go_slots).reshape(experts, capacity, width))
        saved.append((id_rows,) + tuple(outs[1:]) + (x_slots,))

    mine = jnp.stack([me_e, jnp.int32(experts)]).astype(jnp.int32)
    held, grads = [], None
    for n in range(batches):
        x = saved[n][-1].reshape(slot_count, width)
        go = go_slots[n].reshape(slot_count, width)
        y, dx, *grads = expert_call(
            n, batches, experts, mine, x, go, router_wide, win_full, wout_full, grads
        )
        grads = [y] + grads
        dx_back = all_to_all(dx.reshape(experts, capacity, width + 128))
        held.append((x, dx_back.reshape(slot_count, width + 128)))

    def backward(n, dx_back):
        id_rows, _, qkv, lse, _, h1, probs, _ = saved[n]
        return backward_call(
            heads,
            experts,
            dx_back,
            targets[n],
            routes[n],
            probs,
            h1,
            out_grads[n],
            gain2,
            router_wide,
            attn_w,
            qkv,
            lse,
            bias,
            id_rows,
            id_rows.T,
        )

    core = me_d % 2
    _, gt, du, dy = grads
    joined = weight_in_call(dp, [h[0] for h in held], after(du, held[0][1]))
    joined = after(weight_out_call(gt, dy, joined), held[1][1])
    backs = [backward(n, after(held[n][1], joined)) for n in range(batches)]
    attn_keep, attn_send = weight_attn_call(
        dp,
        core,
        [v[1] for v in saved],
        [v[4] for v in saved],
        [v[2] for v in backs],
        [v[1] for v in backs],
    )
    y_back = all_to_all(after(grads[0], attn_keep))
    attn_core = scatter_core(attn_keep, attn_send, dp)
    space, tile = joined.shape[1:]
    summed = lax.psum_scatter(
        joined.reshape(dp * space, tile), "dp", scatter_dimension=0, tiled=True
    )
    in_total, out_total = spread_call(summed, w_in.shape[1:], w_out.shape[1:])

    router_grad = sum(v[4] for v in backs)[:experts].T
    gain_moe_grad = sum(v[5] for v in backs)[0]
    table_grad = jnp.einsum(
        "nhkq,kqc->ch",
        after(jnp.stack([v[3] for v in backs]), attn_core),
        bucket_hot.astype(BF16),
        preferred_element_type=F32,
    )
    input_grads, gain_attn_grad = finish_call(
        tokens, gain1, attn_w, [after(v[2], attn_core) for v in backs], [v[0] for v in backs]
    )
    small = jnp.concatenate(
        [gain_attn_grad[0], table_grad.reshape(-1), gain_moe_grad, router_grad.reshape(-1)]
    )
    small = sum_over(small.reshape(-1, 128), "dp", dp)
    attn_sum = scatter_dp(attn_core, dp, (input_grads, table_grad))
    small = sum_ring(after(small, attn_sum), "expert", experts).reshape(-1)
    attn_total = scatter_expert(attn_sum, experts)
    qkv_total, proj_total = attn_total[:, : 3 * width], attn_total[:, 3 * width :]
    outputs = output_call(
        after(y_back, attn_sum), targets, routes, [v[6] for v in saved], [v[5] for v in saved]
    )
    cuts = (width, width + table_grad.size, 2 * width + table_grad.size)
    return (
        outputs,
        input_grads,
        small[: cuts[0]],
        qkv_total,
        proj_total,
        small[cuts[0] : cuts[1]].reshape(table_grad.shape),
        small[cuts[1] : cuts[2]],
        small[cuts[2] :].reshape(router_grad.shape),
        in_total[None],
        out_total[None],
    )


def solution(mesh):
    rows = P(None, ("dp", "expert"), None)
    in_specs = (
        rows,
        rows,
        P(None, ("dp", "expert")),
        P(None, ("dp", "expert")),
        rows,
        P(),
        P(("dp", "expert"), None),
        P(("dp", "expert"), None),
        P(),
        P(),
        P(),
        P("expert", "dp", None),
        P("expert", "dp", None),
    )
    out_specs = (
        rows,
        rows,
        P(),
        P(("dp", "expert"), None),
        P(("dp", "expert"), None),
        P(),
        P(),
        P(),
        P("expert", "dp", None),
        P("expert", "dp", None),
    )
    return jax.shard_map(
        partial(on_device, dict(mesh.shape)),
        mesh=mesh,
        in_specs=in_specs,
        out_specs=out_specs,
        check_vma=False,
    )
```

```python
from functools import partial

import jax
import jax.numpy as jnp
from jax import lax
from jax.experimental import pallas as pl
from jax.experimental.pallas import tpu as pltpu
from jax.sharding import PartitionSpec as P

EPSILON = 1e-06
NEG_BIG = -1e30
LIMITS = (12, 16, 23, 32, 46, 64, 91)
F32 = jnp.float32
BF16 = jnp.bfloat16


def bucket_of(offset):
    distance = jnp.abs(offset)
    far_part = 8 + sum(((distance >= limit).astype(jnp.int32) for limit in LIMITS))
    near_far = jnp.where(distance < 8, distance, far_part)
    return jnp.where(offset > 0, 16, 0) + near_far


def slot_positions(routes, experts):
    order = jnp.concatenate([routes[:, 0], routes[:, 1]])
    chosen = (order[:, None] == jnp.arange(experts, dtype=jnp.int32)[None, :]).astype(jnp.int32)
    before = jnp.cumsum(chosen, axis=0) - chosen
    place = jnp.sum(before * chosen, axis=1)
    return place.reshape(2, -1).T


def tree_mask(segment, parent):
    same = segment[None, :] == segment[:, None]
    upward = segment[None, :] == parent[:, None]
    downward = parent[None, :] == segment[:, None]
    return same | upward | downward


def rms_scale(values):
    return lax.rsqrt(jnp.mean(values * values, axis=-1, keepdims=True) + EPSILON)


def gelu_product(gate_part, up_part):
    return jax.nn.gelu(gate_part, approximate=True) * up_part


def after(value, *others):
    return lax.optimization_barrier((value, others))[0]


def flip(value, axis, size, bit):
    return lax.ppermute(value, axis, [(i, i ^ bit) for i in range(size)])


def shift(value, axis, size, step):
    return lax.ppermute(value, axis, [(i, (i + step) % size) for i in range(size)])


def halving_orders(size):
    bits = [1 << k for k in range(1, size.bit_length() - 1)]
    return (bits, bits[::-1])


def gather_first(block, size, hold):
    half = block.shape[0] // 2
    out = []
    for part, order in enumerate(halving_orders(size)):
        have = after(block[None, part * half : (part + 1) * half], hold)
        out.append(jnp.concatenate([have, flip(have, "dp", size, order[0])], axis=0))
    return out


def gather_dp(first, size, hold):
    near, rels = [], []
    for have, order in zip(first, halving_orders(size)):
        have = after(have, hold)
        order_rels = [0, order[0]]
        for bit in order[1:]:
            have = jnp.concatenate([have, flip(have, "dp", size, bit)], axis=0)
            order_rels = order_rels + [rel ^ bit for rel in order_rels]
        near.append(have)
        rels.append(order_rels)
    far = [flip(have, "dp", size, 1) for have in near]
    return near + far, rels


def gather_expert(block, size):
    me = lax.axis_index("expert")
    full = jnp.zeros((size,) + block.shape, block.dtype)
    for step in range(size):
        piece = shift(block, "expert", size, step) if step else block
        full = lax.dynamic_update_slice(full, piece[None], ((me - step) % size, 0, 0))
    return full.reshape(size * block.shape[0], block.shape[1])


def all_to_all(value):
    return lax.all_to_all(value, "expert", split_axis=0, concat_axis=0, tiled=True)


def split_bit(value, me, bit):
    mine = (me // bit) % 2
    kept = lax.dynamic_index_in_dim(value, mine, 0, keepdims=False)
    sent = lax.dynamic_index_in_dim(value, 1 - mine, 0, keepdims=False)
    return kept, sent


def scatter_core(keep, send, size):
    return (keep.astype(F32) + flip(send, "dp", size, 1).astype(F32)).astype(BF16)


def scatter_dp(summed, size, hold):
    me = lax.axis_index("dp")
    _, rows, width = summed.shape
    half = rows // 2
    outs = []
    for part, order in enumerate(halving_orders(size)):
        value = summed[:, part * half : (part + 1) * half]
        left = [1 << k for k in range(1, size.bit_length() - 1)]
        for bit in order:
            place = left.index(bit)
            high, low = 1 << (len(left) - 1 - place), 1 << place
            shaped = value.astype(BF16).reshape(high, 2, low, half, width)
            kept, sent = split_bit(jnp.moveaxis(shaped, 1, 0), me, bit)
            got = flip(sent, "dp", size, bit)
            value = kept.astype(F32) + after(got, hold).astype(F32)
            left.remove(bit)
        outs.append(value.reshape(half, width))
    return jnp.concatenate(outs, axis=0)


def scatter_expert(total, size):
    rows = total.shape[0] // size
    low = total.astype(BF16).reshape(size, rows, total.shape[1])
    return jnp.sum(all_to_all(low).astype(F32), axis=0)


def sum_over(value, axis, size):
    bit = 1
    while bit < size:
        value = value + flip(value, axis, size, bit)
        bit *= 2
    return value


def sum_ring(value, axis, size):
    terms = [shift(value, axis, size, step) if step else value for step in range(size)]
    while len(terms) > 1:
        half = len(terms) // 2
        terms = [terms[k] + terms[k + half] for k in range(half)]
    return terms[0]


def dot(left, right):
    return jnp.dot(left, right, preferred_element_type=F32)


def dot_t(left, right):
    return lax.dot_general(left, right, (((1,), (1,)), ((), ())), preferred_element_type=F32)


def t_dot(left, right):
    return lax.dot_general(left, right, (((0,), (0,)), ((), ())), preferred_element_type=F32)

LIGHT = pl.CostEstimate(flops=1, bytes_accessed=1, transcendentals=0)


GELU_C = 0.7978845608028654
GELU_A = 0.044715


def expert_body(
    mine, x_ref, go_ref, wr_ref, wg_ref, wu_ref, wo_ref, *refs
):
    y_ref, dx_ref, gt_ref, du_ref, dy_ref, y_acc, dx_acc = refs[-7:]
    step, last = pl.program_id(0), pl.num_programs(0) - 1

    @pl.when(step == 0)
    def _():
        logits = dot(x_ref[...], wr_ref[...])
        lane = lax.broadcasted_iota(jnp.int32, logits.shape, 1)
        logits = jnp.where(lane < mine[1], logits, NEG_BIG)
        top = jnp.max(logits, axis=-1, keepdims=True)
        weights = jnp.exp(logits - top)
        total = jnp.sum(weights, axis=-1, keepdims=True)
        gate = jnp.sum(jnp.where(lane == mine[0], weights, 0.0), axis=-1, keepdims=True) / total
        dy_ref[...] = (gate * go_ref[...].astype(F32)).astype(BF16)
        y_acc[...] = jnp.zeros_like(y_acc)
        dx_acc[...] = jnp.zeros_like(dx_acc)

    x = x_ref[...]
    wg, wu, wo = wg_ref[...], wu_ref[...], wo_ref[...]
    a, b = dot(x, wg), dot(x, wu)
    dg = dot_t(dy_ref[...], wo)
    square = a * a
    t = jnp.tanh(GELU_C * (a + GELU_A * (a * square)))
    half = 0.5 + 0.5 * t
    act = a * half
    slope = half + (0.5 * GELU_C) * a * (1.0 - t * t) * (1.0 + (3.0 * GELU_A) * square)
    g = (act * b).astype(BF16)
    da = (dg * b * slope).astype(BF16)
    db = (dg * act).astype(BF16)
    gt_ref[...] = g.T
    du_ref[0] = da
    du_ref[1] = db
    y_acc[...] += dot(g, wo)
    dx_acc[...] += dot_t(jnp.concatenate([da, db], axis=1), jnp.concatenate([wg, wu], axis=1))

    @pl.when(step == last)
    def _():
        y = y_acc[...].astype(BF16)
        y_ref[:, 0] = y.reshape(-1, *y_ref.shape[2:])
        width = y.shape[1]
        dx_ref[:, :width] = dx_acc[...].astype(BF16)
        product = go_ref[...].astype(F32) * y.astype(F32)
        rest = jnp.sum(product, axis=-1, keepdims=True)
        lane = lax.broadcasted_iota(jnp.int32, (y.shape[0], 128), 1)
        terms = jnp.zeros(lane.shape, F32)
        for place in range(3):
            term = rest.astype(BF16).astype(F32)
            terms = jnp.where(lane == place, term, terms)
            rest = rest - term
        dx_ref[:, width:] = terms.astype(BF16)


def tile_of(size, most):
    return max(t for t in range(128, most + 1, 128) if size % t == 0)


def expert_call(batch, batches, experts, mine, x, go, w_router, w_in, w_out, held):
    rows, width = x.shape
    inner = w_out.shape[0]
    tile = tile_of(inner, 256)
    tiles = inner // tile
    whole = lambda shape: pl.BlockSpec(shape, lambda j: (0,) * len(shape))
    in_specs = [
        pl.BlockSpec(memory_space=pltpu.SMEM),
        whole((rows, width)),
        whole((rows, width)),
        whole(w_router.shape),
        pl.BlockSpec((width, tile), lambda j: (0, j)),
        pl.BlockSpec((width, tile), lambda j: (0, tiles + j)),
        pl.BlockSpec((tile, width), lambda j: (j, 0)),
    ]
    args = [mine, x, go, w_router, w_in, w_in, w_out]
    aliases = {}
    if held is not None:
        in_specs += [pl.BlockSpec(memory_space=pl.ANY)] * 4
        aliases = {len(args): 0, len(args) + 1: 2, len(args) + 2: 3, len(args) + 3: 4}
        args += list(held)
    flops = 12 * rows * width * inner
    return pl.pallas_call(
        expert_body,
        grid=(tiles,),
        in_specs=in_specs,
        out_specs=[
            pl.BlockSpec((experts, 1, rows // experts, width), lambda j: (0, batch, 0, 0)),
            whole((rows, width + 128)),
            pl.BlockSpec((tile, rows), lambda j: (j, batch)),
            pl.BlockSpec((2, rows, tile), lambda j: (0, batch, j)),
            pl.BlockSpec((rows, width), lambda j: (batch, 0)),
        ],
        out_shape=[
            jax.ShapeDtypeStruct((experts, batches, rows // experts, width), BF16),
            jax.ShapeDtypeStruct((rows, width + 128), BF16),
            jax.ShapeDtypeStruct((inner, batches * rows), BF16),
            jax.ShapeDtypeStruct((2, batches * rows, inner), BF16),
            jax.ShapeDtypeStruct((batches * rows, width), BF16),
        ],
        scratch_shapes=[pltpu.VMEM((rows, width), F32), pltpu.VMEM((rows, width), F32)],
        input_output_aliases=aliases,
        compiler_params=pltpu.CompilerParams(vmem_limit_bytes=56 << 20),
        cost_estimate=LIGHT,
        name="expert",
    )(*args)


def keep_and_send(value, core, keep_ref, send_ref, place):
    value = value.reshape((-1, 2) + value.shape[1:])
    even, odd = value[:, 0], value[:, 1]
    keep_ref[place] = jnp.where(core == 0, even, odd)
    send_ref[place] = jnp.where(core == 0, odd, even)


def weight_in_body(*refs):
    xs, du_ref, out_ref, flipped = refs[:-3], refs[-3], refs[-2], refs[-1]
    rows = xs[0].shape[0]

    @pl.when(pl.program_id(0) == 0)
    def _():
        for n, x_ref in enumerate(xs):
            flipped[:, n * rows : (n + 1) * rows] = x_ref[...].T

    tile = out_ref.shape[2]
    part = flipped.shape[0] // out_ref.shape[0]
    for place in range(out_ref.shape[1] // part):
        value = dot(flipped[...], du_ref[0, :, place * tile : (place + 1) * tile]).astype(BF16)
        out_ref[:, place * part : (place + 1) * part] = value.reshape(-1, part, tile)


def weight_in_call(size, xs, du):
    rows, width = xs[0].shape
    _, total, inner = du.shape
    tile = tile_of(inner, 256)
    tiles = inner // tile
    part = width // size
    space = 2 * tiles * part + (inner // size) * (width // tile)
    return pl.pallas_call(
        weight_in_body,
        grid=(2,),
        in_specs=[pl.BlockSpec((rows, width), lambda j: (0, 0)) for _ in xs]
        + [pl.BlockSpec((1, total, inner), lambda j: (j, 0, 0))],
        out_specs=pl.BlockSpec((size, tiles * part, tile), lambda j: (0, j, 0)),
        out_shape=jax.ShapeDtypeStruct((size, space, tile), BF16),
        scratch_shapes=[pltpu.VMEM((width, total), BF16)],
        compiler_params=pltpu.CompilerParams(vmem_limit_bytes=56 << 20),
        cost_estimate=LIGHT,
        name="weight_in",
    )(*xs, du)


def weight_out_body(gt_ref, dy_ref, _, out_ref):
    out_ref[...] = dot(gt_ref[...], dy_ref[...]).astype(BF16).reshape(out_ref.shape)


def weight_out_call(gt, dy, joined):
    inner, total = gt.shape
    width = dy.shape[1]
    size, space, tile = joined.shape
    part = inner // size
    first = (space - part * (width // tile)) // part
    assert first * part + part * (width // tile) == space
    return pl.pallas_call(
        weight_out_body,
        grid=(width // tile,),
        in_specs=[
            pl.BlockSpec((inner, total), lambda j: (0, 0)),
            pl.BlockSpec((total, tile), lambda j: (0, j)),
            pl.BlockSpec(memory_space=pl.ANY),
        ],
        out_specs=pl.BlockSpec((size, part, tile), lambda j: (0, first + j, 0)),
        out_shape=jax.ShapeDtypeStruct(joined.shape, BF16),
        input_output_aliases={2: 0},
        compiler_params=pltpu.CompilerParams(vmem_limit_bytes=40 << 20),
        cost_estimate=LIGHT,
        name="weight_out",
    )(gt, dy, joined)


def spread_body(count, summed_ref, in_ref, out_ref):
    part, tile = in_ref.shape[0], summed_ref.shape[1]
    for place in range(count):
        piece = summed_ref[place * part : (place + 1) * part]
        in_ref[:, place * tile : (place + 1) * tile] = piece.astype(F32)
    base, part = count * part, out_ref.shape[0]
    for place in range(out_ref.shape[1] // tile):
        piece = summed_ref[base + place * part : base + (place + 1) * part]
        out_ref[:, place * tile : (place + 1) * tile] = piece.astype(F32)


def spread_call(summed, in_shape, out_shape):
    return pl.pallas_call(
        partial(spread_body, in_shape[1] // summed.shape[1]),
        out_shape=[jax.ShapeDtypeStruct(shape, F32) for shape in (in_shape, out_shape)],
        compiler_params=pltpu.CompilerParams(vmem_limit_bytes=32 << 20),
        cost_estimate=LIGHT,
        name="spread",
    )(summed)


def weight_attn_body(count, core_ref, *refs):
    n1s, os, dqkvs, dbranches = (refs[k * count : (k + 1) * count] for k in range(4))
    keep_ref, send_ref, flipped, right = refs[4 * count :]
    step, last = pl.program_id(0), pl.num_programs(0) - 1
    length = n1s[0].shape[0]
    blocks = 2 * keep_ref.shape[0]

    def fill(lefts, rights):
        for n in range(count):
            if lefts is not None:
                flipped[:, n * length : (n + 1) * length] = lefts[n][...].T
            right[n * length : (n + 1) * length] = rights[n][...]

    @pl.when(step == 0)
    def _():
        fill(n1s, dqkvs)

    @pl.when((step > 0) & (step < last))
    def _():
        fill(None, dqkvs)

    @pl.when(step == last)
    def _():
        fill(os, dbranches)

    value = dot(flipped[...], right[...]).astype(BF16)
    value = value.reshape(blocks, -1, value.shape[1])
    keep_and_send(value, core_ref[0], keep_ref, send_ref, slice(None))


def weight_attn_call(size, core, n1s, os, dqkvs, dbranches):
    count = len(n1s)
    length, width = n1s[0].shape
    whole = pl.BlockSpec((length, width), lambda j: (0, 0))
    half = pl.BlockSpec((size // 2, width // size, width), lambda j: (0, 0, j))
    return pl.pallas_call(
        partial(weight_attn_body, count),
        grid=(4,),
        in_specs=[pl.BlockSpec(memory_space=pltpu.SMEM)]
        + [whole] * (2 * count)
        + [pl.BlockSpec((length, width), lambda j: (0, jnp.minimum(j, 2)))] * count
        + [whole] * count,
        out_specs=[half, half],
        out_shape=[jax.ShapeDtypeStruct((size // 2, width // size, 4 * width), BF16)] * 2,
        scratch_shapes=[
            pltpu.VMEM((width, count * length), BF16),
            pltpu.VMEM((count * length, width), BF16),
        ],
        compiler_params=pltpu.CompilerParams(vmem_limit_bytes=32 << 20),
        cost_estimate=LIGHT,
        name="weight_attn",
    )(core, *n1s, *os, *dqkvs, *dbranches)


def lane_below(shape, limit):
    return lax.broadcasted_iota(jnp.int32, shape, 1) < limit


def allowed_keys(rows, columns):
    segment_q, parent_q = rows[0:1], rows[1:2]
    segment_k, parent_k = columns[:, 0:1], columns[:, 1:2]
    return (segment_k == segment_q) | (segment_k == parent_q) | (parent_k == segment_q)


def pair_scores(h, head_size, scale, q, k, bias, allowed):
    low = lane_below(k.shape, head_size)
    mine = low if h % 2 == 0 else ~low
    raw = dot_t(jnp.where(mine, k, jnp.zeros_like(k)), q) * scale + bias
    return jnp.where(allowed, raw, NEG_BIG)


def piece_moves(me, pieces, rels, whole, arrived):
    moves = []
    for number, piece in enumerate(pieces):
        part, other = number % 2, number // 2
        half = piece.shape[1]
        for place, rel in enumerate(rels[part]):
            row = pl.multiple_of((me ^ rel ^ other) * (2 * half) + part * half, half)
            moves.append(
                pltpu.make_async_copy(
                    piece.at[place], whole.at[pl.ds(row, half)], arrived.at[len(moves)]
                )
            )
            moves[-1].start()
    return moves


def join_body(rels, me_ref, *refs):
    pieces, whole, arrived = refs[:-2], refs[-2], refs[-1]
    for move in piece_moves(me_ref[0], pieces, rels, whole, arrived):
        move.wait()


def join_call(me, pieces, rels):
    outside = pl.BlockSpec(memory_space=pl.ANY)
    count = 4 * len(rels[0])
    return pl.pallas_call(
        partial(join_body, rels),
        in_specs=[pl.BlockSpec(memory_space=pltpu.SMEM)] + [outside] * len(pieces),
        out_specs=pl.BlockSpec(memory_space=pltpu.VMEM),
        out_shape=jax.ShapeDtypeStruct((count * pieces[0].shape[1], pieces[0].shape[2]), BF16),
        scratch_shapes=[pltpu.SemaphoreType.DMA((count,))],
        cost_estimate=LIGHT,
        name="join",
    )(me, *pieces)


def forward_body(heads, experts, rels, *refs):
    if rels is None:
        weights_ref, refs = refs[0], refs[1:]
    else:
        me_ref, pieces, refs = refs[0], refs[1:5], refs[5:]
        refs, (full_ref, weights_ref, arrived, written) = refs[:-4], refs[-4:]
        moves = piece_moves(me_ref[0], pieces, rels, weights_ref, arrived)
    (
        tokens_ref,
        gain1_ref,
        bias_ref,
        rows_ref,
        columns_ref,
        gain2_ref,
        router_ref,
        targets_ref,
        x_ref,
        n1_ref,
        qkv_ref,
        lse_ref,
        o_ref,
        h1_ref,
        probs_ref,
    ) = refs
    length, width = tokens_ref.shape
    head_size = width // heads
    scale = head_size ** (-0.5)
    h0 = tokens_ref[...].astype(F32)
    n1 = (h0 * rms_scale(h0) * gain1_ref[...]).astype(BF16)
    n1_ref[...] = n1
    if rels is not None:
        for move in moves:
            move.wait()
        keep = pltpu.make_async_copy(weights_ref, full_ref, written)
        keep.start()
    for part in range(3):
        columns = slice(part * width, (part + 1) * width)
        qkv_ref[:, columns] = dot(n1, weights_ref[:, columns]).astype(BF16)
    allowed = allowed_keys(rows_ref[...], columns_ref[...])
    span = 2 * head_size
    for pair in range(heads // 2):
        at = pair * span
        q = qkv_ref[:, at : at + span]
        k = qkv_ref[:, width + at : width + at + span]
        flipped = qkv_ref[:, 2 * width + at : 2 * width + at + span].T
        parts = []
        for half in range(2):
            h = 2 * pair + half
            s = pair_scores(h, head_size, scale, q, k, bias_ref[h], allowed)
            top = jnp.max(s, axis=0, keepdims=True)
            e = jnp.exp(s - top)
            total = jnp.sum(e, axis=0, keepdims=True)
            lse_ref[h : h + 1] = top + jnp.log(total)
            p = (e * (1.0 / total)).astype(BF16)
            parts.append(dot(flipped[half * head_size : (half + 1) * head_size], p))
        o_ref[:, at : at + span] = jnp.concatenate(parts, axis=0).T.astype(BF16)
    h1 = h0 + dot(o_ref[...], weights_ref[:, 3 * width :])
    h1_ref[...] = h1
    n2 = (h1 * rms_scale(h1) * gain2_ref[...]).astype(BF16)
    logits = dot(n2, router_ref[...])
    logits = jnp.where(lane_below(logits.shape, experts), logits, NEG_BIG)
    top = jnp.max(logits, axis=-1, keepdims=True)
    e = jnp.exp(logits - top)
    probs_ref[...] = e / jnp.sum(e, axis=-1, keepdims=True)
    slots = lax.broadcasted_iota(jnp.int32, (x_ref.shape[0], length), 0)
    place = (slots == targets_ref[0:1]) | (slots == targets_ref[1:2])
    x_ref[...] = dot(place.astype(F32).astype(BF16), n2).astype(BF16)
    if rels is not None:
        keep.wait()


def forward_call(heads, experts, slot_count, weights, rels, *args):
    length, width = args[0].shape
    shapes = [
        ((slot_count, width), BF16),
        ((length, width), BF16),
        ((length, 3 * width), BF16),
        ((heads, length), F32),
        ((length, width), BF16),
        ((length, width), F32),
        ((length, 128), F32),
    ]
    inside = pl.BlockSpec(memory_space=pltpu.VMEM)
    outside = pl.BlockSpec(memory_space=pl.ANY)
    in_specs = [inside] * len(args)
    out_specs = [inside] * len(shapes)
    scratch = []
    if rels is None:
        args, in_specs = (weights,) + args, [inside] + in_specs
    else:
        me, pieces = weights
        args = (me, *pieces) + args
        in_specs = [pl.BlockSpec(memory_space=pltpu.SMEM)] + [outside] * len(pieces) + in_specs
        shapes.append(((width, 4 * width), BF16))
        out_specs.append(outside)
        scratch = [
            pltpu.VMEM((width, 4 * width), BF16),
            pltpu.SemaphoreType.DMA((4 * len(rels[0]),)),
            pltpu.SemaphoreType.DMA,
        ]
    return pl.pallas_call(
        partial(forward_body, heads, experts, rels),
        in_specs=in_specs,
        out_specs=out_specs,
        out_shape=[jax.ShapeDtypeStruct(*s) for s in shapes],
        scratch_shapes=scratch,
        compiler_params=pltpu.CompilerParams(vmem_limit_bytes=32 << 20),
        cost_estimate=LIGHT,
        name="attention_forward",
    )(*args)


def backward_body(
    heads,
    experts,
    dx_ref,
    targets_ref,
    routes_ref,
    probs_ref,
    h1_ref,
    go_ref,
    gain2_ref,
    router_ref,
    proj_ref,
    qkv_ref,
    lse_ref,
    bias_ref,
    rows_ref,
    columns_ref,
    dh1_ref,
    dbranch_ref,
    dqkv_ref,
    ds_ref,
    router_grad_ref,
    gain_grad_ref,
    do_ref,
):
    length, width = h1_ref.shape
    head_size = width // heads
    scale = head_size ** (-0.5)
    slots = lax.broadcasted_iota(jnp.int32, (length, dx_ref.shape[0]), 1)
    hot = [slots == targets_ref[:, j : j + 1] for j in range(2)]
    pick = [m.astype(F32).astype(BF16) for m in hot]
    dgate = [jnp.sum(dot(m, dx_ref[:, width:]), axis=-1, keepdims=True) for m in pick]
    probs = probs_ref[...]
    lane = lax.broadcasted_iota(jnp.int32, probs.shape, 1)
    dprobs = sum(jnp.where(lane == routes_ref[:, j : j + 1], dgate[j], 0.0) for j in range(2))
    dlogits = probs * (dprobs - jnp.sum(probs * dprobs, axis=-1, keepdims=True))
    dlogits = dlogits.astype(BF16)
    dn2 = dot(pick[0] + pick[1], dx_ref[:, :width]) + dot_t(dlogits, router_ref[...])
    h1 = h1_ref[...]
    r2 = rms_scale(h1)
    n2_hat = h1 * r2
    gain2 = gain2_ref[...]
    n2 = (n2_hat * gain2).astype(BF16)
    router_grad_ref[...] = t_dot(dlogits, n2)
    gain_grad_ref[...] = jnp.sum(dn2 * n2_hat, axis=0, keepdims=True)
    scaled = dn2 * gain2
    mean = jnp.mean(scaled * n2_hat, axis=-1, keepdims=True)
    dh1 = go_ref[...].astype(F32) + r2 * (scaled - n2_hat * mean)
    dh1_ref[...] = dh1
    dbranch = dh1.astype(BF16)
    dbranch_ref[...] = dbranch
    do_ref[...] = dot_t(dbranch, proj_ref[...]).astype(BF16)
    allowed = allowed_keys(rows_ref[...], columns_ref[...])
    span = 2 * head_size
    low = lane_below((length, span), head_size)
    for pair in range(heads // 2):
        at = pair * span
        q = qkv_ref[:, at : at + span]
        k = qkv_ref[:, width + at : width + at + span]
        v = qkv_ref[:, 2 * width + at : 2 * width + at + span]
        do = do_ref[:, at : at + span]
        flipped = k.T
        dq, dk, dv = [], [], []
        for half in range(2):
            h = 2 * pair + half
            s = pair_scores(h, head_size, scale, q, k, bias_ref[h], allowed)
            p = jnp.exp(s - lse_ref[h : h + 1])
            mine = low if half == 0 else ~low
            dp = dot_t(jnp.where(mine, v, jnp.zeros_like(v)), do)
            inner = jnp.sum(p * dp, axis=0, keepdims=True)
            ds = (p * (dp - inner)).astype(BF16)
            ds_ref[h] = ds
            dv.append(dot(p.astype(BF16), do))
            dk.append(dot(ds, q))
            dq.append(dot(flipped[half * head_size : (half + 1) * head_size], ds))
        dqkv_ref[:, at : at + span] = (jnp.concatenate(dq, axis=0).T * scale).astype(BF16)
        dqkv_ref[:, width + at : width + at + span] = (jnp.where(low, *dk) * scale).astype(BF16)
        dqkv_ref[:, 2 * width + at : 2 * width + at + span] = jnp.where(low, *dv).astype(BF16)


def backward_call(heads, experts, dx, targets, routes, probs, h1, go, gain2, router, proj, *rest):
    length, width = h1.shape
    shapes = [
        ((length, width), F32),
        ((length, width), BF16),
        ((length, 3 * width), BF16),
        ((heads, length, length), BF16),
        ((128, width), F32),
        ((1, width), F32),
    ]
    args = (dx, targets, routes, probs, h1, go, gain2, router, proj) + rest
    in_specs = [pl.BlockSpec(a.shape, lambda i, n=a.ndim: (0,) * n) for a in args]
    in_specs[8] = pl.BlockSpec((width, width), lambda i: (0, 3))
    return pl.pallas_call(
        partial(backward_body, heads, experts),
        grid=(1,),
        in_specs=in_specs,
        out_specs=[pl.BlockSpec(s, lambda i, n=len(s): (0,) * n) for s, _ in shapes],
        out_shape=[jax.ShapeDtypeStruct(*s) for s in shapes],
        scratch_shapes=[pltpu.VMEM((length, width), BF16)],
        compiler_params=pltpu.CompilerParams(vmem_limit_bytes=32 << 20),
        cost_estimate=LIGHT,
        name="attention_backward",
    )(*args)


def finish_body(count, tokens_ref, gain_ref, weights_ref, *refs):
    dqkvs, dh1s = refs[:count], refs[count : 2 * count]
    out_ref, gain_grad_ref = refs[2 * count :]
    gain = gain_ref[...]
    total = jnp.zeros(gain.shape, F32)
    for n in range(count):
        h0 = tokens_ref[n].astype(F32)
        r1 = rms_scale(h0)
        n1_hat = h0 * r1
        dn1 = dot_t(dqkvs[n][...], weights_ref[...])
        total = total + jnp.sum(dn1 * n1_hat, axis=0, keepdims=True)
        scaled = dn1 * gain
        mean = jnp.mean(scaled * n1_hat, axis=-1, keepdims=True)
        out_ref[n] = (dh1s[n][...] + r1 * (scaled - n1_hat * mean)).astype(BF16)
    gain_grad_ref[...] = total


def finish_call(tokens, gain, weights, dqkvs, dh1s):
    args = (tokens, gain, weights, *dqkvs, *dh1s)
    in_specs = [pl.BlockSpec(a.shape, lambda i, n=a.ndim: (0,) * n) for a in args]
    in_specs[2] = pl.BlockSpec((tokens.shape[2], 3 * tokens.shape[2]), lambda i: (0, 0))
    return pl.pallas_call(
        partial(finish_body, len(dqkvs)),
        grid=(1,),
        in_specs=in_specs,
        out_specs=[
            pl.BlockSpec(tokens.shape, lambda i: (0, 0, 0)),
            pl.BlockSpec(gain.shape, lambda i: (0, 0)),
        ],
        out_shape=[
            jax.ShapeDtypeStruct(tokens.shape, BF16),
            jax.ShapeDtypeStruct(gain.shape, F32),
        ],
        compiler_params=pltpu.CompilerParams(vmem_limit_bytes=32 << 20),
        cost_estimate=LIGHT,
        name="finish",
    )(*args)


def output_body(count, y_ref, targets_ref, routes_ref, *refs):
    probs, h1s, out_ref = refs[:count], refs[count : 2 * count], refs[-1]
    width = out_ref.shape[2]
    for n in range(count):
        y = y_ref[:, n].reshape(-1, width)
        slots = lax.broadcasted_iota(jnp.int32, (out_ref.shape[1], y.shape[0]), 1)
        total = h1s[n][...]
        moe = 0.0
        for j in range(2):
            weights = probs[n][...]
            lane = lax.broadcasted_iota(jnp.int32, weights.shape, 1)
            mine = lane == routes_ref[n, :, j : j + 1]
            gate = jnp.sum(jnp.where(mine, weights, 0.0), axis=-1, keepdims=True)
            pick = (slots == targets_ref[n, :, j : j + 1]).astype(F32).astype(BF16)
            moe = moe + gate * dot(pick, y)
        out_ref[n] = (total + moe).astype(BF16)


def output_call(y, targets, routes, probs, h1s):
    length, width = h1s[0].shape
    return pl.pallas_call(
        partial(output_body, len(h1s)),
        out_shape=jax.ShapeDtypeStruct((len(h1s), length, width), BF16),
        compiler_params=pltpu.CompilerParams(vmem_limit_bytes=32 << 20),
        cost_estimate=LIGHT,
        name="output",
    )(y, targets, routes, *probs, *h1s)


def on_device(
    sizes,
    tokens,
    cotangent,
    segment_ids,
    parent_ids,
    routes,
    gain_attn,
    w_qkv,
    w_proj,
    rel_bias,
    gain_moe,
    w_router,
    w_in,
    w_out,
):
    dp, experts = sizes["dp"], sizes["expert"]
    batches, length, width = tokens.shape
    heads = rel_bias.shape[1]
    head_size = width // heads
    inner = w_in.shape[2] // 2
    capacity = (10 * length + 4 * experts - 1) // (4 * experts)
    slot_count = experts * capacity
    scale = head_size ** (-0.5)
    me_e = lax.axis_index("expert")

    attn_block = gather_expert(jnp.concatenate([w_qkv, w_proj], axis=1), experts)
    places = jax.vmap(partial(slot_positions, experts=experts))(routes)
    targets = routes * capacity + places
    hot = targets[..., None] == jnp.arange(slot_count, dtype=jnp.int32)
    select = hot.astype(BF16)
    both = select[:, :, 0] + select[:, :, 1]
    out_grads = [cotangent[n] for n in range(batches)]
    outgoing = [
        t_dot(both[n], out_grads[n]).astype(BF16).reshape(experts, capacity, width)
        for n in range(batches)
    ]
    go_joint = all_to_all(after(jnp.stack(outgoing, axis=1), attn_block))
    go_slots = [go_joint[:, n] for n in range(batches)]

    positions = jnp.arange(length, dtype=jnp.int32)
    buckets = bucket_of(positions[:, None] - positions[None, :])
    bucket_hot = (buckets[:, :, None] == jnp.arange(rel_bias.shape[0], dtype=jnp.int32)).astype(F32)
    bias = jnp.einsum("kqc,ch->hkq", bucket_hot, rel_bias, precision=lax.Precision.HIGHEST)

    me_d = lax.axis_index("dp").astype(jnp.int32)[None]
    attn_first = gather_first(attn_block, dp, outgoing)
    pieces, rels = gather_dp(attn_first, dp, bias)
    wout_full = lax.all_gather(w_out[0], "dp", axis=0, tiled=True)
    win_full = lax.all_gather(
        after(w_in[0], pieces[:2], go_slots[0]), "dp", axis=0, tiled=True
    )

    router_wide = jnp.pad(w_router, ((0, 0), (0, 128 - experts)))
    gain1, gain2 = gain_attn[None], gain_moe[None]
    saved = []
    for n in range(batches):
        id_rows = jnp.stack([segment_ids[n], parent_ids[n]])
        target_columns = targets[n]
        weights = attn_w if n else (me_d, pieces)
        outs = forward_call(
            heads,
            experts,
            slot_count,
            weights,
            None if n else rels,
            tokens[n],
            gain1,
            bias,
            id_rows,
            id_rows.T,
            gain2,
            router_wide,
            target_columns.T,
        )
        if n == 0:
            *outs, attn_w = outs
        x_slots = all_to_all(after(outs[0], go_slots).reshape(experts, capacity, width))
        saved.append((id_rows,) + tuple(outs[1:]) + (x_slots,))

    mine = jnp.stack([me_e, jnp.int32(experts)]).astype(jnp.int32)
    held, grads = [], None
    for n in range(batches):
        x = saved[n][-1].reshape(slot_count, width)
        go = go_slots[n].reshape(slot_count, width)
        y, dx, *grads = expert_call(
            n, batches, experts, mine, x, go, router_wide, win_full, wout_full, grads
        )
        grads = [y] + grads
        dx_back = all_to_all(dx.reshape(experts, capacity, width + 128))
        held.append((x, dx_back.reshape(slot_count, width + 128)))

    def backward(n, dx_back):
        id_rows, _, qkv, lse, _, h1, probs, _ = saved[n]
        return backward_call(
            heads,
            experts,
            dx_back,
            targets[n],
            routes[n],
            probs,
            h1,
            out_grads[n],
            gain2,
            router_wide,
            attn_w,
            qkv,
            lse,
            bias,
            id_rows,
            id_rows.T,
        )

    core = me_d % 2
    _, gt, du, dy = grads
    joined = weight_in_call(dp, [h[0] for h in held], after(du, held[0][1]))
    joined = after(weight_out_call(gt, dy, joined), held[1][1])
    backs = [backward(n, after(held[n][1], joined)) for n in range(batches)]
    attn_keep, attn_send = weight_attn_call(
        dp,
        core,
        [v[1] for v in saved],
        [v[4] for v in saved],
        [v[2] for v in backs],
        [v[1] for v in backs],
    )
    y_back = all_to_all(after(grads[0], attn_keep))
    attn_core = scatter_core(attn_keep, attn_send, dp)
    space, tile = joined.shape[1:]
    summed = lax.psum_scatter(
        joined.reshape(dp * space, tile), "dp", scatter_dimension=0, tiled=True
    )
    in_total, out_total = spread_call(summed, w_in.shape[1:], w_out.shape[1:])

    router_grad = sum(v[4] for v in backs)[:experts].T
    gain_moe_grad = sum(v[5] for v in backs)[0]
    table_grad = jnp.einsum(
        "nhkq,kqc->ch",
        after(jnp.stack([v[3] for v in backs]), attn_core),
        bucket_hot.astype(BF16),
        preferred_element_type=F32,
    )
    input_grads, gain_attn_grad = finish_call(
        tokens, gain1, attn_w, [after(v[2], attn_core) for v in backs], [v[0] for v in backs]
    )
    small = jnp.concatenate(
        [gain_attn_grad[0], table_grad.reshape(-1), gain_moe_grad, router_grad.reshape(-1)]
    )
    small = sum_over(small.reshape(-1, 128), "dp", dp)
    attn_sum = scatter_dp(attn_core, dp, (input_grads, table_grad))
    small = sum_ring(after(small, attn_sum), "expert", experts).reshape(-1)
    attn_total = scatter_expert(attn_sum, experts)
    qkv_total, proj_total = attn_total[:, : 3 * width], attn_total[:, 3 * width :]
    outputs = output_call(
        after(y_back, attn_sum), targets, routes, [v[6] for v in saved], [v[5] for v in saved]
    )
    cuts = (width, width + table_grad.size, 2 * width + table_grad.size)
    return (
        outputs,
        input_grads,
        small[: cuts[0]],
        qkv_total,
        proj_total,
        small[cuts[0] : cuts[1]].reshape(table_grad.shape),
        small[cuts[1] : cuts[2]],
        small[cuts[2] :].reshape(router_grad.shape),
        in_total[None],
        out_total[None],
    )


def solution(mesh):
    rows = P(None, ("dp", "expert"), None)
    in_specs = (
        rows,
        rows,
        P(None, ("dp", "expert")),
        P(None, ("dp", "expert")),
        rows,
        P(),
        P(("dp", "expert"), None),
        P(("dp", "expert"), None),
        P(),
        P(),
        P(),
        P("expert", "dp", None),
        P("expert", "dp", None),
    )
    out_specs = (
        rows,
        rows,
        P(),
        P(("dp", "expert"), None),
        P(("dp", "expert"), None),
        P(),
        P(),
        P(),
        P("expert", "dp", None),
        P("expert", "dp", None),
    )
    return jax.shard_map(
        partial(on_device, dict(mesh.shape)),
        mesh=mesh,
        in_specs=in_specs,
        out_specs=out_specs,
        check_vma=False,
    )
```

```python
from functools import partial

import jax
import jax.numpy as jnp
from jax import lax
from jax.experimental import pallas as pl
from jax.experimental.pallas import tpu as pltpu
from jax.sharding import PartitionSpec as P

EPSILON = 1e-06
NEG_BIG = -1e30
LIMITS = (12, 16, 23, 32, 46, 64, 91)
F32 = jnp.float32
BF16 = jnp.bfloat16


def bucket_of(offset):
    distance = jnp.abs(offset)
    far_part = 8 + sum(((distance >= limit).astype(jnp.int32) for limit in LIMITS))
    near_far = jnp.where(distance < 8, distance, far_part)
    return jnp.where(offset > 0, 16, 0) + near_far


def slot_positions(routes, experts):
    order = jnp.concatenate([routes[:, 0], routes[:, 1]])
    chosen = (order[:, None] == jnp.arange(experts, dtype=jnp.int32)[None, :]).astype(jnp.int32)
    before = jnp.cumsum(chosen, axis=0) - chosen
    place = jnp.sum(before * chosen, axis=1)
    return place.reshape(2, -1).T


def tree_mask(segment, parent):
    same = segment[None, :] == segment[:, None]
    upward = segment[None, :] == parent[:, None]
    downward = parent[None, :] == segment[:, None]
    return same | upward | downward


def rms_scale(values):
    return lax.rsqrt(jnp.mean(values * values, axis=-1, keepdims=True) + EPSILON)


def gelu_product(gate_part, up_part):
    return jax.nn.gelu(gate_part, approximate=True) * up_part


def after(value, *others):
    return lax.optimization_barrier((value, others))[0]


def flip(value, axis, size, bit):
    return lax.ppermute(value, axis, [(i, i ^ bit) for i in range(size)])


def shift(value, axis, size, step):
    return lax.ppermute(value, axis, [(i, (i + step) % size) for i in range(size)])


def halving_orders(size):
    bits = [1 << k for k in range(1, size.bit_length() - 1)]
    return (bits, bits[::-1])


def gather_first(block, size, hold):
    half = block.shape[0] // 2
    out = []
    for part, order in enumerate(halving_orders(size)):
        have = after(block[None, part * half : (part + 1) * half], hold)
        out.append(jnp.concatenate([have, flip(have, "dp", size, order[0])], axis=0))
    return out


def gather_dp(first, size, hold):
    near, rels = [], []
    for have, order in zip(first, halving_orders(size)):
        have = after(have, hold)
        order_rels = [0, order[0]]
        for bit in order[1:]:
            have = jnp.concatenate([have, flip(have, "dp", size, bit)], axis=0)
            order_rels = order_rels + [rel ^ bit for rel in order_rels]
        near.append(have)
        rels.append(order_rels)
    far = [flip(have, "dp", size, 1) for have in near]
    return near + far, rels


def gather_expert(block, size):
    me = lax.axis_index("expert")
    full = jnp.zeros((size,) + block.shape, block.dtype)
    for step in range(size):
        piece = shift(block, "expert", size, step) if step else block
        full = lax.dynamic_update_slice(full, piece[None], ((me - step) % size, 0, 0))
    return full.reshape(size * block.shape[0], block.shape[1])


def all_to_all(value):
    return lax.all_to_all(value, "expert", split_axis=0, concat_axis=0, tiled=True)


def split_bit(value, me, bit):
    mine = (me // bit) % 2
    kept = lax.dynamic_index_in_dim(value, mine, 0, keepdims=False)
    sent = lax.dynamic_index_in_dim(value, 1 - mine, 0, keepdims=False)
    return kept, sent


def scatter_core(keep, send, size):
    return (keep.astype(F32) + flip(send, "dp", size, 1).astype(F32)).astype(BF16)


def scatter_dp(summed, size, hold):
    me = lax.axis_index("dp")
    _, rows, width = summed.shape
    half = rows // 2
    outs = []
    for part, order in enumerate(halving_orders(size)):
        value = summed[:, part * half : (part + 1) * half]
        left = [1 << k for k in range(1, size.bit_length() - 1)]
        for bit in order:
            place = left.index(bit)
            high, low = 1 << (len(left) - 1 - place), 1 << place
            shaped = value.astype(BF16).reshape(high, 2, low, half, width)
            kept, sent = split_bit(jnp.moveaxis(shaped, 1, 0), me, bit)
            got = flip(sent, "dp", size, bit)
            value = kept.astype(F32) + after(got, hold).astype(F32)
            left.remove(bit)
        outs.append(value.reshape(half, width))
    return jnp.concatenate(outs, axis=0)


def scatter_expert(total, size):
    rows = total.shape[0] // size
    low = total.astype(BF16).reshape(size, rows, total.shape[1])
    return jnp.sum(all_to_all(low).astype(F32), axis=0)


def sum_over(value, axis, size):
    bit = 1
    while bit < size:
        value = value + flip(value, axis, size, bit)
        bit *= 2
    return value


def sum_ring(value, axis, size):
    terms = [shift(value, axis, size, step) if step else value for step in range(size)]
    while len(terms) > 1:
        half = len(terms) // 2
        terms = [terms[k] + terms[k + half] for k in range(half)]
    return terms[0]


def dot(left, right):
    return jnp.dot(left, right, preferred_element_type=F32)


def dot_t(left, right):
    return lax.dot_general(left, right, (((1,), (1,)), ((), ())), preferred_element_type=F32)


def t_dot(left, right):
    return lax.dot_general(left, right, (((0,), (0,)), ((), ())), preferred_element_type=F32)

LIGHT = pl.CostEstimate(flops=1, bytes_accessed=1, transcendentals=0)


GELU_C = 0.7978845608028654
GELU_A = 0.044715


def expert_body(
    mine, x_ref, go_ref, wr_ref, wg_ref, wu_ref, wo_ref, *refs
):
    y_ref, dx_ref, gt_ref, du_ref, dy_ref, y_acc, dx_acc = refs[-7:]
    step, last = pl.program_id(0), pl.num_programs(0) - 1

    @pl.when(step == 0)
    def _():
        logits = dot(x_ref[...], wr_ref[...])
        lane = lax.broadcasted_iota(jnp.int32, logits.shape, 1)
        logits = jnp.where(lane < mine[1], logits, NEG_BIG)
        top = jnp.max(logits, axis=-1, keepdims=True)
        weights = jnp.exp(logits - top)
        total = jnp.sum(weights, axis=-1, keepdims=True)
        gate = jnp.sum(jnp.where(lane == mine[0], weights, 0.0), axis=-1, keepdims=True) / total
        dy_ref[...] = (gate * go_ref[...].astype(F32)).astype(BF16)
        y_acc[...] = jnp.zeros_like(y_acc)
        dx_acc[...] = jnp.zeros_like(dx_acc)

    x = x_ref[...]
    wg, wu, wo = wg_ref[...], wu_ref[...], wo_ref[...]
    a, b = dot(x, wg), dot(x, wu)
    dg = dot_t(dy_ref[...], wo)
    square = a * a
    t = jnp.tanh(GELU_C * (a + GELU_A * (a * square)))
    half = 0.5 + 0.5 * t
    act = a * half
    slope = half + (0.5 * GELU_C) * a * (1.0 - t * t) * (1.0 + (3.0 * GELU_A) * square)
    g = (act * b).astype(BF16)
    da = (dg * b * slope).astype(BF16)
    db = (dg * act).astype(BF16)
    gt_ref[...] = g.T
    du_ref[0] = da
    du_ref[1] = db
    y_acc[...] += dot(g, wo)
    dx_acc[...] += dot_t(jnp.concatenate([da, db], axis=1), jnp.concatenate([wg, wu], axis=1))

    @pl.when(step == last)
    def _():
        y = y_acc[...].astype(BF16)
        y_ref[:, 0] = y.reshape(-1, *y_ref.shape[2:])
        width = y.shape[1]
        dx_ref[:, :width] = dx_acc[...].astype(BF16)
        product = go_ref[...].astype(F32) * y.astype(F32)
        rest = jnp.sum(product, axis=-1, keepdims=True)
        lane = lax.broadcasted_iota(jnp.int32, (y.shape[0], 128), 1)
        terms = jnp.zeros(lane.shape, F32)
        for place in range(3):
            term = rest.astype(BF16).astype(F32)
            terms = jnp.where(lane == place, term, terms)
            rest = rest - term
        dx_ref[:, width:] = terms.astype(BF16)


def tile_of(size, most):
    return max(t for t in range(128, most + 1, 128) if size % t == 0)


def expert_call(batch, batches, experts, mine, x, go, w_router, w_in, w_out, held):
    rows, width = x.shape
    inner = w_out.shape[0]
    tile = tile_of(inner, 256)
    tiles = inner // tile
    whole = lambda shape: pl.BlockSpec(shape, lambda j: (0,) * len(shape))
    in_specs = [
        pl.BlockSpec(memory_space=pltpu.SMEM),
        whole((rows, width)),
        whole((rows, width)),
        whole(w_router.shape),
        pl.BlockSpec((width, tile), lambda j: (0, j)),
        pl.BlockSpec((width, tile), lambda j: (0, tiles + j)),
        pl.BlockSpec((tile, width), lambda j: (j, 0)),
    ]
    args = [mine, x, go, w_router, w_in, w_in, w_out]
    aliases = {}
    if held is not None:
        in_specs += [pl.BlockSpec(memory_space=pl.ANY)] * 4
        aliases = {len(args): 0, len(args) + 1: 2, len(args) + 2: 3, len(args) + 3: 4}
        args += list(held)
    flops = 12 * rows * width * inner
    return pl.pallas_call(
        expert_body,
        grid=(tiles,),
        in_specs=in_specs,
        out_specs=[
            pl.BlockSpec((experts, 1, rows // experts, width), lambda j: (0, batch, 0, 0)),
            whole((rows, width + 128)),
            pl.BlockSpec((tile, rows), lambda j: (j, batch)),
            pl.BlockSpec((2, rows, tile), lambda j: (0, batch, j)),
            pl.BlockSpec((rows, width), lambda j: (batch, 0)),
        ],
        out_shape=[
            jax.ShapeDtypeStruct((experts, batches, rows // experts, width), BF16),
            jax.ShapeDtypeStruct((rows, width + 128), BF16),
            jax.ShapeDtypeStruct((inner, batches * rows), BF16),
            jax.ShapeDtypeStruct((2, batches * rows, inner), BF16),
            jax.ShapeDtypeStruct((batches * rows, width), BF16),
        ],
        scratch_shapes=[pltpu.VMEM((rows, width), F32), pltpu.VMEM((rows, width), F32)],
        input_output_aliases=aliases,
        compiler_params=pltpu.CompilerParams(vmem_limit_bytes=56 << 20),
        cost_estimate=LIGHT,
        name="expert",
    )(*args)


def keep_and_send(value, core, keep_ref, send_ref, place):
    value = value.reshape((-1, 2) + value.shape[1:])
    even, odd = value[:, 0], value[:, 1]
    keep_ref[place] = jnp.where(core == 0, even, odd)
    send_ref[place] = jnp.where(core == 0, odd, even)


def weight_in_body(*refs):
    xs, du_ref, out_ref, flipped = refs[:-3], refs[-3], refs[-2], refs[-1]
    rows = xs[0].shape[0]

    @pl.when(pl.program_id(0) == 0)
    def _():
        for n, x_ref in enumerate(xs):
            flipped[:, n * rows : (n + 1) * rows] = x_ref[...].T

    tile = out_ref.shape[2]
    part = flipped.shape[0] // out_ref.shape[0]
    for place in range(out_ref.shape[1] // part):
        value = dot(flipped[...], du_ref[0, :, place * tile : (place + 1) * tile]).astype(BF16)
        out_ref[:, place * part : (place + 1) * part] = value.reshape(-1, part, tile)


def weight_in_call(size, xs, du):
    rows, width = xs[0].shape
    _, total, inner = du.shape
    tile = tile_of(inner, 256)
    tiles = inner // tile
    part = width // size
    space = 2 * tiles * part + (inner // size) * (width // tile)
    return pl.pallas_call(
        weight_in_body,
        grid=(2,),
        in_specs=[pl.BlockSpec((rows, width), lambda j: (0, 0)) for _ in xs]
        + [pl.BlockSpec((1, total, inner), lambda j: (j, 0, 0))],
        out_specs=pl.BlockSpec((size, tiles * part, tile), lambda j: (0, j, 0)),
        out_shape=jax.ShapeDtypeStruct((size, space, tile), BF16),
        scratch_shapes=[pltpu.VMEM((width, total), BF16)],
        compiler_params=pltpu.CompilerParams(vmem_limit_bytes=40 << 20),
        cost_estimate=LIGHT,
        name="weight_in",
    )(*xs, du)


def weight_out_body(gt_ref, dy_ref, _, out_ref):
    out_ref[...] = dot(gt_ref[...], dy_ref[...]).astype(BF16).reshape(out_ref.shape)


def weight_out_call(gt, dy, joined):
    inner, total = gt.shape
    width = dy.shape[1]
    size, space, tile = joined.shape
    part = inner // size
    first = (space - part * (width // tile)) // part
    assert first * part + part * (width // tile) == space
    return pl.pallas_call(
        weight_out_body,
        grid=(width // tile,),
        in_specs=[
            pl.BlockSpec((inner, total), lambda j: (0, 0)),
            pl.BlockSpec((total, tile), lambda j: (0, j)),
            pl.BlockSpec(memory_space=pl.ANY),
        ],
        out_specs=pl.BlockSpec((size, part, tile), lambda j: (0, first + j, 0)),
        out_shape=jax.ShapeDtypeStruct(joined.shape, BF16),
        input_output_aliases={2: 0},
        compiler_params=pltpu.CompilerParams(vmem_limit_bytes=40 << 20),
        cost_estimate=LIGHT,
        name="weight_out",
    )(gt, dy, joined)


def spread_body(count, summed_ref, in_ref, out_ref):
    part, tile = in_ref.shape[0], summed_ref.shape[1]
    for place in range(count):
        piece = summed_ref[place * part : (place + 1) * part]
        in_ref[:, place * tile : (place + 1) * tile] = piece.astype(F32)
    base, part = count * part, out_ref.shape[0]
    for place in range(out_ref.shape[1] // tile):
        piece = summed_ref[base + place * part : base + (place + 1) * part]
        out_ref[:, place * tile : (place + 1) * tile] = piece.astype(F32)


def spread_call(summed, in_shape, out_shape):
    return pl.pallas_call(
        partial(spread_body, in_shape[1] // summed.shape[1]),
        out_shape=[jax.ShapeDtypeStruct(shape, F32) for shape in (in_shape, out_shape)],
        compiler_params=pltpu.CompilerParams(vmem_limit_bytes=32 << 20),
        cost_estimate=LIGHT,
        name="spread",
    )(summed)


def weight_attn_body(count, core_ref, *refs):
    n1s, os, dqkvs, dbranches = (refs[k * count : (k + 1) * count] for k in range(4))
    keep_ref, send_ref, flipped, right = refs[4 * count :]
    step, last = pl.program_id(0), pl.num_programs(0) - 1
    length = n1s[0].shape[0]
    blocks = 2 * keep_ref.shape[0]

    def fill(lefts, rights):
        for n in range(count):
            if lefts is not None:
                flipped[:, n * length : (n + 1) * length] = lefts[n][...].T
            right[n * length : (n + 1) * length] = rights[n][...]

    @pl.when(step == 0)
    def _():
        fill(n1s, dqkvs)

    @pl.when((step > 0) & (step < last))
    def _():
        fill(None, dqkvs)

    @pl.when(step == last)
    def _():
        fill(os, dbranches)

    value = dot(flipped[...], right[...]).astype(BF16)
    value = value.reshape(blocks, -1, value.shape[1])
    keep_and_send(value, core_ref[0], keep_ref, send_ref, slice(None))


def weight_attn_call(size, core, n1s, os, dqkvs, dbranches):
    count = len(n1s)
    length, width = n1s[0].shape
    whole = pl.BlockSpec((length, width), lambda j: (0, 0))
    half = pl.BlockSpec((size // 2, width // size, width), lambda j: (0, 0, j))
    return pl.pallas_call(
        partial(weight_attn_body, count),
        grid=(4,),
        in_specs=[pl.BlockSpec(memory_space=pltpu.SMEM)]
        + [whole] * (2 * count)
        + [pl.BlockSpec((length, width), lambda j: (0, jnp.minimum(j, 2)))] * count
        + [whole] * count,
        out_specs=[half, half],
        out_shape=[jax.ShapeDtypeStruct((size // 2, width // size, 4 * width), BF16)] * 2,
        scratch_shapes=[
            pltpu.VMEM((width, count * length), BF16),
            pltpu.VMEM((count * length, width), BF16),
        ],
        compiler_params=pltpu.CompilerParams(vmem_limit_bytes=32 << 20),
        cost_estimate=LIGHT,
        name="weight_attn",
    )(core, *n1s, *os, *dqkvs, *dbranches)


def lane_below(shape, limit):
    return lax.broadcasted_iota(jnp.int32, shape, 1) < limit


def allowed_keys(rows, columns):
    segment_q, parent_q = rows[0:1], rows[1:2]
    segment_k, parent_k = columns[:, 0:1], columns[:, 1:2]
    return (segment_k == segment_q) | (segment_k == parent_q) | (parent_k == segment_q)


def pair_scores(h, head_size, scale, q, k, bias, allowed):
    low = lane_below(k.shape, head_size)
    mine = low if h % 2 == 0 else ~low
    raw = dot_t(jnp.where(mine, k, jnp.zeros_like(k)), q) * scale + bias
    return jnp.where(allowed, raw, NEG_BIG)


def piece_moves(me, pieces, rels, whole, arrived):
    moves = []
    for number, piece in enumerate(pieces):
        part, other = number % 2, number // 2
        half = piece.shape[1]
        for place, rel in enumerate(rels[part]):
            row = pl.multiple_of((me ^ rel ^ other) * (2 * half) + part * half, half)
            moves.append(
                pltpu.make_async_copy(
                    piece.at[place], whole.at[pl.ds(row, half)], arrived.at[len(moves)]
                )
            )
            moves[-1].start()
    return moves


def join_body(rels, me_ref, *refs):
    pieces, whole, arrived = refs[:-2], refs[-2], refs[-1]
    for move in piece_moves(me_ref[0], pieces, rels, whole, arrived):
        move.wait()


def join_call(me, pieces, rels):
    outside = pl.BlockSpec(memory_space=pl.ANY)
    count = 4 * len(rels[0])
    return pl.pallas_call(
        partial(join_body, rels),
        in_specs=[pl.BlockSpec(memory_space=pltpu.SMEM)] + [outside] * len(pieces),
        out_specs=pl.BlockSpec(memory_space=pltpu.VMEM),
        out_shape=jax.ShapeDtypeStruct((count * pieces[0].shape[1], pieces[0].shape[2]), BF16),
        scratch_shapes=[pltpu.SemaphoreType.DMA((count,))],
        cost_estimate=LIGHT,
        name="join",
    )(me, *pieces)


def forward_body(heads, experts, rels, *refs):
    if rels is None:
        weights_ref, refs = refs[0], refs[1:]
    else:
        me_ref, pieces, refs = refs[0], refs[1:5], refs[5:]
        refs, (full_ref, weights_ref, arrived, written) = refs[:-4], refs[-4:]
        moves = piece_moves(me_ref[0], pieces, rels, weights_ref, arrived)
    (
        tokens_ref,
        gain1_ref,
        bias_ref,
        rows_ref,
        columns_ref,
        gain2_ref,
        router_ref,
        targets_ref,
        x_ref,
        n1_ref,
        qkv_ref,
        lse_ref,
        o_ref,
        h1_ref,
        probs_ref,
    ) = refs
    length, width = tokens_ref.shape
    head_size = width // heads
    scale = head_size ** (-0.5)
    h0 = tokens_ref[...].astype(F32)
    n1 = (h0 * rms_scale(h0) * gain1_ref[...]).astype(BF16)
    n1_ref[...] = n1
    if rels is not None:
        for move in moves:
            move.wait()
        keep = pltpu.make_async_copy(weights_ref, full_ref, written)
        keep.start()
    for part in range(3):
        columns = slice(part * width, (part + 1) * width)
        qkv_ref[:, columns] = dot(n1, weights_ref[:, columns]).astype(BF16)
    allowed = allowed_keys(rows_ref[...], columns_ref[...])
    span = 2 * head_size
    for pair in range(heads // 2):
        at = pair * span
        q = qkv_ref[:, at : at + span]
        k = qkv_ref[:, width + at : width + at + span]
        flipped = qkv_ref[:, 2 * width + at : 2 * width + at + span].T
        parts = []
        for half in range(2):
            h = 2 * pair + half
            s = pair_scores(h, head_size, scale, q, k, bias_ref[h], allowed)
            top = jnp.max(s, axis=0, keepdims=True)
            e = jnp.exp(s - top)
            total = jnp.sum(e, axis=0, keepdims=True)
            lse_ref[h : h + 1] = top + jnp.log(total)
            p = (e * (1.0 / total)).astype(BF16)
            parts.append(dot(flipped[half * head_size : (half + 1) * head_size], p))
        o_ref[:, at : at + span] = jnp.concatenate(parts, axis=0).T.astype(BF16)
    h1 = h0 + dot(o_ref[...], weights_ref[:, 3 * width :])
    h1_ref[...] = h1
    n2 = (h1 * rms_scale(h1) * gain2_ref[...]).astype(BF16)
    logits = dot(n2, router_ref[...])
    logits = jnp.where(lane_below(logits.shape, experts), logits, NEG_BIG)
    top = jnp.max(logits, axis=-1, keepdims=True)
    e = jnp.exp(logits - top)
    probs_ref[...] = e / jnp.sum(e, axis=-1, keepdims=True)
    slots = lax.broadcasted_iota(jnp.int32, (x_ref.shape[0], length), 0)
    place = (slots == targets_ref[0:1]) | (slots == targets_ref[1:2])
    x_ref[...] = dot(place.astype(F32).astype(BF16), n2).astype(BF16)
    if rels is not None:
        keep.wait()


def forward_call(heads, experts, slot_count, weights, rels, *args):
    length, width = args[0].shape
    shapes = [
        ((slot_count, width), BF16),
        ((length, width), BF16),
        ((length, 3 * width), BF16),
        ((heads, length), F32),
        ((length, width), BF16),
        ((length, width), F32),
        ((length, 128), F32),
    ]
    inside = pl.BlockSpec(memory_space=pltpu.VMEM)
    outside = pl.BlockSpec(memory_space=pl.ANY)
    in_specs = [inside] * len(args)
    out_specs = [inside] * len(shapes)
    scratch = []
    if rels is None:
        args, in_specs = (weights,) + args, [inside] + in_specs
    else:
        me, pieces = weights
        args = (me, *pieces) + args
        in_specs = [pl.BlockSpec(memory_space=pltpu.SMEM)] + [outside] * len(pieces) + in_specs
        shapes.append(((width, 4 * width), BF16))
        out_specs.append(outside)
        scratch = [
            pltpu.VMEM((width, 4 * width), BF16),
            pltpu.SemaphoreType.DMA((4 * len(rels[0]),)),
            pltpu.SemaphoreType.DMA,
        ]
    return pl.pallas_call(
        partial(forward_body, heads, experts, rels),
        in_specs=in_specs,
        out_specs=out_specs,
        out_shape=[jax.ShapeDtypeStruct(*s) for s in shapes],
        scratch_shapes=scratch,
        compiler_params=pltpu.CompilerParams(vmem_limit_bytes=32 << 20),
        cost_estimate=LIGHT,
        name="attention_forward",
    )(*args)


def backward_body(
    heads,
    experts,
    dx_ref,
    targets_ref,
    routes_ref,
    probs_ref,
    h1_ref,
    go_ref,
    gain2_ref,
    router_ref,
    proj_ref,
    qkv_ref,
    lse_ref,
    bias_ref,
    rows_ref,
    columns_ref,
    dh1_ref,
    dbranch_ref,
    dqkv_ref,
    ds_ref,
    router_grad_ref,
    gain_grad_ref,
    do_ref,
):
    length, width = h1_ref.shape
    head_size = width // heads
    scale = head_size ** (-0.5)
    slots = lax.broadcasted_iota(jnp.int32, (length, dx_ref.shape[0]), 1)
    hot = [slots == targets_ref[:, j : j + 1] for j in range(2)]
    pick = [m.astype(F32).astype(BF16) for m in hot]
    dgate = [jnp.sum(dot(m, dx_ref[:, width:]), axis=-1, keepdims=True) for m in pick]
    probs = probs_ref[...]
    lane = lax.broadcasted_iota(jnp.int32, probs.shape, 1)
    dprobs = sum(jnp.where(lane == routes_ref[:, j : j + 1], dgate[j], 0.0) for j in range(2))
    dlogits = probs * (dprobs - jnp.sum(probs * dprobs, axis=-1, keepdims=True))
    dlogits = dlogits.astype(BF16)
    dn2 = dot(pick[0] + pick[1], dx_ref[:, :width]) + dot_t(dlogits, router_ref[...])
    h1 = h1_ref[...]
    r2 = rms_scale(h1)
    n2_hat = h1 * r2
    gain2 = gain2_ref[...]
    n2 = (n2_hat * gain2).astype(BF16)
    router_grad_ref[...] = t_dot(dlogits, n2)
    gain_grad_ref[...] = jnp.sum(dn2 * n2_hat, axis=0, keepdims=True)
    scaled = dn2 * gain2
    mean = jnp.mean(scaled * n2_hat, axis=-1, keepdims=True)
    dh1 = go_ref[...].astype(F32) + r2 * (scaled - n2_hat * mean)
    dh1_ref[...] = dh1
    dbranch = dh1.astype(BF16)
    dbranch_ref[...] = dbranch
    do_ref[...] = dot_t(dbranch, proj_ref[...]).astype(BF16)
    allowed = allowed_keys(rows_ref[...], columns_ref[...])
    span = 2 * head_size
    low = lane_below((length, span), head_size)
    for pair in range(heads // 2):
        at = pair * span
        q = qkv_ref[:, at : at + span]
        k = qkv_ref[:, width + at : width + at + span]
        v = qkv_ref[:, 2 * width + at : 2 * width + at + span]
        do = do_ref[:, at : at + span]
        flipped = k.T
        dq, dk, dv = [], [], []
        for half in range(2):
            h = 2 * pair + half
            s = pair_scores(h, head_size, scale, q, k, bias_ref[h], allowed)
            p = jnp.exp(s - lse_ref[h : h + 1])
            mine = low if half == 0 else ~low
            dp = dot_t(jnp.where(mine, v, jnp.zeros_like(v)), do)
            inner = jnp.sum(p * dp, axis=0, keepdims=True)
            ds = (p * (dp - inner)).astype(BF16)
            ds_ref[h] = ds
            dv.append(dot(p.astype(BF16), do))
            dk.append(dot(ds, q))
            dq.append(dot(flipped[half * head_size : (half + 1) * head_size], ds))
        dqkv_ref[:, at : at + span] = (jnp.concatenate(dq, axis=0).T * scale).astype(BF16)
        dqkv_ref[:, width + at : width + at + span] = (jnp.where(low, *dk) * scale).astype(BF16)
        dqkv_ref[:, 2 * width + at : 2 * width + at + span] = jnp.where(low, *dv).astype(BF16)


def backward_call(heads, experts, dx, targets, routes, probs, h1, go, gain2, router, proj, *rest):
    length, width = h1.shape
    shapes = [
        ((length, width), F32),
        ((length, width), BF16),
        ((length, 3 * width), BF16),
        ((heads, length, length), BF16),
        ((128, width), F32),
        ((1, width), F32),
    ]
    args = (dx, targets, routes, probs, h1, go, gain2, router, proj) + rest
    in_specs = [pl.BlockSpec(a.shape, lambda i, n=a.ndim: (0,) * n) for a in args]
    in_specs[8] = pl.BlockSpec((width, width), lambda i: (0, 3))
    return pl.pallas_call(
        partial(backward_body, heads, experts),
        grid=(1,),
        in_specs=in_specs,
        out_specs=[pl.BlockSpec(s, lambda i, n=len(s): (0,) * n) for s, _ in shapes],
        out_shape=[jax.ShapeDtypeStruct(*s) for s in shapes],
        scratch_shapes=[pltpu.VMEM((length, width), BF16)],
        compiler_params=pltpu.CompilerParams(vmem_limit_bytes=32 << 20),
        cost_estimate=LIGHT,
        name="attention_backward",
    )(*args)


def finish_body(count, tokens_ref, gain_ref, weights_ref, *refs):
    dqkvs, dh1s = refs[:count], refs[count : 2 * count]
    out_ref, gain_grad_ref = refs[2 * count :]
    gain = gain_ref[...]
    total = jnp.zeros(gain.shape, F32)
    for n in range(count):
        h0 = tokens_ref[n].astype(F32)
        r1 = rms_scale(h0)
        n1_hat = h0 * r1
        dn1 = dot_t(dqkvs[n][...], weights_ref[...])
        total = total + jnp.sum(dn1 * n1_hat, axis=0, keepdims=True)
        scaled = dn1 * gain
        mean = jnp.mean(scaled * n1_hat, axis=-1, keepdims=True)
        out_ref[n] = (dh1s[n][...] + r1 * (scaled - n1_hat * mean)).astype(BF16)
    gain_grad_ref[...] = total


def finish_call(tokens, gain, weights, dqkvs, dh1s):
    args = (tokens, gain, weights, *dqkvs, *dh1s)
    in_specs = [pl.BlockSpec(a.shape, lambda i, n=a.ndim: (0,) * n) for a in args]
    in_specs[2] = pl.BlockSpec((tokens.shape[2], 3 * tokens.shape[2]), lambda i: (0, 0))
    return pl.pallas_call(
        partial(finish_body, len(dqkvs)),
        grid=(1,),
        in_specs=in_specs,
        out_specs=[
            pl.BlockSpec(tokens.shape, lambda i: (0, 0, 0)),
            pl.BlockSpec(gain.shape, lambda i: (0, 0)),
        ],
        out_shape=[
            jax.ShapeDtypeStruct(tokens.shape, BF16),
            jax.ShapeDtypeStruct(gain.shape, F32),
        ],
        compiler_params=pltpu.CompilerParams(vmem_limit_bytes=32 << 20),
        cost_estimate=LIGHT,
        name="finish",
    )(*args)


def output_body(count, y_ref, targets_ref, routes_ref, *refs):
    probs, h1s, out_ref = refs[:count], refs[count : 2 * count], refs[-1]
    width = out_ref.shape[2]
    for n in range(count):
        y = y_ref[:, n].reshape(-1, width)
        slots = lax.broadcasted_iota(jnp.int32, (out_ref.shape[1], y.shape[0]), 1)
        total = h1s[n][...]
        moe = 0.0
        for j in range(2):
            weights = probs[n][...]
            lane = lax.broadcasted_iota(jnp.int32, weights.shape, 1)
            mine = lane == routes_ref[n, :, j : j + 1]
            gate = jnp.sum(jnp.where(mine, weights, 0.0), axis=-1, keepdims=True)
            pick = (slots == targets_ref[n, :, j : j + 1]).astype(F32).astype(BF16)
            moe = moe + gate * dot(pick, y)
        out_ref[n] = (total + moe).astype(BF16)


def output_call(y, targets, routes, probs, h1s):
    length, width = h1s[0].shape
    return pl.pallas_call(
        partial(output_body, len(h1s)),
        out_shape=jax.ShapeDtypeStruct((len(h1s), length, width), BF16),
        compiler_params=pltpu.CompilerParams(vmem_limit_bytes=32 << 20),
        cost_estimate=LIGHT,
        name="output",
    )(y, targets, routes, *probs, *h1s)


def on_device(
    sizes,
    tokens,
    cotangent,
    segment_ids,
    parent_ids,
    routes,
    gain_attn,
    w_qkv,
    w_proj,
    rel_bias,
    gain_moe,
    w_router,
    w_in,
    w_out,
):
    dp, experts = sizes["dp"], sizes["expert"]
    batches, length, width = tokens.shape
    heads = rel_bias.shape[1]
    head_size = width // heads
    inner = w_in.shape[2] // 2
    capacity = (10 * length + 4 * experts - 1) // (4 * experts)
    slot_count = experts * capacity
    scale = head_size ** (-0.5)
    me_e = lax.axis_index("expert")

    attn_block = gather_expert(jnp.concatenate([w_qkv, w_proj], axis=1), experts)
    places = jax.vmap(partial(slot_positions, experts=experts))(routes)
    targets = routes * capacity + places
    hot = targets[..., None] == jnp.arange(slot_count, dtype=jnp.int32)
    select = hot.astype(BF16)
    both = select[:, :, 0] + select[:, :, 1]
    out_grads = [cotangent[n] for n in range(batches)]
    outgoing = [
        t_dot(both[n], out_grads[n]).astype(BF16).reshape(experts, capacity, width)
        for n in range(batches)
    ]
    go_joint = all_to_all(after(jnp.stack(outgoing, axis=1), attn_block))
    go_slots = [go_joint[:, n] for n in range(batches)]

    positions = jnp.arange(length, dtype=jnp.int32)
    buckets = bucket_of(positions[:, None] - positions[None, :])
    bucket_hot = (buckets[:, :, None] == jnp.arange(rel_bias.shape[0], dtype=jnp.int32)).astype(F32)
    bias = jnp.einsum("kqc,ch->hkq", bucket_hot, rel_bias, precision=lax.Precision.HIGHEST)

    me_d = lax.axis_index("dp").astype(jnp.int32)[None]
    attn_first = gather_first(attn_block, dp, outgoing)
    pieces, rels = gather_dp(attn_first, dp, bias)
    wout_full = lax.all_gather(w_out[0], "dp", axis=0, tiled=True)
    win_full = lax.all_gather(
        after(w_in[0], pieces[:2], go_slots[0]), "dp", axis=0, tiled=True
    )

    router_wide = jnp.pad(w_router, ((0, 0), (0, 128 - experts)))
    gain1, gain2 = gain_attn[None], gain_moe[None]
    saved = []
    for n in range(batches):
        id_rows = jnp.stack([segment_ids[n], parent_ids[n]])
        target_columns = targets[n]
        weights = attn_w if n else (me_d, pieces)
        outs = forward_call(
            heads,
            experts,
            slot_count,
            weights,
            None if n else rels,
            tokens[n],
            gain1,
            bias,
            id_rows,
            id_rows.T,
            gain2,
            router_wide,
            target_columns.T,
        )
        if n == 0:
            *outs, attn_w = outs
        x_slots = all_to_all(after(outs[0], go_slots).reshape(experts, capacity, width))
        saved.append((id_rows,) + tuple(outs[1:]) + (x_slots,))

    mine = jnp.stack([me_e, jnp.int32(experts)]).astype(jnp.int32)
    held, grads = [], None
    for n in range(batches):
        x = saved[n][-1].reshape(slot_count, width)
        go = go_slots[n].reshape(slot_count, width)
        y, dx, *grads = expert_call(
            n, batches, experts, mine, x, go, router_wide, win_full, wout_full, grads
        )
        grads = [y] + grads
        dx_back = all_to_all(dx.reshape(experts, capacity, width + 128))
        held.append((x, dx_back.reshape(slot_count, width + 128)))

    def backward(n, dx_back):
        id_rows, _, qkv, lse, _, h1, probs, _ = saved[n]
        return backward_call(
            heads,
            experts,
            dx_back,
            targets[n],
            routes[n],
            probs,
            h1,
            out_grads[n],
            gain2,
            router_wide,
            attn_w,
            qkv,
            lse,
            bias,
            id_rows,
            id_rows.T,
        )

    core = me_d % 2
    _, gt, du, dy = grads
    joined = weight_in_call(dp, [h[0] for h in held], after(du, held[0][1]))
    joined = after(weight_out_call(gt, dy, joined), held[1][1])
    backs = [backward(n, after(held[n][1], joined)) for n in range(batches)]
    attn_keep, attn_send = weight_attn_call(
        dp,
        core,
        [v[1] for v in saved],
        [v[4] for v in saved],
        [v[2] for v in backs],
        [v[1] for v in backs],
    )
    y_back = all_to_all(after(grads[0], attn_keep))
    attn_core = scatter_core(attn_keep, attn_send, dp)
    space, tile = joined.shape[1:]
    summed = lax.psum_scatter(
        joined.reshape(dp * space, tile), "dp", scatter_dimension=0, tiled=True
    )
    in_total, out_total = spread_call(summed, w_in.shape[1:], w_out.shape[1:])

    router_grad = sum(v[4] for v in backs)[:experts].T
    gain_moe_grad = sum(v[5] for v in backs)[0]
    table_grad = jnp.einsum(
        "nhkq,kqc->ch",
        after(jnp.stack([v[3] for v in backs]), attn_core),
        bucket_hot.astype(BF16),
        preferred_element_type=F32,
    )
    input_grads, gain_attn_grad = finish_call(
        tokens, gain1, attn_w, [after(v[2], attn_core) for v in backs], [v[0] for v in backs]
    )
    small = jnp.concatenate(
        [gain_attn_grad[0], table_grad.reshape(-1), gain_moe_grad, router_grad.reshape(-1)]
    )
    small = sum_over(small.reshape(-1, 128), "dp", dp)
    attn_sum = scatter_dp(attn_core, dp, (input_grads, table_grad))
    small = sum_ring(after(small, attn_sum), "expert", experts).reshape(-1)
    attn_total = scatter_expert(attn_sum, experts)
    qkv_total, proj_total = attn_total[:, : 3 * width], attn_total[:, 3 * width :]
    outputs = output_call(
        after(y_back, attn_sum), targets, routes, [v[6] for v in saved], [v[5] for v in saved]
    )
    cuts = (width, width + table_grad.size, 2 * width + table_grad.size)
    return (
        outputs,
        input_grads,
        small[: cuts[0]],
        qkv_total,
        proj_total,
        small[cuts[0] : cuts[1]].reshape(table_grad.shape),
        small[cuts[1] : cuts[2]],
        small[cuts[2] :].reshape(router_grad.shape),
        in_total[None],
        out_total[None],
    )


def solution(mesh):
    rows = P(None, ("dp", "expert"), None)
    in_specs = (
        rows,
        rows,
        P(None, ("dp", "expert")),
        P(None, ("dp", "expert")),
        rows,
        P(),
        P(("dp", "expert"), None),
        P(("dp", "expert"), None),
        P(),
        P(),
        P(),
        P("expert", "dp", None),
        P("expert", "dp", None),
    )
    out_specs = (
        rows,
        rows,
        P(),
        P(("dp", "expert"), None),
        P(("dp", "expert"), None),
        P(),
        P(),
        P(),
        P("expert", "dp", None),
        P("expert", "dp", None),
    )
    return jax.shard_map(
        partial(on_device, dict(mesh.shape)),
        mesh=mesh,
        in_specs=in_specs,
        out_specs=out_specs,
        check_vma=False,
    )
```
